128 devices in a mesh: gx: 32 (over x, z_hi, y), gy: 4 (over z_lo, core).
Axes of the slice: x: 4, y: 4, z: 4 (z_hi: 2, z_lo: 2; z = z_hi * 2 + z_lo), core: 2. Of those that a mesh axis runs over, the one named last changes fastest.
Arguments:
- nodes: bfloat16 [64, 8, 32, 128], P('gx', 'gy'), may hold values from -6 to 6
- edges: bfloat16 [64, 8, 32, 64, 128], P('gx', 'gy'), may hold values from -6 to 6
- nbr_index: int32 [64, 8, 32, 64], P('gx', 'gy'), may hold values from 0 to 511, as said below
- nbr_mask: int32 [64, 8, 32, 64], P('gx', 'gy'), may hold values from 0 to 1, as said below
- edge_w1: bfloat16 [2, 384, 128], replicated, may hold values from -0.3125 to 0.3125
- edge_b1: float32 [2, 128], replicated, may hold values from -3 to 3
- edge_w2: bfloat16 [2, 128, 128], replicated, may hold values from -0.5 to 0.5
- edge_b2: float32 [2, 128], replicated, may hold values from -3 to 3
- edge_w3: bfloat16 [2, 128, 128], replicated, may hold values from -0.5 to 0.5
- edge_b3: float32 [2, 128], replicated, may hold values from -3 to 3
- edge_gain: float32 [2, 128], replicated, may hold values from 0.25 to 1.75
- edge_shift: float32 [2, 128], replicated, may hold values from -3 to 3
- node_w1: bfloat16 [2, 256, 128], replicated, may hold values from -0.375 to 0.375
- node_b1: float32 [2, 128], replicated, may hold values from -3 to 3
- node_w2: bfloat16 [2, 128, 128], replicated, may hold values from -0.5 to 0.5
- node_b2: float32 [2, 128], replicated, may hold values from -3 to 3
- node_w3: bfloat16 [2, 128, 128], replicated, may hold values from -0.5 to 0.5
- node_b3: float32 [2, 128], replicated, may hold values from -3 to 3
- node_gain: float32 [2, 128], replicated, may hold values from 0.25 to 1.75
- node_shift: float32 [2, 128], replicated, may hold values from -3 to 3
- ct_nodes: bfloat16 [64, 8, 32, 128], P('gx', 'gy'), may hold values from -6 to 6
- ct_edges: bfloat16 [64, 8, 32, 64, 128], P('gx', 'gy'), may hold values from -6 to 6
Outputs:
- nodes_out: bfloat16 [64, 8, 32, 128], P('gx', 'gy')
- edges_out: bfloat16 [64, 8, 32, 64, 128], P('gx', 'gy')
- grad_nodes: float32 [64, 8, 32, 128], P('gx', 'gy')
- grad_edges: float32 [64, 8, 32, 64, 128], P('gx', 'gy')
- grad_edge_w1: float32 [2, 384, 128], replicated
- grad_edge_b1: float32 [2, 128], replicated
- grad_edge_w2: float32 [2, 128, 128], replicated
- grad_edge_b2: float32 [2, 128], replicated
- grad_edge_w3: float32 [2, 128, 128], replicated
- grad_edge_b3: float32 [2, 128], replicated
- grad_edge_gain: float32 [2, 128], replicated
- grad_edge_shift: float32 [2, 128], replicated
- grad_node_w1: float32 [2, 256, 128], replicated
- grad_node_b1: float32 [2, 128], replicated
- grad_node_w2: float32 [2, 128, 128], replicated
- grad_node_b2: float32 [2, 128], replicated
- grad_node_w3: float32 [2, 128, 128], replicated
- grad_node_b3: float32 [2, 128], replicated
- grad_node_gain: float32 [2, 128], replicated
- grad_node_shift: float32 [2, 128], replicated
The draws below stay inside these ranges and needn't reach their ends.
Inputs may be any that keep to these rules, and one draw needn't show every extreme that they name: `nbr_index`: every slot names a particle slot of the 3 x 3 cells around the receiver's cell; both ends of the range are named on every device. `nbr_mask`: the live slots of a particle are its first c slots, 1 <= c <= 60; on every device some particle has c = 60 and some particle has c = 1.
All inputs are finite; a program needn't handle non-finite values.
Results may differ from the reference program's by a relative error of at most 0.035.
Values may be sent and summed in bfloat16 or wider, within the bound.
A program may use at most 64 MiB of HBM per device.

```python
from functools import partial
import jax
import jax.numpy as jnp
from jax import lax

LATENT = 128
K = 64
MOST = 60
CX = 2
CY = 2
CAP = 32
LAYERS = 2
NCX = 64
NCY = 8


def draw_nbr_index(key, part):
    key = jax.random.fold_in(key, 11)
    subkeys = jax.random.split(key, 3)
    shape = (NCX, NCY, CAP, K)
    step_x = jax.random.randint(subkeys[0], shape, -1, 2, dtype=jnp.int32)
    step_y = jax.random.randint(subkeys[1], shape, -1, 2, dtype=jnp.int32)
    member = jax.random.randint(subkeys[2], shape, 0, CAP, dtype=jnp.int32)
    cell_x = (jnp.arange(NCX, dtype=jnp.int32) % CX)[:, None, None, None]
    cell_y = (jnp.arange(NCY, dtype=jnp.int32) % CY)[None, :, None, None]
    slot_index = jnp.arange(K, dtype=jnp.int32)[None, None, None, :]
    first_slot = (jnp.arange(CAP, dtype=jnp.int32) == 0)[None, None, :, None]
    upper_end = first_slot & (slot_index == K - 1)
    lower_end = first_slot & (slot_index == K - 2)
    step_x = jnp.where(upper_end, 1, jnp.where(lower_end, -1, step_x))
    step_y = jnp.where(upper_end, 1, jnp.where(lower_end, -1, step_y))
    member = jnp.where(upper_end, CAP - 1, jnp.where(lower_end, 0, member))
    return (((cell_x + 1 + step_x) * (CY + 2) + cell_y + 1 + step_y) * CAP + member).astype(jnp.int32)


def draw_nbr_mask(key, part):
    key = jax.random.fold_in(key, 23)
    subkeys = jax.random.split(key, 2)
    cell_x = (jnp.arange(NCX, dtype=jnp.int32) % CX)[:, None, None, None]
    cell_y = (jnp.arange(NCY, dtype=jnp.int32) % CY)[None, :, None, None]
    corner_cell = (cell_x == 0) & (cell_y == 0)
    cell_most = jax.random.randint(subkeys[0], (NCX, NCY, 1, 1), MOST // 2, MOST + 1, dtype=jnp.int32)
    cell_most = jnp.where(corner_cell, MOST, cell_most)
    fewest = jnp.maximum(cell_most // 2, 1)
    live_count = jax.random.randint(subkeys[1], (NCX, NCY, CAP, 1), fewest, cell_most + 1, dtype=jnp.int32)
    slot_place = jnp.arange(CAP, dtype=jnp.int32)[None, None, :, None]
    live_count = jnp.where(slot_place == 0, cell_most, live_count)
    live_count = jnp.where(corner_cell & (slot_place == CAP - 1), 1, live_count)
    slot_index = jnp.arange(K, dtype=jnp.int32)[None, None, None, :]
    return (slot_index < live_count).astype(jnp.int32)


def block_levels(key, shape, shards, least, top_value):
    gain = 1.0
    for axis_at, shards_of in shards:
        steps = jax.random.uniform(jax.random.fold_in(jax.random.fold_in(key, 6), axis_at), (shards_of,), jnp.float32, least / len(shards), top_value / len(shards))
        gain = gain * jnp.repeat(jnp.exp(steps), shape[axis_at] // shards_of).reshape((-1,) + (1,) * (len(shape) - 1 - axis_at))
    return gain


def normal_values(own_key, extent, scale, bound, cuts=(), kind=jnp.bfloat16):
    result = jax.random.normal(own_key, extent, jnp.float32) * scale
    if len(cuts) > 0:
        result = block_levels(own_key, extent, cuts, -0.22, 0.18) * result
    return jnp.clip(result, min=-bound, max=bound).astype(kind)


def setup_inputs(seed: int = 0) -> dict:
    key_list = jax.random.split(jax.random.key(seed), 23)
    nodes = normal_values(key_list[0], (NCX, NCY, CAP, LATENT), 1.0, 6.0, ((0, 32), (1, 4)))
    edges = normal_values(key_list[1], (NCX, NCY, CAP, K, LATENT), 1.0, 6.0, ((0, 32), (1, 4)))
    nbr_index = draw_nbr_index(jax.random.fold_in(key_list[22], 71), 0)
    nbr_mask = draw_nbr_mask(jax.random.fold_in(key_list[22], 71), 0)
    edge_w1 = normal_values(key_list[4], (LAYERS, 3 * LATENT, LATENT), (3 * LATENT) ** -0.5, 0.3125)
    edge_b1 = normal_values(key_list[5], (LAYERS, LATENT), 0.5, 3.0, (), jnp.float32)
    edge_w2 = normal_values(key_list[6], (LAYERS, LATENT, LATENT), LATENT ** -0.5, 0.5)
    edge_b2 = normal_values(key_list[7], (LAYERS, LATENT), 0.5, 3.0, (), jnp.float32)
    edge_w3 = normal_values(key_list[8], (LAYERS, LATENT, LATENT), LATENT ** -0.5, 0.5)
    edge_b3 = normal_values(key_list[9], (LAYERS, LATENT), 0.5, 3.0, (), jnp.float32)
    edge_gain = jnp.clip(1.0 + 0.15 * jax.random.normal(key_list[10], (LAYERS, LATENT), jnp.float32), 0.25, 1.75)
    edge_shift = normal_values(key_list[11], (LAYERS, LATENT), 0.5, 3.0, (), jnp.float32)
    node_w1 = normal_values(key_list[12], (LAYERS, 2 * LATENT, LATENT), (2 * LATENT) ** -0.5, 0.375)
    node_b1 = normal_values(key_list[13], (LAYERS, LATENT), 0.5, 3.0, (), jnp.float32)
    node_w2 = normal_values(key_list[14], (LAYERS, LATENT, LATENT), LATENT ** -0.5, 0.5)
    node_b2 = normal_values(key_list[15], (LAYERS, LATENT), 0.5, 3.0, (), jnp.float32)
    node_w3 = normal_values(key_list[16], (LAYERS, LATENT, LATENT), LATENT ** -0.5, 0.5)
    node_b3 = normal_values(key_list[17], (LAYERS, LATENT), 0.5, 3.0, (), jnp.float32)
    node_gain = jnp.clip(1.0 + 0.15 * jax.random.normal(key_list[18], (LAYERS, LATENT), jnp.float32), 0.25, 1.75)
    node_shift = normal_values(key_list[19], (LAYERS, LATENT), 0.5, 3.0, (), jnp.float32)
    ct_nodes = normal_values(key_list[20], (NCX, NCY, CAP, LATENT), 1.0, 6.0, ((0, 32), (1, 4)))
    ct_edges = normal_values(key_list[21], (NCX, NCY, CAP, K, LATENT), 1.0, 6.0, ((0, 32), (1, 4)))
    return dict(nodes=nodes, edges=edges, nbr_index=nbr_index, nbr_mask=nbr_mask, edge_w1=edge_w1, edge_b1=edge_b1, edge_w2=edge_w2, edge_b2=edge_b2, edge_w3=edge_w3, edge_b3=edge_b3, edge_gain=edge_gain, edge_shift=edge_shift, node_w1=node_w1, node_b1=node_b1, node_w2=node_w2, node_b2=node_b2, node_w3=node_w3, node_b3=node_b3, node_gain=node_gain, node_shift=node_shift, ct_nodes=ct_nodes, ct_edges=ct_edges)


EPS = 1e-05

@jax.custom_vjp
def low(v):
    return lax.optimization_barrier(v.astype(jnp.bfloat16)).astype(jnp.float32)

@jax.custom_vjp
def low_back(v):
    return v

def low_keep(v):
    return (low(v), None)

def low_pass(kept, grad):
    return (grad,)

def back_keep(v):
    return (v, None)

def back_low(kept, grad):
    return (low(grad),)
low.defvjp(low_keep, low_pass)
low_back.defvjp(back_keep, back_low)

def row_matmul(values, weight):
    return jnp.einsum('...i,ij->...j', values, weight, precision=lax.Precision.HIGHEST)

def layer_norm(values, norm_gain, norm_shift):
    average = lax.optimization_barrier(jnp.mean(values, -1, keepdims=True))
    centred = values - average
    inverse = lax.rsqrt(lax.optimization_barrier(jnp.mean(centred * centred, -1, keepdims=True)) + EPS)
    return centred * inverse * norm_gain + norm_shift

def small_network(joined, params):
    weight_one, bias_one, weight_two, bias_two, weight_three, bias_three, norm_gain, norm_shift = params
    pre_one = low_back(row_matmul(joined, weight_one) + bias_one)
    act_one = low(jax.nn.silu(pre_one))
    pre_two = low_back(row_matmul(act_one, weight_two) + bias_two)
    act_two = low(jax.nn.silu(pre_two))
    pre_three = low_back(row_matmul(act_two, weight_three) + bias_three)
    return layer_norm(pre_three, norm_gain, norm_shift)

def sender_rows(nbr_index):
    row_slots = (CY + 2) * CAP
    column_x = nbr_index // row_slots
    remain = nbr_index % row_slots
    column_y = remain // CAP
    member = remain % CAP
    base_x = (jnp.arange(NCX, dtype=jnp.int32) // CX * CX)[:, None, None, None]
    base_y = (jnp.arange(NCY, dtype=jnp.int32) // CY * CY)[None, :, None, None]
    return (((base_x + column_x) * (NCY + 2) + base_y + column_y) * CAP + member).astype(jnp.int32)

def edge_block(padded_rows, edge_params, block_items):
    node_row, edge_row, index_row, mask_row = block_items
    senders = jnp.take(padded_rows, index_row, axis=0)
    receivers = jnp.broadcast_to(node_row[:, :, None, :], senders.shape)
    joined = jnp.concatenate([receivers, senders, edge_row], -1)
    update = small_network(joined, edge_params)
    new_edges = low(edge_row + mask_row[..., None] * update)
    summed = low(lax.optimization_barrier(jnp.sum(mask_row[..., None] * new_edges, axis=2)))
    return (new_edges, summed)

def forward(node_state, edge_state, global_index, live_mask, params):
    edge_all = params[:8]
    node_all = params[8:]
    for layer_index in range(LAYERS):
        edge_params = tuple((member[layer_index] for member in edge_all))
        node_params = tuple((member[layer_index] for member in node_all))
        padded = jnp.pad(node_state, ((1, 1), (1, 1), (0, 0), (0, 0)))
        padded_rows = padded.reshape(-1, node_state.shape[-1])
        block_step = jax.checkpoint(partial(edge_block, padded_rows, edge_params))
        edge_state, summed = lax.map(block_step, (node_state, edge_state, global_index, live_mask))
        joined = jnp.concatenate([node_state, summed], -1)
        node_state = low(node_state + small_network(joined, node_params))
    return (node_state, edge_state)

def reference(nodes, edges, nbr_index, nbr_mask, edge_w1, edge_b1, edge_w2, edge_b2, edge_w3, edge_b3, edge_gain, edge_shift, node_w1, node_b1, node_w2, node_b2, node_w3, node_b3, node_gain, node_shift, ct_nodes, ct_edges):
    global_index = sender_rows(nbr_index)
    live_mask = nbr_mask.astype(jnp.float32)
    params = tuple((member.astype(jnp.float32) for member in (edge_w1, edge_b1, edge_w2, edge_b2, edge_w3, edge_b3, edge_gain, edge_shift, node_w1, node_b1, node_w2, node_b2, node_w3, node_b3, node_gain, node_shift)))

    def runner(node_in, edge_in, *weights):
        return forward(node_in, edge_in, global_index, live_mask, weights)
    outputs, pullback = jax.vjp(runner, nodes.astype(jnp.float32), edges.astype(jnp.float32), *params)
    grads = pullback((ct_nodes.astype(jnp.float32), ct_edges.astype(jnp.float32)))
    return (outputs[0].astype(jnp.bfloat16), outputs[1].astype(jnp.bfloat16), grads[0], grads[1], grads[2], grads[3], grads[4], grads[5], grads[6], grads[7], grads[8], grads[9], grads[10], grads[11], grads[12], grads[13], grads[14], grads[15], grads[16], grads[17])
```

```python
import functools

import jax
import jax.numpy as jnp
from jax import lax
from jax.experimental import pallas as pl
from jax.experimental.pallas import tpu as pltpu
from jax.sharding import PartitionSpec as P

EPS = 1e-05
BF = jnp.bfloat16
F32 = jnp.float32
MESH = pl.DeviceIdType.MESH

D = 128
ROWS = 8192
CELL = 2048
SUB = 4
PARTS = 128

DIRS = tuple((dx, dy) for dx in (-1, 0, 1) for dy in (-1, 0, 1) if (dx, dy) != (0, 0))
PLANE = tuple((dx, dy) for dx in range(4) for dy in range(4) if (dx, dy) != (0, 0))
COLUMN = tuple((dz, dg) for dz in range(2) for dg in range(4) if (dz, dg) != (0, 0))

CH1 = 112
CH0 = 48
EDGE_W1, EDGE_W2, EDGE_W3 = 0, 384, 512
NODE_W1, NODE_W2, NODE_W3 = 640, 896, 1024
NODE0 = 1152
VEC1 = 1664
VEC0 = 640


def dot(a, b):
    return jnp.dot(a, b, preferred_element_type=F32)


def dot_nt(a, b):
    return lax.dot_general(a, b, (((1,), (1,)), ((), ())), preferred_element_type=F32)


def dot_tn(a, b):
    return lax.dot_general(a, b, (((0,), (0,)), ((), ())), preferred_element_type=F32)


def iota(shape, dim):
    return lax.broadcasted_iota(jnp.int32, shape, dim)


def silu_parts(half):
    wide = 1.0 + jnp.tanh(half)
    act = half * wide
    slope = wide * (0.5 + half - 0.5 * act)
    return act, slope


def rows_of(start, count):
    return pl.ds(pl.multiple_of(start, count), count)


def partial_rows(x):
    return jnp.sum(x.reshape(-1, 8, D), 0)


def column_sum(x):
    return jnp.sum(x, 0, keepdims=True)


def span(step, low, high, both):
    return low if step < 0 else (high if step > 0 else both)


class Sum:
    def __init__(self, chunk, refs, place):
        self.chunk = chunk
        self.src, self.part, self.col, self.out = refs[:4]
        self.send1, self.recv1, self.send2, self.recv2, self.send3, self.recv3 = refs[4:]
        self.gx, self.gy = place
        self.x, self.z, self.y = self.gx // 8, (self.gx // 4) % 2, self.gx % 4
        self.me = self.x * 4 + self.y
        self.mine = self.z * 4 + self.gy

    def plane_copy(self, k, dx, dy, src, dst, send, recv, slot):
        px, py = (self.x + dx) % 4, (self.y + dy) % 4
        return pltpu.make_async_remote_copy(
            src_ref=src,
            dst_ref=dst,
            send_sem=send.at[k],
            recv_sem=recv.at[slot],
            device_id=((px * 2 + self.z) * 4 + py, self.gy),
            device_id_type=MESH,
        )

    def rows(self, index):
        return pl.ds(pl.multiple_of(index * self.chunk, 16), self.chunk)

    def scatter_start(self):
        for k, (dx, dy) in enumerate(PLANE):
            peer = ((self.x + dx) % 4) * 4 + (self.y + dy) % 4
            self.plane_copy(
                k, dx, dy, self.src.at[self.rows(peer)], self.part.at[self.me], self.send1, self.recv1, self.me
            ).start()
        self.part[self.me] = self.src[self.rows(self.me), :]

    def scatter_finish(self):
        for k, (dx, dy) in enumerate(PLANE):
            peer = ((self.x - dx) % 4) * 4 + (self.y - dy) % 4
            copy = self.plane_copy(
                k, dx, dy, self.src.at[self.rows(peer)], self.part.at[peer], self.send1, self.recv1, peer
            )
            copy.wait_send()
            copy.wait_recv()
        total = self.part[0].astype(F32)
        for k in range(1, 16):
            total = total + self.part[k].astype(F32)
        self.col[self.mine] = total.astype(BF)

    def column_copy(self, k, dz, dg, slot):
        pz, pg = (self.z + dz) % 2, (self.gy + dg) % 4
        return pltpu.make_async_remote_copy(
            src_ref=self.col.at[self.mine],
            dst_ref=self.col.at[slot],
            send_sem=self.send2.at[k],
            recv_sem=self.recv2.at[slot],
            device_id=((self.x * 2 + pz) * 4 + self.y, pg),
            device_id_type=MESH,
        )

    def column_start(self):
        for k, (dz, dg) in enumerate(COLUMN):
            self.column_copy(k, dz, dg, self.mine).start()

    def column_finish(self):
        for k, (dz, dg) in enumerate(COLUMN):
            peer = ((self.z - dz) % 2) * 4 + (self.gy - dg) % 4
            copy = self.column_copy(k, dz, dg, peer)
            copy.wait_send()
            copy.wait_recv()
        total = self.col[0].astype(F32)
        for k in range(1, 8):
            total = total + self.col[k].astype(F32)
        self.out[self.rows(self.me), :] = total.astype(BF)

    def gather_start(self):
        own = self.out.at[self.rows(self.me)]
        for k, (dx, dy) in enumerate(PLANE):
            self.plane_copy(k, dx, dy, own, own, self.send3, self.recv3, self.me).start()

    def gather_finish(self):
        for k, (dx, dy) in enumerate(PLANE):
            peer = ((self.x - dx) % 4) * 4 + (self.y - dy) % 4
            landing = self.out.at[self.rows(peer)]
            copy = self.plane_copy(k, dx, dy, landing, landing, self.send3, self.recv3, peer)
            copy.wait_send()
            copy.wait_recv()


def main_kernel(*refs):
    (
        nodes, edges, index, mask,
        ew1, eb1, ew2, eb2, ew3, eb3, egain, eshift,
        nw1, nb1, nw2, nb2, nw3, nb3, ngain, nshift,
        ct_nodes, ct_edges,
        nodes_out, edges_out, grad_nodes, grad_edges, sum1_out, sum0_out,
        onehot, e0, e1, e2, ct,
        a1_0, s1_0, a2_0, s2_0, n_0, r_0,
        a1_1, s1_1, a2_1, s2_1, n_1, r_1,
        ge, live_count,
        tab, wbig, w2half, w3mid, w1et, w2t, w3t, averager,
        msum, gm, tt, dw2, dw3, sums,
        sender_sum, sender_low, receiver_sum, rim_in,
        nm, nc1, nc2, nsl1, nsl2, nnorm, ninv, gz1_buf, gh_buf,
        src1, part1, col1, src0, part0, col0,
        in_sem, out_sem, halo_send, halo_recv, rim_send, rim_recv,
        *sum_sems,
    ) = refs
    gx, gy = lax.axis_index("gx"), lax.axis_index("gy")
    sum1 = Sum(CH1, (src1, part1, col1, sum1_out, *sum_sems[:6]), (gx, gy))
    sum0 = Sum(CH0, (src0, part0, col0, sum0_out, *sum_sems[6:]), (gx, gy))
    kept = ((a1_0, s1_0, a2_0, s2_0, n_0, r_0), (a1_1, s1_1, a2_1, s2_1, n_1, r_1))
    edge_in = (e0, e1, e2)

    def neighbour(dx, dy):
        return (lax.rem(gx + dx + 32, 32), lax.rem(gy + dy + 4, 4))

    def load(ref, scratch, which, t):
        s = rows_of(t * CELL, CELL)
        return pltpu.make_async_copy(ref.at[s], scratch.at[s], in_sem.at[which, t])

    for t in range(4):
        load(edges, e0, 0, t).start()

    barrier = pltpu.get_barrier_semaphore()
    x, z, y = sum1.x, sum1.z, sum1.y
    partners = [neighbour(dx, dy) for dx, dy in DIRS]
    partners += [(((x + dx) % 4 * 2 + z) * 4 + (y + dy) % 4, gy) for dx, dy in PLANE]
    partners += [((x * 2 + (z + dz) % 2) * 4 + y, (gy + dg) % 4) for dz, dg in COLUMN]
    for partner in partners:
        pl.semaphore_signal(barrier, inc=1, device_id=partner, device_id_type=MESH)
    pl.semaphore_wait(barrier, len(partners))

    def halo_copy(layer, k):
        dx, dy = DIRS[k]
        src = tab.at[layer, span(dx, 1, 2, pl.ds(1, 2)), span(dy, 1, 2, pl.ds(1, 2))]
        dst = tab.at[layer, span(dx, 3, 0, pl.ds(1, 2)), span(dy, 3, 0, pl.ds(1, 2))]
        return pltpu.make_async_remote_copy(
            src_ref=src,
            dst_ref=dst,
            send_sem=halo_send.at[layer, k],
            recv_sem=halo_recv.at[layer, k],
            device_id=neighbour(dx, dy),
            device_id_type=MESH,
        )

    def halo_start(layer, latents):
        for cell in range(4):
            tab[layer, 1 + cell // 2, 1 + cell % 2] = latents[32 * cell : 32 * cell + 32]
        for k in range(8):
            halo_copy(layer, k).start()

    def halo_finish(layer):
        for k in range(8):
            copy = halo_copy(layer, k)
            copy.wait_send()
            copy.wait_recv()
        blank_row = jnp.zeros((4, 32, D), BF)
        for edge, at in ((0, 0), (31, 3)):

            @pl.when(gx == edge)
            def _():
                tab[layer, at] = blank_row

        for edge, at in ((0, 0), (3, 3)):

            @pl.when(gy == edge)
            def _():
                for a in range(4):
                    tab[layer, a, at] = blank_row[0]

    halo_start(0, nodes[...])
    for t in range(4):
        load(ct_edges, ct, 1, t).start()

    averager[...] = jnp.full((D, D), 1.0 / D, BF)
    for layer in range(2):
        w2half[layer] = (0.5 * ew2[layer].astype(F32)).astype(BF)
        w3 = ew3[layer].astype(F32)
        w3mid[layer] = (w3 - jnp.mean(w3, -1, keepdims=True)).astype(BF)
        w3t[layer] = ew3[layer].T
        w2t[layer] = ew2[layer].T
        w1et[layer] = ew1[layer, 2 * D : 3 * D, :].T
    sums[...] = jnp.zeros_like(sums)
    tt[...] = jnp.zeros_like(tt)
    dw2[...] = jnp.zeros_like(dw2)
    dw3[...] = jnp.zeros_like(dw3)

    count = jnp.sum(mask[...].astype(F32), -1, keepdims=True)
    live_count[...] = jnp.broadcast_to(count, (PARTS, D))
    cell_of = iota((PARTS, 64), 0) // 32
    place = index[...] - (cell_of // 2) * 128 - (cell_of % 2) * 32
    place = (place // 128) * 96 + place % 128
    dead = mask[...] == 0
    high = jnp.where(dead, 127, place // 16)
    low = jnp.where(dead, 0, place % 16)
    digits = jnp.concatenate([high, low], 1).astype(F32).astype(BF)
    spread = jnp.where(iota((D, D), 0) < 64, 16.0, 1.0).astype(BF)

    def onehot_step(t, carry):
        row = iota((CELL, D), 0)
        lane = iota((CELL, D), 1)
        pick = jnp.where(lane == t * 32 + row // 64, 1.0, 0.0).astype(BF)
        spread_out = dot(pick, digits)
        own = jnp.where(lane % 64 == row % 64, spread_out, 0.0).astype(BF)
        found = dot(own, spread).astype(jnp.int32)
        s = rows_of(t * CELL, CELL)
        onehot[s, 0:128] = jnp.where(found == lane, 1.0, 0.0).astype(BF)
        onehot[s, 128:256] = jnp.where(found == lane + 128, 1.0, 0.0).astype(BF)
        fixed = (lane == 32 + row // 64) | (lane == 64) | (lane == 65)
        onehot[s, 256:384] = jnp.where((found == lane + 256) | fixed, 1.0, 0.0).astype(BF)
        return carry

    lax.fori_loop(0, 4, onehot_step, 0)

    def prepare(layer):
        senders = dot(tab[layer].reshape(512, D), ew1[layer, D : 2 * D, :])
        senders = (0.5 * senders).astype(BF).reshape(4, 4, 32, D)
        own = jnp.concatenate([tab[layer, 1 + c // 2, 1 + c % 2] for c in range(4)], 0)
        receivers = (0.5 * dot(own, ew1[layer, 0:D, :])).astype(BF)
        bias = 0.5 * eb1[layer : layer + 1, :]
        bias_high = bias.astype(BF).astype(F32)
        at = iota((64, D), 0)
        bias_rows = jnp.where(at == 0, bias_high, jnp.where(at == 1, bias - bias_high, 0.0)).astype(BF)
        edge_rows = (0.5 * ew1[layer, 2 * D : 3 * D, :].astype(F32)).astype(BF)
        for c in range(4):
            i, j = c // 2, c % 2
            for a in range(3):
                wbig[c, 96 * a : 96 * a + 96, :] = senders[i + a, j : j + 3].reshape(96, D)
            wbig[c, 288:320, :] = receivers[32 * c : 32 * c + 32]
            wbig[c, 320:384, :] = bias_rows
            wbig[c, 384:512, :] = edge_rows

    step = CELL // SUB
    per = step // 64

    def live_of(p):
        slot = iota((per, 64, D), 1).astype(F32)
        return slot < live_count[p, :][:, None, :]

    def forward(layer):
        a1, s1, a2, s2, nn, rr = kept[layer]
        e_in, e_out = edge_in[layer], edge_in[layer + 1]
        b2 = 0.5 * eb2[layer : layer + 1, :]
        b3 = eb3[layer : layer + 1, :]
        b3 = b3 - jnp.mean(b3, -1, keepdims=True)
        gain, shift = egain[layer : layer + 1, :], eshift[layer : layer + 1, :]

        def body(t, carry):
            if layer == 0:
                load(edges, e0, 0, t).wait()
            groups = [rows_of(t * CELL + g * step, step) for g in range(SUB)]
            ones = [dot(jnp.concatenate([onehot[s, :], e_in[s, :]], 1), wbig[t]) for s in groups]
            first = []
            for s, half in zip(groups, ones):
                act, slope = silu_parts(half)
                a1[s, :] = act.astype(BF)
                s1[s, :] = slope.astype(BF)
                first.append(act.astype(BF))
            twos = [dot(act, w2half[layer]) + b2 for act in first]
            second = []
            for s, half in zip(groups, twos):
                act, slope = silu_parts(half)
                a2[s, :] = act.astype(BF)
                s2[s, :] = slope.astype(BF)
                second.append(act.astype(BF))
            mids = [dot(act, w3mid[layer]) + b3 for act in second]
            spreads = [dot((mid * mid).astype(BF), averager[...]) for mid in mids]
            for g, (s, mid, var) in enumerate(zip(groups, mids, spreads)):
                inverse = lax.rsqrt(var + EPS)
                normed = mid * inverse
                nn[s, :] = normed.astype(BF)
                rr[s, :] = inverse.astype(BF)
                update = (normed * gain + shift).reshape(per, 64, D)
                p = rows_of(t * 32 + g * per, per)
                live = live_of(p)
                new = e_in[s, :].astype(F32).reshape(per, 64, D) + jnp.where(live, update, 0.0)
                new = new.astype(BF)
                e_out[s, :] = new.reshape(step, D)
                msum[p, :] = jnp.sum(jnp.where(live, new.astype(F32), 0.0), 1)
            if layer == 1:
                s = rows_of(t * CELL, CELL)
                pltpu.make_async_copy(e2.at[s], edges_out.at[s], out_sem.at[0, t]).start()
            return carry

        lax.fori_loop(0, 4, body, 0)

    def node_forward(layer, h):
        m = msum[...].astype(BF)
        z1 = dot(h, nw1[layer, 0:D, :]) + dot(m, nw1[layer, D : 2 * D, :]) + nb1[layer : layer + 1, :]
        c1, slope1 = silu_parts(0.5 * z1)
        c1 = c1.astype(BF)
        z2 = dot(c1, nw2[layer]) + nb2[layer : layer + 1, :]
        c2, slope2 = silu_parts(0.5 * z2)
        c2 = c2.astype(BF)
        z3 = dot(c2, nw3[layer]) + nb3[layer : layer + 1, :]
        mid = z3 - jnp.mean(z3, -1, keepdims=True)
        inverse = lax.rsqrt(jnp.mean(mid * mid, -1, keepdims=True) + EPS)
        normed = mid * inverse
        nm[layer], nc1[layer], nc2[layer] = m, c1, c2
        nsl1[layer], nsl2[layer], nnorm[layer] = slope1, slope2, normed
        ninv[layer] = jnp.broadcast_to(inverse, (PARTS, D))
        update = normed * ngain[layer : layer + 1, :] + nshift[layer : layer + 1, :]
        return (h.astype(F32) + update).astype(BF)

    def node_backward(layer, h, gh, dst, row, vec):
        normed = nnorm[layer]
        q = gh * ngain[layer : layer + 1, :]
        inner = q - jnp.mean(q, -1, keepdims=True) - normed * jnp.mean(q * normed, -1, keepdims=True)
        gz3 = ninv[layer] * inner
        low3 = gz3.astype(BF)
        gz2 = dot_nt(low3, nw3[layer]) * nsl2[layer]
        low2 = gz2.astype(BF)
        gz1 = dot_nt(low2, nw2[layer]) * nsl1[layer]
        low1 = gz1.astype(BF)
        gz1_buf[...] = low1
        gm[...] = dot_nt(low1, nw1[layer, D : 2 * D, :])
        dst[row : row + 128, :] = dot_tn(h, low1).astype(BF)
        dst[row + 128 : row + 256, :] = dot_tn(nm[layer], low1).astype(BF)
        dst[row + 256 : row + 384, :] = dot_tn(nc1[layer], low2).astype(BF)
        dst[row + 384 : row + 512, :] = dot_tn(nc2[layer], low3).astype(BF)
        vec.extend([column_sum(gz1), column_sum(gz2), column_sum(gz3), column_sum(gh * normed), column_sum(gh)])

    def backward(layer):
        a1, s1, a2, s2, nn, rr = kept[layer]
        e_in = edge_in[layer]
        gain = egain[layer : layer + 1, :]

        def body(t, carry):
            if layer == 1:
                load(ct_edges, ct, 1, t).wait()
            groups = [rows_of(t * CELL + g * step, step) for g in range(SUB)]
            firsts = []
            for g, s in enumerate(groups):
                p = rows_of(t * 32 + g * per, per)
                live = live_of(p)
                old = ct[s, :].astype(F32) if layer == 1 else ge[s, :]
                total = old.reshape(per, 64, D) + jnp.where(live, gm[p, :][:, None, :], 0.0)
                gy_ = jnp.where(live, total, 0.0).reshape(step, D)
                normed = nn[s, :].astype(F32)
                q = gy_ * gain
                qn = q * normed
                mean_q = dot(q.astype(BF), averager[...])
                mean_qn = dot(qn.astype(BF), averager[...])
                firsts.append((total.reshape(step, D), gy_, q, qn, normed, mean_q, mean_qn))
            g3 = [
                rr[s, :].astype(F32) * (f[2] - f[5] - f[4] * f[6]) for s, f in zip(groups, firsts)
            ]
            low3 = [g.astype(BF) for g in g3]
            g2 = [dot(g, w3t[layer]) * s2[s, :].astype(F32) for s, g in zip(groups, low3)]
            low2 = [g.astype(BF) for g in g2]
            low1 = [(dot(g, w2t[layer]) * s1[s, :].astype(F32)).astype(BF) for s, g in zip(groups, low2)]
            for s, g, f in zip(groups, low1, firsts):
                ge[s, :] = f[0] + dot(g, w1et[layer])
            sums[layer, 0] += sum(partial_rows(f[3]) for f in firsts)
            sums[layer, 1] += sum(partial_rows(f[1]) for f in firsts)
            sums[layer, 2] += sum(partial_rows(g) for g in g3)
            sums[layer, 3] += sum(partial_rows(g) for g in g2)
            s = rows_of(t * CELL, CELL)
            left = jnp.concatenate([onehot[s, :], e_in[s, :]], 1)
            tt[layer, t] = dot_tn(jnp.concatenate(low1, 0), left)
            dw2[layer] += dot_tn(jnp.concatenate(low2, 0), a1[s, :])
            dw3[layer] += dot_tn(jnp.concatenate(low3, 0), a2[s, :])
            if layer == 0:
                pltpu.make_async_copy(ge.at[s], grad_edges.at[s], out_sem.at[1, t]).start()

                @pl.when(t == 1)
                def _():
                    sum1.scatter_finish()
                    sum1.column_start()

                @pl.when(t == 3)
                def _():
                    sum1.column_finish()
                    sum1.gather_start()

            return carry

        lax.fori_loop(0, 4, body, 0)

    def rim_copy(layer, k):
        dx, dy = DIRS[k]
        src = sender_low.at[layer, span(dx, 0, 3, pl.ds(1, 2)), span(dy, 0, 3, pl.ds(1, 2))]
        dst = rim_in.at[layer, k, 0] if dx != 0 and dy != 0 else rim_in.at[layer, k]
        return pltpu.make_async_remote_copy(
            src_ref=src,
            dst_ref=dst,
            send_sem=rim_send.at[layer, k],
            recv_sem=rim_recv.at[layer, k],
            device_id=neighbour(dx, dy),
            device_id_type=MESH,
        )

    def rims_start(layer):
        sender_sum[...] = jnp.zeros_like(sender_sum)
        for c in range(4):
            i, j = c // 2, c % 2
            by_row = tt[layer, c, :, 0:384].T
            for a in range(3):
                piece = by_row[96 * a : 96 * a + 96].reshape(3, 32, D)
                for b in range(3):
                    sender_sum[i + a, j + b] += piece[b]
            receiver_sum[32 * c : 32 * c + 32, :] = by_row[288:320]
            sums[layer, 4] += jnp.where(iota((8, D), 0) == 0, by_row[320:328], 0.0)
        sender_low[layer] = sender_sum[...].astype(BF)
        for k in range(8):
            rim_copy(layer, k).start()

    def edge_grads(layer, h, dst, row, vec):
        dst[row : row + 128, :] = dot_tn(h, receiver_sum[...].astype(BF)).astype(BF)
        senders = dot_tn(tab[layer].reshape(512, D), sender_low[layer].reshape(512, D))
        dst[row + 128 : row + 256, :] = senders.astype(BF)
        by_edge = sum(tt[layer, c, :, 384:512] for c in range(4))
        dst[row + 256 : row + 384, :] = by_edge.T.astype(BF)
        dst[row + 384 : row + 512, :] = dw2[layer].T.astype(BF)
        dst[row + 512 : row + 640, :] = dw3[layer].T.astype(BF)
        s = [column_sum(sums[layer, k]) for k in range(5)]
        vec.extend([s[4], s[3], s[2], s[0] / egain[layer : layer + 1, :], s[1]])

    def rims_finish(layer, gh):
        for k in range(8):
            copy = rim_copy(layer, k)
            copy.wait_send()
            copy.wait_recv()
        own = [sender_sum[1 + c // 2, 1 + c % 2] for c in range(4)]
        for k, (dx, dy) in enumerate(DIRS):
            fits = jnp.bool_(True)
            if dx != 0:
                fits = gx != (0 if dx > 0 else 31)
            if dy != 0:
                fits = fits & (gy != (0 if dy > 0 else 3))
            scale = jnp.where(fits, 1.0, 0.0)
            cells = [
                (i, j)
                for i in ((0, 1) if dx == 0 else ((0,) if dx > 0 else (1,)))
                for j in ((0, 1) if dy == 0 else ((0,) if dy > 0 else (1,)))
            ]
            for at, (i, j) in enumerate(cells):
                own[2 * i + j] = own[2 * i + j] + scale * rim_in[layer, k, at].astype(F32)
        own = jnp.concatenate(own, 0).astype(BF)
        gh = gh + dot_nt(gz1_buf[...], nw1[layer, 0:D, :])
        gh = gh + dot_nt(receiver_sum[...].astype(BF), ew1[layer, 0:D, :])
        return gh + dot_nt(own, ew1[layer, D : 2 * D, :])

    def put_vectors(dst, row, vec):
        at = iota((16, D), 0)
        block = jnp.zeros((16, D), F32)
        for k, v in enumerate(vec):
            block = jnp.where(at == k, v, block)
        dst[row : row + 16, :] = block.astype(BF)

    halo_finish(0)
    prepare(0)
    forward(0)
    h1 = node_forward(0, nodes[...])
    halo_start(1, h1)
    halo_finish(1)
    prepare(1)
    forward(1)
    own1 = jnp.concatenate([tab[1, 1 + c // 2, 1 + c % 2] for c in range(4)], 0)
    nodes_out[...] = node_forward(1, own1)

    vec1 = []
    gh_buf[...] = ct_nodes[...].astype(F32)
    src1[VEC1 + 16 :, :] = jnp.zeros((CH1 * 16 - VEC1 - 16, D), BF)
    src0[VEC0 + 16 :, :] = jnp.zeros((CH0 * 16 - VEC0 - 16, D), BF)
    node_backward(1, own1, gh_buf[...], src1, NODE_W1, vec1)
    backward(1)
    rims_start(1)
    edge_grads(1, own1, src1, EDGE_W1, vec1)
    gh_buf[...] = rims_finish(1, gh_buf[...])

    node_backward(0, nodes[...], gh_buf[...], src1, NODE0, vec1)
    put_vectors(src1, VEC1, vec1)
    sum1.scatter_start()
    backward(0)
    rims_start(0)
    vec0 = []
    edge_grads(0, nodes[...], src0, EDGE_W1, vec0)
    put_vectors(src0, VEC0, vec0)
    sum0.scatter_start()
    grad_nodes[...] = rims_finish(0, gh_buf[...])
    sum0.scatter_finish()
    sum0.column_start()
    sum1.gather_finish()
    sum0.column_finish()
    sum0.gather_start()
    for t in range(4):
        s = rows_of(t * CELL, CELL)
        pltpu.make_async_copy(e2.at[s], edges_out.at[s], out_sem.at[0, t]).wait()
        pltpu.make_async_copy(ge.at[s], grad_edges.at[s], out_sem.at[1, t]).wait()
    sum0.gather_finish()


def unpack_kernel(sum1, sum0, *outs):
    w1, b1, w2, b2, w3, b3, gain, shift, v1, c1, v2, c2, v3, c3, ngain, nshift = outs

    def put(ref, layer, buffer, row):
        height = ref.shape[1]
        ref[layer] = buffer[row : row + height, :].astype(F32)

    for layer, buffer, row in ((1, sum1, 0), (0, sum0, 0)):
        put(w1, layer, buffer, row + EDGE_W1)
        put(w2, layer, buffer, row + EDGE_W2)
        put(w3, layer, buffer, row + EDGE_W3)
    for layer, row in ((1, 0), (0, NODE0 - NODE_W1)):
        put(v1, layer, sum1, row + NODE_W1)
        put(v2, layer, sum1, row + NODE_W2)
        put(v3, layer, sum1, row + NODE_W3)
    first = sum1[VEC1 : VEC1 + 16, :].astype(F32)
    second = sum0[VEC0 : VEC0 + 16, :].astype(F32)
    for k, ref in enumerate((c1, c2, c3, ngain, nshift)):
        ref[1:2, :] = first[k : k + 1]
        ref[0:1, :] = first[10 + k : 11 + k]
    for k, ref in enumerate((b1, b2, b3, gain, shift)):
        ref[1:2, :] = first[5 + k : 6 + k]
        ref[0:1, :] = second[k : k + 1]


def per_device(nodes, edges, nbr_index, nbr_mask, *rest):
    weights, ct_nodes, ct_edges = rest[:16], rest[16], rest[17]
    vmem = pl.BlockSpec(memory_space=pltpu.VMEM)
    hbm = pl.BlockSpec(memory_space=pl.ANY)
    shape = jax.ShapeDtypeStruct
    big = pltpu.VMEM((ROWS, D), BF)
    node_bf = pltpu.VMEM((2, PARTS, D), BF)
    node_f32 = pltpu.VMEM((2, PARTS, D), F32)
    square = pltpu.VMEM((2, D, D), BF)
    dma = pltpu.SemaphoreType.DMA

    def sum_scratch(chunk):
        return [
            pltpu.VMEM((16 * chunk, D), BF),
            pltpu.VMEM((16, chunk, D), BF),
            pltpu.VMEM((8, chunk, D), BF),
        ]

    scratch = [
        pltpu.VMEM((ROWS, 3 * D), BF),
        big, big, big, big,
        *([big] * 12),
        pltpu.VMEM((ROWS, D), F32),
        pltpu.VMEM((PARTS, D), F32),
        pltpu.VMEM((2, 4, 4, 32, D), BF),
        pltpu.VMEM((4, 4 * D, D), BF),
        square, square, square, square, square,
        pltpu.VMEM((D, D), BF),
        pltpu.VMEM((PARTS, D), F32),
        pltpu.VMEM((PARTS, D), F32),
        pltpu.VMEM((2, 4, D, 4 * D), F32),
        pltpu.VMEM((2, D, D), F32),
        pltpu.VMEM((2, D, D), F32),
        pltpu.VMEM((2, 5, 8, D), F32),
        pltpu.VMEM((4, 4, 32, D), F32),
        pltpu.VMEM((2, 4, 4, 32, D), BF),
        pltpu.VMEM((PARTS, D), F32),
        pltpu.VMEM((2, 8, 2, 32, D), BF),
        node_bf, node_bf, node_bf, node_f32, node_f32, node_f32, node_f32,
        pltpu.VMEM((PARTS, D), BF),
        pltpu.VMEM((PARTS, D), F32),
        *sum_scratch(CH1),
        *sum_scratch(CH0),
        dma((2, 4)), dma((2, 4)), dma((2, 8)), dma((2, 8)), dma((2, 8)), dma((2, 8)),
        *([dma((15,)), dma((16,)), dma((7,)), dma((8,)), dma((15,)), dma((16,))] * 2),
    ]
    nodes_out, edges_out, grad_nodes, grad_edges, sum1, sum0 = pl.pallas_call(
        main_kernel,
        out_shape=(
            shape((PARTS, D), BF),
            shape((ROWS, D), BF),
            shape((PARTS, D), F32),
            shape((ROWS, D), F32),
            shape((16 * CH1, D), BF),
            shape((16 * CH0, D), BF),
        ),
        in_specs=[vmem, hbm] + [vmem] * 19 + [hbm],
        out_specs=(vmem, hbm, vmem, hbm, vmem, vmem),
        scratch_shapes=scratch,
        compiler_params=pltpu.CompilerParams(
            collective_id=0, has_side_effects=True, vmem_limit_bytes=60 * 1024 * 1024
        ),
        name="interaction_layers",
    )(
        nodes.reshape(PARTS, D),
        edges.reshape(ROWS, D),
        nbr_index.reshape(PARTS, 64),
        nbr_mask.reshape(PARTS, 64),
        *weights,
        ct_nodes.reshape(PARTS, D),
        ct_edges.reshape(ROWS, D),
    )
    grads = pl.pallas_call(
        unpack_kernel,
        out_shape=tuple(shape(w.shape, F32) for w in weights),
        in_specs=[vmem, vmem],
        out_specs=(vmem,) * 16,
        name="unpack_sums",
    )(sum1, sum0)
    return (
        nodes_out.reshape(nodes.shape),
        edges_out.reshape(edges.shape),
        grad_nodes.reshape(nodes.shape),
        grad_edges.reshape(edges.shape),
        *grads,
    )


def solution(mesh):
    cells = P("gx", "gy", None, None)
    wide = P("gx", "gy", None, None, None)
    in_specs = (cells, wide, cells, cells) + (P(),) * 16 + (cells, wide)
    out_specs = (cells, wide, cells, wide) + (P(),) * 16
    return jax.shard_map(
        per_device, mesh=mesh, in_specs=in_specs, out_specs=out_specs, check_vma=False
    )
```

```python
import functools

import jax
import jax.numpy as jnp
from jax import lax
from jax.experimental import pallas as pl
from jax.experimental.pallas import tpu as pltpu
from jax.sharding import PartitionSpec as P

EPS = 1e-05
BF = jnp.bfloat16
F32 = jnp.float32
MESH = pl.DeviceIdType.MESH

D = 128
ROWS = 8192
CELL = 2048
SUB = 4
PARTS = 128

DIRS = tuple((dx, dy) for dx in (-1, 0, 1) for dy in (-1, 0, 1) if (dx, dy) != (0, 0))
PLANE = tuple((dx, dy) for dx in range(4) for dy in range(4) if (dx, dy) != (0, 0))
COLUMN = tuple((dz, dg) for dz in range(2) for dg in range(4) if (dz, dg) != (0, 0))

CH1 = 80
CHN = 32
CH0 = 48
EDGE_W1, EDGE_W2, EDGE_W3 = 0, 384, 512
NODE_W1, NODE_W2, NODE_W3 = 640, 896, 1024
VEC1 = 1152
VEC0 = 640
FIRST_HALO = ((3, 1), (3, 2), (3, 3), (1, 3), (2, 3))
OTHER_HALO = ((0, 0), (0, 1), (0, 2), (0, 3), (1, 0), (2, 0), (3, 0))


def dot(a, b):
    return jnp.dot(a, b, preferred_element_type=F32)


def dot_nt(a, b):
    return lax.dot_general(a, b, (((1,), (1,)), ((), ())), preferred_element_type=F32)


def dot_tn(a, b):
    return lax.dot_general(a, b, (((0,), (0,)), ((), ())), preferred_element_type=F32)


def iota(shape, dim):
    return lax.broadcasted_iota(jnp.int32, shape, dim)


def silu_parts(half):
    wide = 1.0 + jnp.tanh(half)
    act = half * wide
    slope = wide * (0.5 + half - 0.5 * act)
    return act, slope


def rows_of(start, count):
    return pl.ds(pl.multiple_of(start, count), count)


def partial_rows(x):
    return jnp.sum(x.reshape(-1, 8, D), 0)


def column_sum(x):
    return jnp.sum(x, 0, keepdims=True)


def span(step, low, high, both):
    return low if step < 0 else (high if step > 0 else both)


class Sum:
    def __init__(self, chunk, refs, place):
        self.chunk = chunk
        self.src, self.part, self.col, self.out = refs[:4]
        self.send1, self.recv1, self.send2, self.recv2, self.send3, self.recv3 = refs[4:]
        self.gx, self.gy = place
        self.x, self.z, self.y = self.gx // 8, (self.gx // 4) % 2, self.gx % 4
        self.me = self.x * 4 + self.y
        self.mine = self.z * 4 + self.gy

    def plane_copy(self, k, dx, dy, src, dst, send, recv, slot):
        px, py = (self.x + dx) % 4, (self.y + dy) % 4
        return pltpu.make_async_remote_copy(
            src_ref=src,
            dst_ref=dst,
            send_sem=send.at[k],
            recv_sem=recv.at[slot],
            device_id=((px * 2 + self.z) * 4 + py, self.gy),
            device_id_type=MESH,
        )

    def rows(self, index):
        return pl.ds(pl.multiple_of(index * self.chunk, 16), self.chunk)

    def scatter_start(self):
        for k, (dx, dy) in enumerate(PLANE):
            peer = ((self.x + dx) % 4) * 4 + (self.y + dy) % 4
            self.plane_copy(
                k, dx, dy, self.src.at[self.rows(peer)], self.part.at[self.me], self.send1, self.recv1, self.me
            ).start()
        self.part[self.me] = self.src[self.rows(self.me), :]

    def scatter_finish(self):
        for k, (dx, dy) in enumerate(PLANE):
            peer = ((self.x - dx) % 4) * 4 + (self.y - dy) % 4
            copy = self.plane_copy(
                k, dx, dy, self.src.at[self.rows(peer)], self.part.at[peer], self.send1, self.recv1, peer
            )
            copy.wait_send()
            copy.wait_recv()
        total = self.part[0].astype(F32)
        for k in range(1, 16):
            total = total + self.part[k].astype(F32)
        self.col[self.mine] = total.astype(BF)

    def column_copy(self, k, dz, dg, slot):
        pz, pg = (self.z + dz) % 2, (self.gy + dg) % 4
        return pltpu.make_async_remote_copy(
            src_ref=self.col.at[self.mine],
            dst_ref=self.col.at[slot],
            send_sem=self.send2.at[k],
            recv_sem=self.recv2.at[slot],
            device_id=((self.x * 2 + pz) * 4 + self.y, pg),
            device_id_type=MESH,
        )

    def column_start(self):
        for k, (dz, dg) in enumerate(COLUMN):
            self.column_copy(k, dz, dg, self.mine).start()

    def column_finish(self):
        for k, (dz, dg) in enumerate(COLUMN):
            peer = ((self.z - dz) % 2) * 4 + (self.gy - dg) % 4
            copy = self.column_copy(k, dz, dg, peer)
            copy.wait_send()
            copy.wait_recv()
        total = self.col[0].astype(F32)
        for k in range(1, 8):
            total = total + self.col[k].astype(F32)
        self.out[self.rows(self.me), :] = total.astype(BF)

    def gather_start(self):
        own = self.out.at[self.rows(self.me)]
        for k, (dx, dy) in enumerate(PLANE):
            self.plane_copy(k, dx, dy, own, own, self.send3, self.recv3, self.me).start()

    def gather_finish(self):
        for k, (dx, dy) in enumerate(PLANE):
            peer = ((self.x - dx) % 4) * 4 + (self.y - dy) % 4
            landing = self.out.at[self.rows(peer)]
            copy = self.plane_copy(k, dx, dy, landing, landing, self.send3, self.recv3, peer)
            copy.wait_send()
            copy.wait_recv()


def main_kernel(*refs):
    (
        nodes, edges, index, mask,
        ew1, eb1, ew2, eb2, ew3, eb3, egain, eshift,
        nw1, nb1, nw2, nb2, nw3, nb3, ngain, nshift,
        ct_nodes, ct_edges,
        nodes_out, e2, grad_nodes, ge, sum1_out, sumn_out, sum0_out,
        onehot, e0, e1, ct,
        a1_0, s1_0, a2_0, s2_0, n_0, r_0,
        a1_1, s1_1, a2_1, s2_1, n_1, r_1,
        live_count,
        tab, wbig, w2half, w3mid, w1et, w2t, w3t, averager,
        msum, gm, tt, dw2, dw3, sums,
        sender_sum, sender_low, receiver_sum, rim_in,
        nm, nc1, nc2, nsl1, nsl2, nnorm, ninv, gz1_buf, gh_buf,
        src1, part1, col1, srcn, partn, coln, src0, part0, col0,
        in_sem, halo_send, halo_recv, cell_send, cell_recv, rim_send, rim_recv,
        *sum_sems,
    ) = refs
    gx, gy = lax.axis_index("gx"), lax.axis_index("gy")
    sum1 = Sum(CH1, (src1, part1, col1, sum1_out, *sum_sems[:6]), (gx, gy))
    sumn = Sum(CHN, (srcn, partn, coln, sumn_out, *sum_sems[6:12]), (gx, gy))
    sum0 = Sum(CH0, (src0, part0, col0, sum0_out, *sum_sems[12:]), (gx, gy))
    kept = ((a1_0, s1_0, a2_0, s2_0, n_0, r_0), (a1_1, s1_1, a2_1, s2_1, n_1, r_1))
    edge_in = (e0, e1, e2)

    def neighbour(dx, dy):
        return (lax.rem(gx + dx + 32, 32), lax.rem(gy + dy + 4, 4))

    def load(ref, scratch, which, t):
        s = rows_of(t * CELL, CELL)
        return pltpu.make_async_copy(ref.at[s], scratch.at[s], in_sem.at[which, t])

    for t in range(4):
        load(edges, e0, 0, t).start()

    barrier = pltpu.get_barrier_semaphore()
    x, z, y = sum1.x, sum1.z, sum1.y
    partners = [neighbour(dx, dy) for dx, dy in DIRS]
    partners += [(((x + dx) % 4 * 2 + z) * 4 + (y + dy) % 4, gy) for dx, dy in PLANE]
    partners += [((x * 2 + (z + dz) % 2) * 4 + y, (gy + dg) % 4) for dz, dg in COLUMN]
    for partner in partners:
        pl.semaphore_signal(barrier, inc=1, device_id=partner, device_id_type=MESH)
    pl.semaphore_wait(barrier, len(partners))

    def halo_copy(k):
        dx, dy = DIRS[k]
        src = tab.at[0, span(dx, 1, 2, pl.ds(1, 2)), span(dy, 1, 2, pl.ds(1, 2))]
        dst = tab.at[0, span(dx, 3, 0, pl.ds(1, 2)), span(dy, 3, 0, pl.ds(1, 2))]
        return pltpu.make_async_remote_copy(
            src_ref=src,
            dst_ref=dst,
            send_sem=halo_send.at[k],
            recv_sem=halo_recv.at[k],
            device_id=neighbour(dx, dy),
            device_id_type=MESH,
        )

    def clear_outside(layer, places):
        blank = jnp.zeros((32, D), BF)
        for outside, dim, at in ((gx == 0, 0, 0), (gx == 31, 0, 3), (gy == 0, 1, 0), (gy == 3, 1, 3)):
            chosen = [place for place in places if place[dim] == at]
            if chosen:

                @pl.when(outside)
                def _():
                    for a, b in chosen:
                        tab[layer, a, b] = blank

    def halo_start(latents):
        for cell in range(4):
            tab[0, 1 + cell // 2, 1 + cell % 2] = latents[32 * cell : 32 * cell + 32]
        for k in range(8):
            halo_copy(k).start()

    def halo_finish():
        for k in range(8):
            copy = halo_copy(k)
            copy.wait_send()
            copy.wait_recv()
        clear_outside(0, FIRST_HALO + OTHER_HALO)

    def cell_copy(c, k):
        i, j = c // 2, c % 2
        dx = 2 * i - 1 if k != 1 else 0
        dy = 2 * j - 1 if k != 0 else 0
        a = 3 - 3 * i if k != 1 else 1 + i
        b = 3 - 3 * j if k != 0 else 1 + j
        return pltpu.make_async_remote_copy(
            src_ref=tab.at[1, 1 + i, 1 + j],
            dst_ref=tab.at[1, a, b],
            send_sem=cell_send.at[c, k],
            recv_sem=cell_recv.at[a, b],
            device_id=neighbour(dx, dy),
            device_id_type=MESH,
        )

    def cell_start(c):
        for k in range(3):
            cell_copy(c, k).start()

    def cells_arrive(places):
        for a, b in places:
            pltpu.make_async_remote_copy(
                src_ref=tab.at[1, 1, 1],
                dst_ref=tab.at[1, a, b],
                send_sem=cell_send.at[0, 0],
                recv_sem=cell_recv.at[a, b],
                device_id=neighbour(1, 0),
                device_id_type=MESH,
            ).wait_recv()
        clear_outside(1, places)

    halo_start(nodes[...])
    for t in range(4):
        load(ct_edges, ct, 1, t).start()

    averager[...] = jnp.full((D, D), 1.0 / D, BF)
    for layer in range(2):
        w2half[layer] = (0.5 * ew2[layer].astype(F32)).astype(BF)
        w3 = ew3[layer].astype(F32)
        w3mid[layer] = (w3 - jnp.mean(w3, -1, keepdims=True)).astype(BF)
        w3t[layer] = ew3[layer].T
        w2t[layer] = ew2[layer].T
        w1et[layer] = ew1[layer, 2 * D : 3 * D, :].T
    msum[...] = jnp.zeros_like(msum)
    sums[...] = jnp.zeros_like(sums)
    tt[...] = jnp.zeros_like(tt)
    dw2[...] = jnp.zeros_like(dw2)
    dw3[...] = jnp.zeros_like(dw3)

    count = jnp.sum(mask[...].astype(F32), -1, keepdims=True)
    live_count[...] = jnp.broadcast_to(count, (PARTS, D))
    cell_of = iota((PARTS, 64), 0) // 32
    place = index[...] - (cell_of // 2) * 128 - (cell_of % 2) * 32
    place = (place // 128) * 96 + place % 128
    dead = mask[...] == 0
    high = jnp.where(dead, 127, place // 16)
    low = jnp.where(dead, 0, place % 16)
    digits = jnp.concatenate([high, low], 1).astype(F32).astype(BF)
    spread = jnp.where(iota((D, D), 0) < 64, 16.0, 1.0).astype(BF)

    def onehot_step(t, carry):
        row = iota((CELL, D), 0)
        lane = iota((CELL, D), 1)
        pick = jnp.where(lane == t * 32 + row // 64, 1.0, 0.0).astype(BF)
        spread_out = dot(pick, digits)
        own = jnp.where(lane % 64 == row % 64, spread_out, 0.0).astype(BF)
        found = dot(own, spread).astype(jnp.int32)
        s = rows_of(t * CELL, CELL)
        onehot[s, 0:128] = jnp.where(found == lane, 1.0, 0.0).astype(BF)
        onehot[s, 128:256] = jnp.where(found == lane + 128, 1.0, 0.0).astype(BF)
        fixed = (lane == 32 + row // 64) | (lane == 64) | (lane == 65)
        onehot[s, 256:384] = jnp.where((found == lane + 256) | fixed, 1.0, 0.0).astype(BF)
        return carry

    lax.fori_loop(0, 4, onehot_step, 0)

    def prepare(layer, cells):
        base = 1 if cells == (3,) else 0
        width = 4 - base
        senders = dot(tab[layer, base:, base:].reshape(width * width * 32, D), ew1[layer, D : 2 * D, :])
        senders = (0.5 * senders).astype(BF).reshape(width, width, 32, D)
        own = jnp.concatenate([tab[layer, 1 + c // 2, 1 + c % 2] for c in cells], 0)
        receivers = (0.5 * dot(own, ew1[layer, 0:D, :])).astype(BF)
        bias = 0.5 * eb1[layer : layer + 1, :]
        bias_high = bias.astype(BF).astype(F32)
        at = iota((64, D), 0)
        bias_rows = jnp.where(at == 0, bias_high, jnp.where(at == 1, bias - bias_high, 0.0)).astype(BF)
        edge_rows = (0.5 * ew1[layer, 2 * D : 3 * D, :].astype(F32)).astype(BF)
        for k, c in enumerate(cells):
            i, j = c // 2 - base, c % 2 - base
            for a in range(3):
                wbig[c, 96 * a : 96 * a + 96, :] = senders[i + a, j : j + 3].reshape(96, D)
            wbig[c, 288:320, :] = receivers[32 * k : 32 * k + 32]
            wbig[c, 320:384, :] = bias_rows
            wbig[c, 384:512, :] = edge_rows

    step = CELL // SUB
    per = step // 64

    def live_of(p):
        slot = iota((per, 64, D), 1).astype(F32)
        return slot < live_count[p, :][:, None, :]

    def forward(layer):
        a1, s1, a2, s2, nn, rr = kept[layer]
        e_in, e_out = edge_in[layer], edge_in[layer + 1]
        b2 = 0.5 * eb2[layer : layer + 1, :]
        b3 = eb3[layer : layer + 1, :]
        b3 = b3 - jnp.mean(b3, -1, keepdims=True)
        gain, shift = egain[layer : layer + 1, :], eshift[layer : layer + 1, :]

        def body(t, carry):
            if layer == 0:
                load(edges, e0, 0, t).wait()
                node_forward(0, jnp.maximum(t - 1, 0))
            c = t if layer == 0 else 3 - t
            groups = [rows_of(c * CELL + g * step, step) for g in range(SUB)]
            ones = [dot(jnp.concatenate([onehot[s, :], e_in[s, :]], 1), wbig[c]) for s in groups]
            first = []
            for s, half in zip(groups, ones):
                act, slope = silu_parts(half)
                a1[s, :] = act.astype(BF)
                s1[s, :] = slope.astype(BF)
                first.append(act.astype(BF))
            twos = [dot(act, w2half[layer]) + b2 for act in first]
            second = []
            for s, half in zip(groups, twos):
                act, slope = silu_parts(half)
                a2[s, :] = act.astype(BF)
                s2[s, :] = slope.astype(BF)
                second.append(act.astype(BF))
            mids = [dot(act, w3mid[layer]) + b3 for act in second]
            spreads = [dot((mid * mid).astype(BF), averager[...]) for mid in mids]
            for g, (s, mid, var) in enumerate(zip(groups, mids, spreads)):
                inverse = lax.rsqrt(var + EPS)
                normed = mid * inverse
                nn[s, :] = normed.astype(BF)
                rr[s, :] = inverse.astype(BF)
                update = (normed * gain + shift).reshape(per, 64, D)
                p = rows_of(c * 32 + g * per, per)
                live = live_of(p)
                new = e_in[s, :].astype(F32).reshape(per, 64, D) + jnp.where(live, update, 0.0)
                new = new.astype(BF)
                e_out[s, :] = new.reshape(step, D)
                msum[p, :] = jnp.sum(jnp.where(live, new.astype(F32), 0.0), 1)
            if layer == 0:

                @pl.when(t > 0)
                def _():
                    cell_start(t - 1)

            else:

                @pl.when(t == 0)
                def _():
                    cells_arrive(OTHER_HALO)
                    prepare(1, (0, 1, 2))

            return carry

        lax.fori_loop(0, 4, body, 0)

    def node_forward(layer, c=None):
        if c is None:
            p = pl.ds(0, PARTS)
            h = jnp.concatenate([tab[layer, 1 + k // 2, 1 + k % 2] for k in range(4)], 0)
        else:
            p = rows_of(c * 32, 32)
            h = tab[layer, 1 + c // 2, 1 + c % 2]
        m = msum[p, :].astype(BF)
        z1 = dot(h, nw1[layer, 0:D, :]) + dot(m, nw1[layer, D : 2 * D, :]) + nb1[layer : layer + 1, :]
        c1, slope1 = silu_parts(0.5 * z1)
        c1 = c1.astype(BF)
        z2 = dot(c1, nw2[layer]) + nb2[layer : layer + 1, :]
        c2, slope2 = silu_parts(0.5 * z2)
        c2 = c2.astype(BF)
        z3 = dot(c2, nw3[layer]) + nb3[layer : layer + 1, :]
        mid = z3 - jnp.mean(z3, -1, keepdims=True)
        inverse = lax.rsqrt(jnp.mean(mid * mid, -1, keepdims=True) + EPS)
        normed = mid * inverse
        nm[layer, p], nc1[layer, p], nc2[layer, p] = m, c1, c2
        nsl1[layer, p], nsl2[layer, p], nnorm[layer, p] = slope1, slope2, normed
        ninv[layer, p] = jnp.broadcast_to(inverse, h.shape)
        update = normed * ngain[layer : layer + 1, :] + nshift[layer : layer + 1, :]
        result = (h.astype(F32) + update).astype(BF)
        if c is None:
            nodes_out[...] = result
        else:
            tab[1, 1 + c // 2, 1 + c % 2] = result

    def node_backward(layer, h, gh, dst, row, vec):
        normed = nnorm[layer]
        q = gh * ngain[layer : layer + 1, :]
        inner = q - jnp.mean(q, -1, keepdims=True) - normed * jnp.mean(q * normed, -1, keepdims=True)
        gz3 = ninv[layer] * inner
        low3 = gz3.astype(BF)
        gz2 = dot_nt(low3, nw3[layer]) * nsl2[layer]
        low2 = gz2.astype(BF)
        gz1 = dot_nt(low2, nw2[layer]) * nsl1[layer]
        low1 = gz1.astype(BF)
        gz1_buf[...] = low1
        gm[...] = dot_nt(low1, nw1[layer, D : 2 * D, :])
        dst[row : row + 128, :] = dot_tn(h, low1).astype(BF)
        dst[row + 128 : row + 256, :] = dot_tn(nm[layer], low1).astype(BF)
        dst[row + 256 : row + 384, :] = dot_tn(nc1[layer], low2).astype(BF)
        dst[row + 384 : row + 512, :] = dot_tn(nc2[layer], low3).astype(BF)
        vec.extend([column_sum(gz1), column_sum(gz2), column_sum(gz3), column_sum(gh * normed), column_sum(gh)])

    def backward(layer):
        a1, s1, a2, s2, nn, rr = kept[layer]
        e_in = edge_in[layer]
        gain = egain[layer : layer + 1, :]

        def body(t, carry):
            if layer == 1:
                load(ct_edges, ct, 1, t).wait()
            groups = [rows_of(t * CELL + g * step, step) for g in range(SUB)]
            firsts = []
            for g, s in enumerate(groups):
                p = rows_of(t * 32 + g * per, per)
                live = live_of(p)
                old = ct[s, :].astype(F32) if layer == 1 else ge[s, :]
                total = old.reshape(per, 64, D) + jnp.where(live, gm[p, :][:, None, :], 0.0)
                gy_ = jnp.where(live, total, 0.0).reshape(step, D)
                normed = nn[s, :].astype(F32)
                q = gy_ * gain
                qn = q * normed
                mean_q = dot(q.astype(BF), averager[...])
                mean_qn = dot(qn.astype(BF), averager[...])
                firsts.append((total.reshape(step, D), gy_, q, qn, normed, mean_q, mean_qn))
            g3 = [
                rr[s, :].astype(F32) * (f[2] - f[5] - f[4] * f[6]) for s, f in zip(groups, firsts)
            ]
            low3 = [g.astype(BF) for g in g3]
            g2 = [dot(g, w3t[layer]) * s2[s, :].astype(F32) for s, g in zip(groups, low3)]
            low2 = [g.astype(BF) for g in g2]
            low1 = [(dot(g, w2t[layer]) * s1[s, :].astype(F32)).astype(BF) for s, g in zip(groups, low2)]
            for s, g, f in zip(groups, low1, firsts):
                ge[s, :] = f[0]
                s1[s, :] = g
            sums[layer, 0] += sum(partial_rows(f[3]) for f in firsts)
            sums[layer, 1] += sum(partial_rows(f[1]) for f in firsts)
            sums[layer, 2] += sum(partial_rows(g) for g in g3)
            sums[layer, 3] += sum(partial_rows(g) for g in g2)
            s = rows_of(t * CELL, CELL)
            left = jnp.concatenate([onehot[s, :], e_in[s, :]], 1)
            tt[layer, t] = dot_tn(jnp.concatenate(low1, 0), left)
            if layer == 1:
                for s, two, three in zip(groups, low2, low3):
                    s2[s, :] = two
                    nn[s, :] = three
            else:
                dw2[layer] += dot_tn(jnp.concatenate(low2, 0), a1[s, :])
                dw3[layer] += dot_tn(jnp.concatenate(low3, 0), a2[s, :])

                @pl.when(t == 0)
                def _():
                    sum1.scatter_finish()
                    sum1.column_start()

                @pl.when(t == 1)
                def _():
                    sumn.scatter_finish()
                    sumn.column_start()
                    sum1.column_finish()
                    sum1.gather_start()

                @pl.when(t == 2)
                def _():
                    sumn.column_finish()
                    sumn.gather_start()

            return carry

        lax.fori_loop(0, 4, body, 0)

    def backward_rest(layer):
        a1, s1, a2, s2, nn, rr = kept[layer]

        def body(t, carry):
            s = rows_of(t * CELL, CELL)
            ge[s, :] += dot(s1[s, :], w1et[layer])
            if layer == 1:
                dw2[layer] += dot_tn(s2[s, :], a1[s, :])
                dw3[layer] += dot_tn(nn[s, :], a2[s, :])
            return carry

        lax.fori_loop(0, 4, body, 0)

    def rim_copy(layer, k):
        dx, dy = DIRS[k]
        src = sender_low.at[layer, span(dx, 0, 3, pl.ds(1, 2)), span(dy, 0, 3, pl.ds(1, 2))]
        dst = rim_in.at[layer, k, 0] if dx != 0 and dy != 0 else rim_in.at[layer, k]
        return pltpu.make_async_remote_copy(
            src_ref=src,
            dst_ref=dst,
            send_sem=rim_send.at[layer, k],
            recv_sem=rim_recv.at[layer, k],
            device_id=neighbour(dx, dy),
            device_id_type=MESH,
        )

    def rims_start(layer):
        sender_sum[...] = jnp.zeros_like(sender_sum)
        for c in range(4):
            i, j = c // 2, c % 2
            by_row = tt[layer, c, :, 0:384].T
            for a in range(3):
                piece = by_row[96 * a : 96 * a + 96].reshape(3, 32, D)
                for b in range(3):
                    sender_sum[i + a, j + b] += piece[b]
            receiver_sum[32 * c : 32 * c + 32, :] = by_row[288:320]
            sums[layer, 4] += jnp.where(iota((8, D), 0) == 0, by_row[320:328], 0.0)
        sender_low[layer] = sender_sum[...].astype(BF)
        for k in range(8):
            rim_copy(layer, k).start()

    def edge_grads(layer, h, dst, row, vec):
        dst[row : row + 128, :] = dot_tn(h, receiver_sum[...].astype(BF)).astype(BF)
        senders = dot_tn(tab[layer].reshape(512, D), sender_low[layer].reshape(512, D))
        dst[row + 128 : row + 256, :] = senders.astype(BF)
        by_edge = sum(tt[layer, c, :, 384:512] for c in range(4))
        dst[row + 256 : row + 384, :] = by_edge.T.astype(BF)
        dst[row + 384 : row + 512, :] = dw2[layer].T.astype(BF)
        dst[row + 512 : row + 640, :] = dw3[layer].T.astype(BF)
        s = [column_sum(sums[layer, k]) for k in range(5)]
        vec.extend([s[4], s[3], s[2], s[0] / egain[layer : layer + 1, :], s[1]])

    def rims_finish(layer, gh):
        for k in range(8):
            copy = rim_copy(layer, k)
            copy.wait_send()
            copy.wait_recv()
        own = [sender_sum[1 + c // 2, 1 + c % 2] for c in range(4)]
        for k, (dx, dy) in enumerate(DIRS):
            fits = jnp.bool_(True)
            if dx != 0:
                fits = gx != (0 if dx > 0 else 31)
            if dy != 0:
                fits = fits & (gy != (0 if dy > 0 else 3))
            scale = jnp.where(fits, 1.0, 0.0)
            cells = [
                (i, j)
                for i in ((0, 1) if dx == 0 else ((0,) if dx > 0 else (1,)))
                for j in ((0, 1) if dy == 0 else ((0,) if dy > 0 else (1,)))
            ]
            for at, (i, j) in enumerate(cells):
                own[2 * i + j] = own[2 * i + j] + scale * rim_in[layer, k, at].astype(F32)
        own = jnp.concatenate(own, 0).astype(BF)
        gh = gh + dot_nt(gz1_buf[...], nw1[layer, 0:D, :])
        gh = gh + dot_nt(receiver_sum[...].astype(BF), ew1[layer, 0:D, :])
        return gh + dot_nt(own, ew1[layer, D : 2 * D, :])

    def put_vectors(dst, row, vec):
        at = iota((16, D), 0)
        block = jnp.zeros((16, D), F32)
        for k, v in enumerate(vec):
            block = jnp.where(at == k, v, block)
        dst[row : row + 16, :] = block.astype(BF)

    halo_finish()
    prepare(0, (0, 1, 2, 3))
    forward(0)
    node_forward(0, 3)
    cell_start(3)
    cells_arrive(FIRST_HALO)
    prepare(1, (3,))
    forward(1)
    node_forward(1)
    for c in range(4):
        for k in range(3):
            cell_copy(c, k).wait_send()

    vec1, vec0 = [], []
    gh_buf[...] = ct_nodes[...].astype(F32)
    src1[VEC1 + 16 :, :] = jnp.zeros((CH1 * 16 - VEC1 - 16, D), BF)
    src0[VEC0 + 16 :, :] = jnp.zeros((CH0 * 16 - VEC0 - 16, D), BF)
    own1 = jnp.concatenate([tab[1, 1 + c // 2, 1 + c % 2] for c in range(4)], 0)
    node_backward(1, own1, gh_buf[...], src1, NODE_W1, vec1)
    backward(1)
    rims_start(1)
    backward_rest(1)
    edge_grads(1, own1, src1, EDGE_W1, vec1)
    put_vectors(src1, VEC1, vec1)
    sum1.scatter_start()
    gh_buf[...] = rims_finish(1, gh_buf[...])

    node_backward(0, nodes[...], gh_buf[...], srcn, 0, vec0)
    sumn.scatter_start()
    backward(0)
    rims_start(0)
    edge_grads(0, nodes[...], src0, EDGE_W1, vec0)
    put_vectors(src0, VEC0, vec0)
    sum0.scatter_start()
    backward_rest(0)
    grad_nodes[...] = rims_finish(0, gh_buf[...])
    sum0.scatter_finish()
    sum0.column_start()
    sum1.gather_finish()
    sumn.gather_finish()
    sum0.column_finish()
    sum0.gather_start()
    sum0.gather_finish()


def unpack_kernel(nodes_in, edges_in, grad_nodes_in, grad_edges_in, sum1, sumn, sum0, *rest):
    (nodes_out, edges_out, grad_nodes, grad_edges), outs, sems = rest[:4], rest[4:20], rest[20]
    w1, b1, w2, b2, w3, b3, gain, shift, v1, c1, v2, c2, v3, c3, ngain, nshift = outs
    copies = []
    for t in range(4):
        s = pl.ds(t * CELL, CELL)
        copies.append(pltpu.make_async_copy(grad_edges_in.at[s], grad_edges.at[s], sems.at[0, t]))
        copies.append(pltpu.make_async_copy(edges_in.at[s], edges_out.at[s], sems.at[1, t]))
    for copy in copies:
        copy.start()
    nodes_out[...] = nodes_in[...]
    grad_nodes[...] = grad_nodes_in[...]

    def put(ref, layer, buffer, row):
        height = ref.shape[1]
        ref[layer] = buffer[row : row + height, :].astype(F32)

    for layer, buffer in ((1, sum1), (0, sum0)):
        put(w1, layer, buffer, EDGE_W1)
        put(w2, layer, buffer, EDGE_W2)
        put(w3, layer, buffer, EDGE_W3)
    for layer, buffer, row in ((1, sum1, 0), (0, sumn, -NODE_W1)):
        put(v1, layer, buffer, row + NODE_W1)
        put(v2, layer, buffer, row + NODE_W2)
        put(v3, layer, buffer, row + NODE_W3)
    for layer, block in ((1, sum1[VEC1 : VEC1 + 16, :]), (0, sum0[VEC0 : VEC0 + 16, :])):
        rows = block.astype(F32)
        for k, ref in enumerate((c1, c2, c3, ngain, nshift, b1, b2, b3, gain, shift)):
            ref[layer : layer + 1, :] = rows[k : k + 1]
    for copy in copies:
        copy.wait()


def per_device(nodes, edges, nbr_index, nbr_mask, *rest):
    weights, ct_nodes, ct_edges = rest[:16], rest[16], rest[17]
    vmem = pl.BlockSpec(memory_space=pltpu.VMEM)
    hbm = pl.BlockSpec(memory_space=pl.ANY)
    shape = jax.ShapeDtypeStruct
    big = pltpu.VMEM((ROWS, D), BF)
    node_bf = pltpu.VMEM((2, PARTS, D), BF)
    node_f32 = pltpu.VMEM((2, PARTS, D), F32)
    square = pltpu.VMEM((2, D, D), BF)
    dma = pltpu.SemaphoreType.DMA

    def sum_scratch(chunk):
        return [
            pltpu.VMEM((16 * chunk, D), BF),
            pltpu.VMEM((16, chunk, D), BF),
            pltpu.VMEM((8, chunk, D), BF),
        ]

    scratch = [
        pltpu.VMEM((ROWS, 3 * D), BF),
        big, big, big,
        *([big] * 12),
        pltpu.VMEM((PARTS, D), F32),
        pltpu.VMEM((2, 4, 4, 32, D), BF),
        pltpu.VMEM((4, 4 * D, D), BF),
        square, square, square, square, square,
        pltpu.VMEM((D, D), BF),
        pltpu.VMEM((PARTS, D), F32),
        pltpu.VMEM((PARTS, D), F32),
        pltpu.VMEM((2, 4, D, 4 * D), F32),
        pltpu.VMEM((2, D, D), F32),
        pltpu.VMEM((2, D, D), F32),
        pltpu.VMEM((2, 5, 8, D), F32),
        pltpu.VMEM((4, 4, 32, D), F32),
        pltpu.VMEM((2, 4, 4, 32, D), BF),
        pltpu.VMEM((PARTS, D), F32),
        pltpu.VMEM((2, 8, 2, 32, D), BF),
        node_bf, node_bf, node_bf, node_f32, node_f32, node_f32, node_f32,
        pltpu.VMEM((PARTS, D), BF),
        pltpu.VMEM((PARTS, D), F32),
        *sum_scratch(CH1),
        *sum_scratch(CHN),
        *sum_scratch(CH0),
        dma((2, 4)), dma((8,)), dma((8,)), dma((4, 3)), dma((4, 4)), dma((2, 8)), dma((2, 8)),
        *([dma((15,)), dma((16,)), dma((7,)), dma((8,)), dma((15,)), dma((16,))] * 3),
    ]
    held = pl.pallas_call(
        main_kernel,
        out_shape=(
            pltpu.VMEM((PARTS, D), BF),
            pltpu.VMEM((ROWS, D), BF),
            pltpu.VMEM((PARTS, D), F32),
            pltpu.VMEM((ROWS, D), F32),
            pltpu.VMEM((16 * CH1, D), BF),
            pltpu.VMEM((16 * CHN, D), BF),
            pltpu.VMEM((16 * CH0, D), BF),
        ),
        in_specs=[vmem, hbm] + [vmem] * 19 + [hbm],
        out_specs=(vmem,) * 7,
        scratch_shapes=scratch,
        compiler_params=pltpu.CompilerParams(
            collective_id=0, has_side_effects=True, vmem_limit_bytes=48 * 1024 * 1024
        ),
        name="interaction_layers",
    )(
        nodes.reshape(PARTS, D),
        edges.reshape(ROWS, D),
        nbr_index.reshape(PARTS, 64),
        nbr_mask.reshape(PARTS, 64),
        *weights,
        ct_nodes.reshape(PARTS, D),
        ct_edges.reshape(ROWS, D),
    )
    held = [pltpu.with_memory_space_constraint(value, pltpu.VMEM) for value in held]
    nodes_out, edges_out, grad_nodes, grad_edges, *grads = pl.pallas_call(
        unpack_kernel,
        out_shape=(
            shape((PARTS, D), BF),
            shape((ROWS, D), BF),
            shape((PARTS, D), F32),
            shape((ROWS, D), F32),
            *(shape(w.shape, F32) for w in weights),
        ),
        in_specs=[vmem] * 7,
        out_specs=(vmem, hbm, vmem, hbm) + (vmem,) * 16,
        scratch_shapes=[dma((2, 4))],
        compiler_params=pltpu.CompilerParams(vmem_limit_bytes=8 * 1024 * 1024),
        name="unpack_sums",
    )(*held)
    return (
        nodes_out.reshape(nodes.shape),
        edges_out.reshape(edges.shape),
        grad_nodes.reshape(nodes.shape),
        grad_edges.reshape(edges.shape),
        *grads,
    )


def solution(mesh):
    cells = P("gx", "gy", None, None)
    wide = P("gx", "gy", None, None, None)
    in_specs = (cells, wide, cells, cells) + (P(),) * 16 + (cells, wide)
    out_specs = (cells, wide, cells, wide) + (P(),) * 16
    return jax.shard_map(
        per_device, mesh=mesh, in_specs=in_specs, out_specs=out_specs, check_vma=False
    )
```

```python
import functools

import jax
import jax.numpy as jnp
from jax import lax
from jax.experimental import pallas as pl
from jax.experimental.pallas import tpu as pltpu
from jax.sharding import PartitionSpec as P

EPS = 1e-05
BF = jnp.bfloat16
F32 = jnp.float32
MESH = pl.DeviceIdType.MESH

D = 128
ROWS = 8192
CELL = 2048
SUB = 4
PARTS = 128

DIRS = tuple((dx, dy) for dx in (-1, 0, 1) for dy in (-1, 0, 1) if (dx, dy) != (0, 0))
PLANE = tuple((dx, dy) for dx in range(4) for dy in range(4) if (dx, dy) != (0, 0))
COLUMN = tuple((dz, dg) for dz in range(2) for dg in range(4) if (dz, dg) != (0, 0))

CH1 = 80
CHN = 32
CH0 = 48
EDGE_W1, EDGE_W2, EDGE_W3 = 0, 384, 512
NODE_W1, NODE_W2, NODE_W3 = 640, 896, 1024
VEC1 = 1152
VEC0 = 640


def dot(a, b):
    return jnp.dot(a, b, preferred_element_type=F32)


def dot_nt(a, b):
    return lax.dot_general(a, b, (((1,), (1,)), ((), ())), preferred_element_type=F32)


def dot_tn(a, b):
    return lax.dot_general(a, b, (((0,), (0,)), ((), ())), preferred_element_type=F32)


def iota(shape, dim):
    return lax.broadcasted_iota(jnp.int32, shape, dim)


def silu_parts(half):
    wide = 1.0 + jnp.tanh(half)
    act = half * wide
    slope = wide * (0.5 + half - 0.5 * act)
    return act, slope


def rows_of(start, count):
    if isinstance(start, int):
        return slice(start, start + count)
    return pl.ds(pl.multiple_of(start, count), count)


def partial_rows(x):
    return jnp.sum(x.reshape(-1, 8, D), 0)


def column_sum(x):
    return jnp.sum(x, 0, keepdims=True)


def span(step, low, high, both):
    return low if step < 0 else (high if step > 0 else both)


def drain(view, sem):
    pltpu.make_async_copy(view, view, sem).wait()


class Sum:
    def __init__(self, chunk, refs, place):
        self.chunk = chunk
        self.src, self.part, self.col, self.out = refs[:4]
        self.sems = refs[4]
        self.gx, self.gy = place
        self.x, self.z, self.y = self.gx // 8, (self.gx // 4) % 2, self.gx % 4
        self.me = self.x * 4 + self.y
        self.mine = self.z * 4 + self.gy

    def rows(self, index):
        return pl.ds(pl.multiple_of(index * self.chunk, 16), self.chunk)

    def send(self, src, dst, phase, device):
        pltpu.make_async_remote_copy(
            src_ref=src,
            dst_ref=dst,
            send_sem=self.sems.at[phase, 0],
            recv_sem=self.sems.at[phase, 1],
            device_id=device,
            device_id_type=MESH,
        ).start()

    def wait(self, view, phase):
        drain(view, self.sems.at[phase, 0])
        drain(view, self.sems.at[phase, 1])

    def scatter_start(self):
        for dx, dy in PLANE:
            px, py = (self.x + dx) % 4, (self.y + dy) % 4
            src = self.src.at[self.rows(px * 4 + py)]
            self.send(src, self.part.at[self.me], 0, ((px * 2 + self.z) * 4 + py, self.gy))
        self.part[self.me] = self.src[self.rows(self.me), :]

    def scatter_finish(self):
        self.wait(self.part.at[pl.ds(0, 15)], 0)
        total = self.part[0].astype(F32)
        for k in range(1, 16):
            total = total + self.part[k].astype(F32)
        self.col[self.mine] = total.astype(BF)

    def column_start(self):
        own = self.col.at[self.mine]
        for dz, dg in COLUMN:
            pz, pg = (self.z + dz) % 2, (self.gy + dg) % 4
            self.send(own, own, 1, ((self.x * 2 + pz) * 4 + self.y, pg))

    def column_finish(self):
        self.wait(self.col.at[pl.ds(0, 7)], 1)
        total = self.col[0].astype(F32)
        for k in range(1, 8):
            total = total + self.col[k].astype(F32)
        self.out[self.rows(self.me), :] = total.astype(BF)

    def gather_start(self):
        own = self.out.at[self.rows(self.me)]
        for dx, dy in PLANE:
            px, py = (self.x + dx) % 4, (self.y + dy) % 4
            self.send(own, own, 2, ((px * 2 + self.z) * 4 + py, self.gy))

    def gather_finish(self):
        self.wait(self.out.at[pl.ds(0, 15 * self.chunk)], 2)


def main_kernel(*refs):
    (
        nodes_hbm, edges, index_hbm, mask_hbm, *weights_hbm,
    ) = refs[:20]
    ct_nodes_hbm, ct_edges = refs[20:22]
    (
        nodes_out, e2, grad_nodes, ge, sum1_out, sumn_out, sum0_out,
        index, mask,
        ew1, eb1, ew2, eb2, ew3, eb3, egain, eshift,
        nw1, nb1, nw2, nb2, nw3, nb3, ngain, nshift,
        ct_nodes,
        onehot, e0, e1, ct,
        a1_0, s1_0, a2_0, s2_0, n_0, r_0,
        a1_1, s1_1, a2_1, s2_1, n_1, r_1,
        live_count,
        tab, wbig, w2half, w3mid, w1et, w2t, w3t, averager,
        msum, gm, tt, dw2, dw3, sums,
        sender_sum, sender_low, receiver_sum, rim_in,
        nm, nc1, nc2, nsl1, nsl2, nnorm, ninv, gz, gh_buf,
        src1, part1, col1, srcn, partn, coln, src0, part0, col0,
        slot_mask, fixed,
        in_sem, weight_sem, halo_sem, cell_send, cell_recv, rim_sem,
        *sum_sems,
    ) = refs[22:]
    gx, gy = lax.axis_index("gx"), lax.axis_index("gy")
    sum1 = Sum(CH1, (src1, part1, col1, sum1_out, sum_sems[0]), (gx, gy))
    sumn = Sum(CHN, (srcn, partn, coln, sumn_out, sum_sems[1]), (gx, gy))
    sum0 = Sum(CH0, (src0, part0, col0, sum0_out, sum_sems[2]), (gx, gy))
    kept = ((a1_0, s1_0, a2_0, s2_0, n_0, r_0), (a1_1, s1_1, a2_1, s2_1, n_1, r_1))
    edge_in = (e0, e1, e2)

    def neighbour(dx, dy):
        return (gx + dx, gy + dy)

    def inside(dx, dy):
        there = None
        for step_, at, last in ((dx, gx, 31), (dy, gy, 3)):
            if step_:
                here = at > 0 if step_ < 0 else at < last
                there = here if there is None else there & here
        return there

    def when(there, act):
        pl.when(there)(act)

    tab[...] = jnp.zeros_like(tab)
    rim_in[...] = jnp.zeros_like(rim_in)
    barrier = pltpu.get_barrier_semaphore()

    def greet(device):
        pl.semaphore_signal(barrier, inc=1, device_id=device, device_id_type=MESH)

    for dx, dy in DIRS:
        when(inside(dx, dy), functools.partial(greet, neighbour(dx, dy)))
    x, z, y = sum1.x, sum1.z, sum1.y
    for dx, dy in PLANE:
        greet((((x + dx) % 4 * 2 + z) * 4 + (y + dy) % 4, gy))
    for dz, dg in COLUMN:
        greet(((x * 2 + (z + dz) % 2) * 4 + y, (gy + dg) % 4))

    def load(ref, scratch, which, t):
        s = rows_of(t * CELL, CELL)
        return pltpu.make_async_copy(ref.at[s], scratch.at[s], in_sem.at[which, t])

    own_cells = [tab.at[0, 1 + c // 2, 1 + c % 2] for c in range(4)]
    node_loads = [
        pltpu.make_async_copy(nodes_hbm.at[32 * c : 32 * c + 32], own_cells[c], in_sem.at[2, c])
        for c in range(4)
    ]
    weights = (
        ew1, eb1, ew2, eb2, ew3, eb3, egain, eshift, nw1, nb1, nw2, nb2, nw3, nb3, ngain, nshift,
    )
    small_loads = [
        pltpu.make_async_copy(src, dst, weight_sem.at[k])
        for k, (src, dst) in enumerate(
            zip((index_hbm, mask_hbm, ct_nodes_hbm, *weights_hbm), (index, mask, ct_nodes, *weights))
        )
    ]
    for copy in node_loads + small_loads:
        copy.start()
    for t in range(4):
        load(edges, e0, 0, t).start()
    nx = (gx > 0).astype(jnp.int32) + (gx < 31).astype(jnp.int32)
    ny = (gy > 0).astype(jnp.int32) + (gy < 3).astype(jnp.int32)
    pl.semaphore_wait(barrier, nx + ny + nx * ny + len(PLANE) + len(COLUMN))
    for copy in node_loads:
        copy.wait()

    def halo_copy(k):
        dx, dy = DIRS[k]
        src = tab.at[0, span(dx, 1, 2, pl.ds(1, 2)), span(dy, 1, 2, pl.ds(1, 2))]
        dst = tab.at[0, span(dx, 3, 0, pl.ds(1, 2)), span(dy, 3, 0, pl.ds(1, 2))]
        return pltpu.make_async_remote_copy(
            src_ref=src,
            dst_ref=dst,
            send_sem=halo_sem.at[0, k],
            recv_sem=halo_sem.at[1, k],
            device_id=neighbour(dx, dy),
            device_id_type=MESH,
        )

    def exchange_start(copy_of):
        for k, (dx, dy) in enumerate(DIRS):
            when(inside(dx, dy), lambda k=k: copy_of(k).start())

    def exchange_finish(copy_of):
        for k, (dx, dy) in enumerate(DIRS):
            when(inside(-dx, -dy), lambda k=k: copy_of(k).wait_recv())
            when(inside(dx, dy), lambda k=k: copy_of(k).wait_send())

    def cell_copies(c):
        i, j = c // 2, c % 2
        for k, (dx, dy) in enumerate(((2 * i - 1, 0), (0, 2 * j - 1), (2 * i - 1, 2 * j - 1))):
            a = 3 - 3 * i if dx else 1 + i
            b = 3 - 3 * j if dy else 1 + j
            copy = pltpu.make_async_remote_copy(
                src_ref=tab.at[1, 1 + i, 1 + j],
                dst_ref=tab.at[1, a, b],
                send_sem=cell_send.at[c, k],
                recv_sem=cell_recv.at[a, b],
                device_id=neighbour(dx, dy),
                device_id_type=MESH,
            )
            yield dx, dy, copy

    def cell_start(c):
        for dx, dy, copy in cell_copies(c):
            when(inside(dx, dy), copy.start)

    def cells_sent():
        for c in range(4):
            for dx, dy, copy in cell_copies(c):
                when(inside(dx, dy), copy.wait_send)

    def cells_arrive(group):
        views = {
            1: ((1, 0, ((3, 1), (3, 2))), (0, 1, ((1, 3), (2, 3))), (1, 1, ((3, 3),))),
            2: ((0, -1, ((1, 0), (2, 0))), (1, -1, ((3, 0),))),
            3: ((-1, 0, ((0, 1), (0, 2))), (-1, -1, ((0, 0),)), (-1, 1, ((0, 3),))),
        }[group]

        def wait(places):
            for a, b in places:
                drain(tab.at[1, a, b], cell_recv.at[a, b])

        for dx, dy, places in views:
            when(inside(dx, dy), functools.partial(wait, places))

    exchange_start(halo_copy)
    for t in range(4):
        load(ct_edges, ct, 1, t).start()
    for copy in small_loads:
        copy.wait()

    def latents(layer, cells=(0, 1, 2, 3)):
        return jnp.concatenate([tab[layer, 1 + c // 2, 1 + c % 2] for c in cells], 0)

    averager[...] = jnp.full((D, D), 1.0 / D, BF)
    for layer in range(2):
        w2half[layer] = (0.5 * ew2[layer].astype(F32)).astype(BF)
        w3 = ew3[layer].astype(F32)
        w3mid[layer] = (w3 - jnp.mean(w3, -1, keepdims=True)).astype(BF)
        w3t[layer] = ew3[layer].T
        w2t[layer] = ew2[layer].T
        w1et[layer] = ew1[layer, 2 * D : 3 * D, :].T
    sums[...] = jnp.zeros_like(sums)
    dw2[...] = jnp.zeros_like(dw2)
    dw3[...] = jnp.zeros_like(dw3)

    count = jnp.sum(mask[...].astype(F32), -1, keepdims=True)
    live_count[...] = jnp.broadcast_to(count, (PARTS, D))
    cell_of = iota((PARTS, 64), 0) // 32
    place = index[...] - (cell_of // 2) * 128 - (cell_of % 2) * 32
    place = (place // 128) * 96 + place % 128
    dead = mask[...] == 0
    high = jnp.where(dead, 127, place // 16)
    low = jnp.where(dead, 0, place % 16)
    digits = jnp.concatenate([high, low], 1).astype(F32).astype(BF)
    spread = jnp.where(iota((D, D), 0) < 64, 16.0, 1.0).astype(BF)
    row = iota((CELL, D), 0)
    lane = iota((CELL, D), 1)
    pick = jnp.where(lane == row // 64, 1.0, 0.0).astype(BF)
    slot_mask[...] = jnp.where(lane % 64 == row % 64, 1.0, 0.0)
    fixed[...] = jnp.where((lane == 32 + row // 64) | (lane == 64) | (lane == 65), 1.0, 0.0)
    for c in range(4):
        digits_of = jnp.concatenate([digits[32 * c : 32 * c + 32], jnp.zeros((96, D), BF)], 0)
        for g in range(4):
            at = slice(512 * g, 512 * g + 512)
            own = (dot(pick[at], digits_of) * slot_mask[at, :]).astype(BF)
            found = dot(own, spread)
            s = slice(c * CELL + 512 * g, c * CELL + 512 * g + 512)
            column = iota((512, D), 1).astype(F32)
            onehot[s, 0:128] = jnp.where(found == column, 1.0, 0.0).astype(BF)
            onehot[s, 128:256] = jnp.where(found == column + 128.0, 1.0, 0.0).astype(BF)
            onehot[s, 256:384] = jnp.where(found == column + 256.0, 1.0, fixed[at, :]).astype(BF)

    def prepare(layer, cells):
        a0, b0 = min(c // 2 for c in cells), min(c % 2 for c in cells)
        high_a, high_b = max(c // 2 for c in cells) + 3 - a0, max(c % 2 for c in cells) + 3 - b0
        region = tab[layer, a0 : a0 + high_a, b0 : b0 + high_b].reshape(high_a * high_b * 32, D)
        senders = (0.5 * dot(region, ew1[layer, D : 2 * D, :])).astype(BF).reshape(high_a, high_b, 32, D)
        receivers = (0.5 * dot(latents(layer, cells), ew1[layer, 0:D, :])).astype(BF)
        bias = 0.5 * eb1[layer : layer + 1, :]
        bias_high = bias.astype(BF).astype(F32)
        at = iota((64, D), 0)
        bias_rows = jnp.where(at == 0, bias_high, jnp.where(at == 1, bias - bias_high, 0.0)).astype(BF)
        edge_rows = (0.5 * ew1[layer, 2 * D : 3 * D, :].astype(F32)).astype(BF)
        for k, c in enumerate(cells):
            i, j = c // 2 - a0, c % 2 - b0
            for a in range(3):
                wbig[c, 96 * a : 96 * a + 96, :] = senders[i + a, j : j + 3].reshape(96, D)
            wbig[c, 288:320, :] = receivers[32 * k : 32 * k + 32]
            wbig[c, 320:384, :] = bias_rows
            wbig[c, 384:512, :] = edge_rows

    step = CELL // SUB
    per = step // 64

    def live_of(p):
        slot = iota((per, 64, D), 1).astype(F32)
        return slot < live_count[p, :][:, None, :]

    def forward(layer, c, parts=tuple(range(SUB))):
        a1, s1, a2, s2, nn, rr = kept[layer]
        e_in, e_out = edge_in[layer], edge_in[layer + 1]
        b2 = 0.5 * eb2[layer : layer + 1, :]
        b3 = eb3[layer : layer + 1, :]
        b3 = b3 - jnp.mean(b3, -1, keepdims=True)
        gain, shift = egain[layer : layer + 1, :], eshift[layer : layer + 1, :]
        groups = [rows_of(c * CELL + g * step, step) for g in parts]
        ones = [dot(jnp.concatenate([onehot[s, :], e_in[s, :]], 1), wbig[c]) for s in groups]
        first = []
        for s, half in zip(groups, ones):
            act, slope = silu_parts(half)
            a1[s, :] = act.astype(BF)
            s1[s, :] = slope.astype(BF)
            first.append(act.astype(BF))
        twos = [dot(act, w2half[layer]) + b2 for act in first]
        second = []
        for s, half in zip(groups, twos):
            act, slope = silu_parts(half)
            a2[s, :] = act.astype(BF)
            s2[s, :] = slope.astype(BF)
            second.append(act.astype(BF))
        mids = [dot(act, w3mid[layer]) + b3 for act in second]
        spreads = [dot((mid * mid).astype(BF), averager[...]) for mid in mids]
        for g, s, mid, var in zip(parts, groups, mids, spreads):
            inverse = lax.rsqrt(var + EPS)
            normed = mid * inverse
            nn[s, :] = normed.astype(BF)
            rr[s, :] = inverse
            update = (normed * gain + shift).reshape(per, 64, D)
            p = rows_of(c * 32 + g * per, per)
            live = live_of(p)
            new = e_in[s, :].astype(F32).reshape(per, 64, D) + jnp.where(live, update, 0.0)
            e_out[s, :] = new.astype(BF).reshape(step, D)
            msum[p, :] = jnp.sum(jnp.where(live, new, 0.0), 1)

    def node_forward(layer, cells):
        p = slice(32 * cells[0], 32 * cells[-1] + 32)
        h = latents(layer, cells)
        m = msum[p, :].astype(BF)
        z1 = dot(h, nw1[layer, 0:D, :]) + dot(m, nw1[layer, D : 2 * D, :]) + nb1[layer : layer + 1, :]
        c1, slope1 = silu_parts(0.5 * z1)
        c1 = c1.astype(BF)
        z2 = dot(c1, nw2[layer]) + nb2[layer : layer + 1, :]
        c2, slope2 = silu_parts(0.5 * z2)
        c2 = c2.astype(BF)
        z3 = dot(c2, nw3[layer]) + nb3[layer : layer + 1, :]
        mid = z3 - jnp.mean(z3, -1, keepdims=True)
        inverse = lax.rsqrt(jnp.mean(mid * mid, -1, keepdims=True) + EPS)
        normed = mid * inverse
        nm[layer, p], nc1[layer, p], nc2[layer, p] = m, c1, c2
        nsl1[layer, p], nsl2[layer, p], nnorm[layer, p] = slope1, slope2, normed
        ninv[layer, p] = jnp.broadcast_to(inverse, h.shape)
        update = normed * ngain[layer : layer + 1, :] + nshift[layer : layer + 1, :]
        result = (h.astype(F32) + update).astype(BF)
        if layer == 1:
            nodes_out[p, :] = result
        else:
            for k, c in enumerate(cells):
                tab[1, 1 + c // 2, 1 + c % 2] = result[32 * k : 32 * k + 32]

    def node_backward(layer, cells):
        p = slice(32 * cells[0], 32 * cells[-1] + 32)
        gh = gh_buf[p, :]
        normed = nnorm[layer, p]
        q = gh * ngain[layer : layer + 1, :]
        inner = q - jnp.mean(q, -1, keepdims=True) - normed * jnp.mean(q * normed, -1, keepdims=True)
        gz3 = ninv[layer, p] * inner
        gz2 = dot_nt(gz3.astype(BF), nw3[layer]) * nsl2[layer, p]
        gz1 = dot_nt(gz2.astype(BF), nw2[layer]) * nsl1[layer, p]
        gz[0, p], gz[1, p], gz[2, p] = gz1, gz2, gz3
        gm[p, :] = dot_nt(gz1.astype(BF), nw1[layer, D : 2 * D, :])

    def node_grads(layer, dst, row_, vec):
        low1, low2, low3 = (gz[k].astype(BF) for k in range(3))
        dst[row_ : row_ + 128, :] = dot_tn(latents(layer), low1).astype(BF)
        dst[row_ + 128 : row_ + 256, :] = dot_tn(nm[layer], low1).astype(BF)
        dst[row_ + 256 : row_ + 384, :] = dot_tn(nc1[layer], low2).astype(BF)
        dst[row_ + 384 : row_ + 512, :] = dot_tn(nc2[layer], low3).astype(BF)
        gh = gh_buf[...]
        vec.extend([column_sum(gz[k]) for k in range(3)])
        vec.extend([column_sum(gh * nnorm[layer]), column_sum(gh)])

    def backward(layer, c):
        a1, s1, a2, s2, nn, rr = kept[layer]
        e_in = edge_in[layer]
        gain = egain[layer : layer + 1, :]
        groups = [rows_of(c * CELL + g * step, step) for g in range(SUB)]
        firsts = []
        for g, s in enumerate(groups):
            p = rows_of(c * 32 + g * per, per)
            live = live_of(p)
            old = ct[s, :].astype(F32) if layer == 1 else ge[s, :]
            total = old.reshape(per, 64, D) + jnp.where(live, gm[p, :][:, None, :], 0.0)
            gy_ = jnp.where(live, total, 0.0).reshape(step, D)
            normed = nn[s, :].astype(F32)
            q = gy_ * gain
            qn = q * normed
            mean_q = dot(q.astype(BF), averager[...])
            mean_qn = dot(qn.astype(BF), averager[...])
            firsts.append((total.reshape(step, D), gy_, q, qn, normed, mean_q, mean_qn))
        g3 = [rr[s, :] * (f[2] - f[5] - f[4] * f[6]) for s, f in zip(groups, firsts)]
        low3 = [g.astype(BF) for g in g3]
        g2 = [dot(g, w3t[layer]) * s2[s, :].astype(F32) for s, g in zip(groups, low3)]
        low2 = [g.astype(BF) for g in g2]
        low1 = [(dot(g, w2t[layer]) * s1[s, :].astype(F32)).astype(BF) for s, g in zip(groups, low2)]
        for s, g, f in zip(groups, low1, firsts):
            ge[s, :] = f[0]
            s1[s, :] = g
        sums[layer, 0] += sum(partial_rows(f[3]) for f in firsts)
        sums[layer, 1] += sum(partial_rows(f[1]) for f in firsts)
        sums[layer, 2] += sum(partial_rows(g) for g in g3)
        sums[layer, 3] += sum(partial_rows(g) for g in g2)
        s = rows_of(c * CELL, CELL)
        left = jnp.concatenate([onehot[s, :], e_in[s, :]], 1)
        tt[layer, c] = dot_tn(jnp.concatenate(low1, 0), left)
        if layer == 1:
            for s, two, three in zip(groups, low2, low3):
                s2[s, :] = two
                nn[s, :] = three
        else:
            dw2[layer] += dot_tn(jnp.concatenate(low2, 0), a1[s, :])
            dw3[layer] += dot_tn(jnp.concatenate(low3, 0), a2[s, :])

    def backward_rest(layer, c):
        a1, s1, a2, s2, nn, rr = kept[layer]
        s = rows_of(c * CELL, CELL)
        ge[s, :] += dot(s1[s, :], w1et[layer])
        if layer == 1:
            dw2[layer] += dot_tn(s2[s, :], a1[s, :])
            dw3[layer] += dot_tn(nn[s, :], a2[s, :])

    def rim_copy(layer, k):
        dx, dy = DIRS[k]
        src = sender_low.at[layer, span(dx, 0, 3, pl.ds(1, 2)), span(dy, 0, 3, pl.ds(1, 2))]
        dst = rim_in.at[layer, k, 0] if dx != 0 and dy != 0 else rim_in.at[layer, k]
        return pltpu.make_async_remote_copy(
            src_ref=src,
            dst_ref=dst,
            send_sem=rim_sem.at[layer, 0, k],
            recv_sem=rim_sem.at[layer, 1, k],
            device_id=neighbour(dx, dy),
            device_id_type=MESH,
        )

    def rims_sum(layer):
        sender_sum[...] = jnp.zeros_like(sender_sum)
        for c in range(4):
            i, j = c // 2, c % 2
            by_row = tt[layer, c, :, 0:384].T
            for a in range(3):
                piece = by_row[96 * a : 96 * a + 96].reshape(3, 32, D)
                for b in range(3):
                    sender_sum[i + a, j + b] += piece[b]
            receiver_sum[32 * c : 32 * c + 32, :] = by_row[288:320]
            sums[layer, 4] += jnp.where(iota((8, D), 0) == 0, by_row[320:328], 0.0)
        sender_low[layer] = sender_sum[...].astype(BF)

    def edge_grads(layer, dst, row_, vec):
        dst[row_ : row_ + 128, :] = dot_tn(latents(layer), receiver_sum[...].astype(BF)).astype(BF)
        senders = dot_tn(tab[layer].reshape(512, D), sender_low[layer].reshape(512, D))
        dst[row_ + 128 : row_ + 256, :] = senders.astype(BF)
        by_edge = sum(tt[layer, c, :, 384:512] for c in range(4))
        dst[row_ + 256 : row_ + 384, :] = by_edge.T.astype(BF)
        dst[row_ + 384 : row_ + 512, :] = dw2[layer].T.astype(BF)
        dst[row_ + 512 : row_ + 640, :] = dw3[layer].T.astype(BF)
        s = [column_sum(sums[layer, k]) for k in range(5)]
        vec.extend([s[4], s[3], s[2], s[0] / egain[layer : layer + 1, :], s[1]])

    def node_share(layer):
        part = dot_nt(gz[0].astype(BF), nw1[layer, 0:D, :])
        gh_buf[...] += part + dot_nt(receiver_sum[...].astype(BF), ew1[layer, 0:D, :])

    def sender_share(layer):
        own = [sender_sum[1 + c // 2, 1 + c % 2] for c in range(4)]
        for k, (dx, dy) in enumerate(DIRS):
            cells = [
                (i, j)
                for i in ((0, 1) if dx == 0 else ((0,) if dx > 0 else (1,)))
                for j in ((0, 1) if dy == 0 else ((0,) if dy > 0 else (1,)))
            ]
            for at, (i, j) in enumerate(cells):
                own[2 * i + j] = own[2 * i + j] + rim_in[layer, k, at].astype(F32)
        own = jnp.concatenate(own, 0).astype(BF)
        return gh_buf[...] + dot_nt(own, ew1[layer, D : 2 * D, :])

    def put_vectors(dst, row_, vec):
        at = iota((16, D), 0)
        block = jnp.zeros((16, D), F32)
        for k, v in enumerate(vec):
            block = jnp.where(at == k, v, block)
        dst[row_ : row_ + 16, :] = block.astype(BF)

    exchange_finish(halo_copy)
    prepare(0, (0, 1, 2, 3))
    half = SUB // 2
    for c in range(4):
        load(edges, e0, 0, c).wait()
    forward(0, 0)
    forward(0, 1)
    node_forward(0, (0, 1))
    forward(0, 2, tuple(range(half)))
    cell_start(0)
    cell_start(1)
    forward(0, 2, tuple(range(half, SUB)))
    node_forward(0, (2,))
    forward(0, 3)
    cell_start(2)
    node_forward(0, (3,))
    cell_start(3)

    gh_buf[...] = ct_nodes[...].astype(F32)
    src1[VEC1 + 16 :, :] = jnp.zeros((CH1 * 16 - VEC1 - 16, D), BF)
    src0[VEC0 + 16 :, :] = jnp.zeros((CH0 * 16 - VEC0 - 16, D), BF)
    cells_arrive(1)
    prepare(1, (3,))
    forward(1, 3)
    cells_arrive(2)
    prepare(1, (2,))
    node_forward(1, (3,))
    node_backward(1, (3,))
    forward(1, 2)
    cells_arrive(3)
    prepare(1, (0, 1))
    cells_sent()
    node_forward(1, (2,))
    node_backward(1, (2,))
    forward(1, 1)
    node_forward(1, (1,))
    node_backward(1, (1,))
    forward(1, 0)

    for c in range(4):
        load(ct_edges, ct, 1, c).wait()
    node_forward(1, (0,))
    node_backward(1, (0,))
    for c in (3, 2, 1, 0):
        backward(1, c)
    rims_sum(1)
    exchange_start(functools.partial(rim_copy, 1))
    vec1, vec0 = [], []
    node_grads(1, src1, NODE_W1, vec1)
    for c in range(4):
        backward_rest(1, c)
    edge_grads(1, src1, EDGE_W1, vec1)
    put_vectors(src1, VEC1, vec1)
    node_share(1)
    sum1.scatter_start()
    exchange_finish(functools.partial(rim_copy, 1))
    gh_buf[...] = sender_share(1)

    node_backward(0, (0, 1, 2, 3))
    node_grads(0, srcn, 0, vec0)
    sumn.scatter_start()
    for c in range(4):
        backward(0, c)
    rims_sum(0)
    edge_grads(0, src0, EDGE_W1, vec0)
    put_vectors(src0, VEC0, vec0)
    sum0.scatter_start()
    exchange_start(functools.partial(rim_copy, 0))
    sum1.scatter_finish()
    sum1.column_start()
    sumn.scatter_finish()
    sumn.column_start()
    for c in range(4):
        backward_rest(0, c)
    node_share(0)
    sum0.scatter_finish()
    sum0.column_start()
    sum1.column_finish()
    sum1.gather_start()
    sumn.column_finish()
    sumn.gather_start()
    exchange_finish(functools.partial(rim_copy, 0))
    grad_nodes[...] = sender_share(0)
    sum0.column_finish()
    sum0.gather_start()
    sum1.gather_finish()
    sumn.gather_finish()
    sum0.gather_finish()


def unpack_kernel(nodes_in, edges_in, grad_nodes_in, grad_edges_in, sum1, sumn, sum0, *rest):
    (nodes_out, edges_out, grad_nodes, grad_edges), outs = rest[:4], rest[4:20]
    held, (sems, small) = rest[20:36], rest[36:]
    w1, b1, w2, b2, w3, b3, gain, shift, v1, c1, v2, c2, v3, c3, ngain, nshift = held
    copies = [
        pltpu.make_async_copy(nodes_in, nodes_out, sems.at[2, 0]),
        pltpu.make_async_copy(grad_nodes_in, grad_nodes, sems.at[2, 1]),
    ]
    for t in range(4):
        s = pl.ds(t * CELL, CELL)
        copies.append(pltpu.make_async_copy(grad_edges_in.at[s], grad_edges.at[s], sems.at[0, t]))
        copies.append(pltpu.make_async_copy(edges_in.at[s], edges_out.at[s], sems.at[1, t]))
    for copy in copies:
        copy.start()

    def put(ref, layer, buffer, row):
        height = ref.shape[1]
        ref[layer] = buffer[row : row + height, :].astype(F32)

    for layer, buffer in ((1, sum1), (0, sum0)):
        put(w1, layer, buffer, EDGE_W1)
        put(w2, layer, buffer, EDGE_W2)
        put(w3, layer, buffer, EDGE_W3)
    for layer, buffer, row in ((1, sum1, 0), (0, sumn, -NODE_W1)):
        put(v1, layer, buffer, row + NODE_W1)
        put(v2, layer, buffer, row + NODE_W2)
        put(v3, layer, buffer, row + NODE_W3)
    for layer, block in ((1, sum1[VEC1 : VEC1 + 16, :]), (0, sum0[VEC0 : VEC0 + 16, :])):
        rows = block.astype(F32)
        for k, ref in enumerate((c1, c2, c3, ngain, nshift, b1, b2, b3, gain, shift)):
            ref[layer : layer + 1, :] = rows[k : k + 1]
    for k, (src, dst) in enumerate(zip(held, outs)):
        copies.append(pltpu.make_async_copy(src, dst, small.at[k]))
        copies[-1].start()
    for copy in copies:
        copy.wait()


def per_device(nodes, edges, nbr_index, nbr_mask, *rest):
    weights, ct_nodes, ct_edges = rest[:16], rest[16], rest[17]
    vmem = pl.BlockSpec(memory_space=pltpu.VMEM)
    hbm = pl.BlockSpec(memory_space=pl.ANY)
    shape = jax.ShapeDtypeStruct
    big = pltpu.VMEM((ROWS, D), BF)
    node_bf = pltpu.VMEM((2, PARTS, D), BF)
    node_f32 = pltpu.VMEM((2, PARTS, D), F32)
    square = pltpu.VMEM((2, D, D), BF)
    dma = pltpu.SemaphoreType.DMA

    def sum_scratch(chunk):
        return [
            pltpu.VMEM((16 * chunk, D), BF),
            pltpu.VMEM((16, chunk, D), BF),
            pltpu.VMEM((8, chunk, D), BF),
        ]

    scratch = [
        pltpu.VMEM((PARTS, 64), jnp.int32),
        pltpu.VMEM((PARTS, 64), jnp.int32),
        *(pltpu.VMEM(w.shape, w.dtype) for w in weights),
        pltpu.VMEM((PARTS, D), BF),
        pltpu.VMEM((ROWS, 3 * D), BF),
        big, big, big,
        *(([big] * 5 + [pltpu.VMEM((ROWS, D), F32)]) * 2),
        pltpu.VMEM((PARTS, D), F32),
        pltpu.VMEM((2, 4, 4, 32, D), BF),
        pltpu.VMEM((4, 4 * D, D), BF),
        square, square, square, square, square,
        pltpu.VMEM((D, D), BF),
        pltpu.VMEM((PARTS, D), F32),
        pltpu.VMEM((PARTS, D), F32),
        pltpu.VMEM((2, 4, D, 4 * D), F32),
        pltpu.VMEM((2, D, D), F32),
        pltpu.VMEM((2, D, D), F32),
        pltpu.VMEM((2, 5, 8, D), F32),
        pltpu.VMEM((4, 4, 32, D), F32),
        pltpu.VMEM((2, 4, 4, 32, D), BF),
        pltpu.VMEM((PARTS, D), F32),
        pltpu.VMEM((2, 8, 2, 32, D), BF),
        node_bf, node_bf, node_bf, node_f32, node_f32, node_f32, node_f32,
        pltpu.VMEM((3, PARTS, D), F32),
        pltpu.VMEM((PARTS, D), F32),
        *sum_scratch(CH1),
        *sum_scratch(CHN),
        *sum_scratch(CH0),
        pltpu.VMEM((CELL, D), F32),
        pltpu.VMEM((CELL, D), F32),
        dma((3, 4)), dma((19,)), dma((2, 8)), dma((4, 3)), dma((4, 4)), dma((2, 2, 8)),
        *([dma((3, 2))] * 3),
    ]
    held = pl.pallas_call(
        main_kernel,
        out_shape=(
            pltpu.VMEM((PARTS, D), BF),
            pltpu.VMEM((ROWS, D), BF),
            pltpu.VMEM((PARTS, D), F32),
            pltpu.VMEM((ROWS, D), F32),
            pltpu.VMEM((16 * CH1, D), BF),
            pltpu.VMEM((16 * CHN, D), BF),
            pltpu.VMEM((16 * CH0, D), BF),
        ),
        in_specs=[hbm] * 22,
        out_specs=(vmem,) * 7,
        scratch_shapes=scratch,
        compiler_params=pltpu.CompilerParams(
            collective_id=0, has_side_effects=True, vmem_limit_bytes=53 * 1024 * 1024
        ),
        name="interaction_layers",
    )(
        nodes.reshape(PARTS, D),
        edges.reshape(ROWS, D),
        nbr_index.reshape(PARTS, 64),
        nbr_mask.reshape(PARTS, 64),
        *weights,
        ct_nodes.reshape(PARTS, D),
        ct_edges.reshape(ROWS, D),
    )
    held = [pltpu.with_memory_space_constraint(value, pltpu.VMEM) for value in held]
    nodes_out, edges_out, grad_nodes, grad_edges, *grads = pl.pallas_call(
        unpack_kernel,
        out_shape=(
            shape((PARTS, D), BF),
            shape((ROWS, D), BF),
            shape((PARTS, D), F32),
            shape((ROWS, D), F32),
            *(shape(w.shape, F32) for w in weights),
        ),
        in_specs=[vmem] * 7,
        out_specs=(hbm,) * 20,
        scratch_shapes=[*(pltpu.VMEM(w.shape, F32) for w in weights), dma((3, 4)), dma((16,))],
        compiler_params=pltpu.CompilerParams(vmem_limit_bytes=8 * 1024 * 1024),
        name="unpack_sums",
    )(*held)
    return (
        nodes_out.reshape(nodes.shape),
        edges_out.reshape(edges.shape),
        grad_nodes.reshape(nodes.shape),
        grad_edges.reshape(edges.shape),
        *grads,
    )


def solution(mesh):
    cells = P("gx", "gy", None, None)
    wide = P("gx", "gy", None, None, None)
    in_specs = (cells, wide, cells, cells) + (P(),) * 16 + (cells, wide)
    out_specs = (cells, wide, cells, wide) + (P(),) * 16
    return jax.shard_map(
        per_device, mesh=mesh, in_specs=in_specs, out_specs=out_specs, check_vma=False
    )
```

```python
import functools

import jax
import jax.numpy as jnp
from jax import lax
from jax.experimental import pallas as pl
from jax.experimental.pallas import tpu as pltpu
from jax.sharding import PartitionSpec as P

EPS = 1e-05
BF = jnp.bfloat16
F32 = jnp.float32
MESH = pl.DeviceIdType.MESH

D = 128
ROWS = 8192
CELL = 2048
SUB = 4
PARTS = 128

DIRS = ((1, 0), (-1, 0), (1, 1), (-1, -1), (1, -1), (-1, 1), (0, 1), (0, -1))
PLANE = (
    (2, 2), (1, 2), (2, 1), (3, 2), (2, 3), (2, 0), (0, 2), (1, 1), (3, 3), (1, 3), (3, 1), (1, 0), (0, 1), (3, 0), (0, 3),
)
COLUMN = ((1, 0), (1, 1), (1, 3), (1, 2), (0, 2), (0, 3), (0, 1))

CH1 = 80
CHN = 32
CH0 = 48
EDGE_W1, EDGE_W2, EDGE_W3 = 0, 384, 512
NODE_W1, NODE_W2, NODE_W3 = 640, 896, 1024
VEC1 = 1152
VEC0 = 640


def dot(a, b):
    return jnp.dot(a, b, preferred_element_type=F32)


def dot_nt(a, b):
    return lax.dot_general(a, b, (((1,), (1,)), ((), ())), preferred_element_type=F32)


def dot_tn(a, b):
    return lax.dot_general(a, b, (((0,), (0,)), ((), ())), preferred_element_type=F32)


def iota(shape, dim):
    return lax.broadcasted_iota(jnp.int32, shape, dim)


def silu_parts(half):
    wide = 1.0 + jnp.tanh(half)
    act = half * wide
    slope = wide * (0.5 + half - 0.5 * act)
    return act, slope


def rows_of(start, count):
    if isinstance(start, int):
        return slice(start, start + count)
    return pl.ds(pl.multiple_of(start, count), count)


def partial_rows(x):
    return jnp.sum(x.reshape(-1, 8, D), 0)


def column_sum(x):
    return jnp.sum(x, 0, keepdims=True)


def span(step, low, high, both):
    return low if step < 0 else (high if step > 0 else both)


def drain(view, sem):
    pltpu.make_async_copy(view, view, sem).wait()


class Sum:
    def __init__(self, chunk, refs, place):
        self.chunk = chunk
        self.src, self.part, self.col, self.out = refs[:4]
        self.sems = refs[4]
        self.gx, self.gy = place
        self.x, self.z, self.y = self.gx // 8, (self.gx // 4) % 2, self.gx % 4
        self.me = self.x * 4 + self.y
        self.mine = self.z * 4 + self.gy

    def rows(self, index):
        return pl.ds(pl.multiple_of(index * self.chunk, 16), self.chunk)

    def send(self, src, dst, phase, device):
        pltpu.make_async_remote_copy(
            src_ref=src,
            dst_ref=dst,
            send_sem=self.sems.at[phase, 0],
            recv_sem=self.sems.at[phase, 1],
            device_id=device,
            device_id_type=MESH,
        ).start()

    def wait(self, view, phase):
        drain(view, self.sems.at[phase, 0])
        drain(view, self.sems.at[phase, 1])

    def scatter_start(self):
        for dx, dy in PLANE:
            px, py = (self.x + dx) % 4, (self.y + dy) % 4
            src = self.src.at[self.rows(px * 4 + py)]
            self.send(src, self.part.at[self.me], 0, ((px * 2 + self.z) * 4 + py, self.gy))
        self.part[self.me] = self.src[self.rows(self.me), :]

    def scatter_finish(self):
        self.wait(self.part.at[pl.ds(0, 15)], 0)
        total = self.part[0].astype(F32)
        for k in range(1, 16):
            total = total + self.part[k].astype(F32)
        self.col[self.mine] = total.astype(BF)

    def column_start(self):
        own = self.col.at[self.mine]
        for dz, dg in COLUMN:
            pz, pg = (self.z + dz) % 2, (self.gy + dg) % 4
            self.send(own, own, 1, ((self.x * 2 + pz) * 4 + self.y, pg))

    def column_finish(self):
        self.wait(self.col.at[pl.ds(0, 7)], 1)
        total = self.col[0].astype(F32)
        for k in range(1, 8):
            total = total + self.col[k].astype(F32)
        self.out[self.rows(self.me), :] = total.astype(BF)

    def gather_start(self):
        own = self.out.at[self.rows(self.me)]
        for dx, dy in PLANE:
            px, py = (self.x + dx) % 4, (self.y + dy) % 4
            self.send(own, own, 2, ((px * 2 + self.z) * 4 + py, self.gy))

    def gather_finish(self):
        self.wait(self.out.at[pl.ds(0, 15 * self.chunk)], 2)


def main_kernel(*refs):
    (
        nodes_hbm, edges, index_hbm, mask_hbm, *weights_hbm,
    ) = refs[:20]
    ct_nodes_hbm, ct_edges = refs[20:22]
    (
        nodes_out, e2, grad_nodes, ge, sum1_out, sumn_out, sum0_out,
        index, mask,
        ew1, eb1, ew2, eb2, ew3, eb3, egain, eshift,
        nw1, nb1, nw2, nb2, nw3, nb3, ngain, nshift,
        ct_nodes,
        onehot, e0, e1, ct,
        a1_0, s1_0, a2_0, s2_0, n_0, r_0,
        a1_1, s1_1, a2_1, s2_1, n_1, r_1,
        live_count,
        tab, wbig, w2half, w3mid, w1et, w2t, w3t, averager,
        msum, gm, tt, dw, sums, window,
        sender_sum, sender_low, receiver_sum, rim_in,
        nm, nc1, nc2, nsl1, nsl2, nnorm, ninv, gz, gh_buf,
        src1, part1, col1, srcn, partn, coln, src0, part0, col0,
        in_sem, weight_sem, halo_sem, cell_send, cell_recv, rim_sem,
        *sum_sems,
    ) = refs[22:]
    gx, gy = lax.axis_index("gx"), lax.axis_index("gy")
    sum1 = Sum(CH1, (src1, part1, col1, sum1_out, sum_sems[0]), (gx, gy))
    sumn = Sum(CHN, (srcn, partn, coln, sumn_out, sum_sems[1]), (gx, gy))
    sum0 = Sum(CH0, (src0, part0, col0, sum0_out, sum_sems[2]), (gx, gy))
    kept = ((a1_0, s1_0, a2_0, s2_0, n_0, r_0), (a1_1, s1_1, a2_1, s2_1, n_1, r_1))
    edge_in = (e0, e1, e2)

    def neighbour(dx, dy):
        return (gx + dx, gy + dy)

    def inside(dx, dy):
        there = None
        for step_, at, last in ((dx, gx, 31), (dy, gy, 3)):
            if step_:
                here = at > 0 if step_ < 0 else at < last
                there = here if there is None else there & here
        return there

    def when(there, act):
        pl.when(there)(act)

    own_cells = [tab.at[0, 1 + c // 2, 1 + c % 2] for c in range(4)]
    node_loads = [
        pltpu.make_async_copy(nodes_hbm.at[32 * c : 32 * c + 32], own_cells[c], in_sem.at[2, c])
        for c in range(4)
    ]
    for copy in node_loads:
        copy.start()
    tab[1] = jnp.zeros_like(tab[1])
    for a in range(4):
        for b in range(4):
            if a in (0, 3) or b in (0, 3):
                tab[0, a, b] = jnp.zeros((32, D), BF)
    rim_in[...] = jnp.zeros_like(rim_in)
    barrier = pltpu.get_barrier_semaphore()

    def greet(device):
        pl.semaphore_signal(barrier, inc=1, device_id=device, device_id_type=MESH)

    for dx, dy in DIRS:
        when(inside(dx, dy), functools.partial(greet, neighbour(dx, dy)))
    x, z, y = sum1.x, sum1.z, sum1.y
    for dx, dy in PLANE:
        greet((((x + dx) % 4 * 2 + z) * 4 + (y + dy) % 4, gy))
    for dz, dg in COLUMN:
        greet(((x * 2 + (z + dz) % 2) * 4 + y, (gy + dg) % 4))

    def load(ref, scratch, which, t):
        s = rows_of(t * CELL, CELL)
        return pltpu.make_async_copy(ref.at[s], scratch.at[s], in_sem.at[which, t])

    weights = (
        ew1, eb1, ew2, eb2, ew3, eb3, egain, eshift, nw1, nb1, nw2, nb2, nw3, nb3, ngain, nshift,
    )
    small_loads = [
        pltpu.make_async_copy(src, dst, weight_sem.at[k])
        for k, (src, dst) in enumerate(
            zip((index_hbm, mask_hbm, ct_nodes_hbm, *weights_hbm), (index, mask, ct_nodes, *weights))
        )
    ]
    for copy in small_loads:
        copy.start()
    for t in range(4):
        load(edges, e0, 0, t).start()
    nx = (gx > 0).astype(jnp.int32) + (gx < 31).astype(jnp.int32)
    ny = (gy > 0).astype(jnp.int32) + (gy < 3).astype(jnp.int32)
    pl.semaphore_wait(barrier, nx + ny + nx * ny + len(PLANE) + len(COLUMN))
    for copy in node_loads:
        copy.wait()

    def halo_copy(k):
        dx, dy = DIRS[k]
        src = tab.at[0, span(dx, 1, 2, pl.ds(1, 2)), span(dy, 1, 2, pl.ds(1, 2))]
        dst = tab.at[0, span(dx, 3, 0, pl.ds(1, 2)), span(dy, 3, 0, pl.ds(1, 2))]
        return pltpu.make_async_remote_copy(
            src_ref=src,
            dst_ref=dst,
            send_sem=halo_sem.at[0, k],
            recv_sem=halo_sem.at[1, k],
            device_id=neighbour(dx, dy),
            device_id_type=MESH,
        )

    def exchange_start(copy_of):
        for k, (dx, dy) in enumerate(DIRS):
            when(inside(dx, dy), lambda k=k: copy_of(k).start())

    def exchange_finish(copy_of):
        for k, (dx, dy) in enumerate(DIRS):
            when(inside(-dx, -dy), lambda k=k: copy_of(k).wait_recv())
            when(inside(dx, dy), lambda k=k: copy_of(k).wait_send())

    def cell_copies(c):
        i, j = c // 2, c % 2
        for k, (dx, dy) in enumerate(((2 * i - 1, 0), (0, 2 * j - 1), (2 * i - 1, 2 * j - 1))):
            a = 3 - 3 * i if dx else 1 + i
            b = 3 - 3 * j if dy else 1 + j
            copy = pltpu.make_async_remote_copy(
                src_ref=tab.at[1, 1 + i, 1 + j],
                dst_ref=tab.at[1, a, b],
                send_sem=cell_send.at[c, k],
                recv_sem=cell_recv.at[a, b],
                device_id=neighbour(dx, dy),
                device_id_type=MESH,
            )
            yield dx, dy, copy

    def cell_start(c):
        for dx, dy, copy in cell_copies(c):
            when(inside(dx, dy), copy.start)

    def cells_sent():
        for c in range(4):
            for dx, dy, copy in cell_copies(c):
                when(inside(dx, dy), copy.wait_send)

    def cells_arrive(group):
        views = {
            1: ((1, 0, ((3, 1), (3, 2))), (0, 1, ((1, 3), (2, 3))), (1, 1, ((3, 3),))),
            2: ((0, -1, ((1, 0), (2, 0))), (1, -1, ((3, 0),))),
            3: ((-1, 0, ((0, 1), (0, 2))), (-1, -1, ((0, 0),)), (-1, 1, ((0, 3),))),
        }[group]

        def wait(places):
            for a, b in places:
                drain(tab.at[1, a, b], cell_recv.at[a, b])

        for dx, dy, places in views:
            when(inside(dx, dy), functools.partial(wait, places))

    exchange_start(halo_copy)
    for t in range(4):
        load(ct_edges, ct, 1, t).start()
    for copy in small_loads:
        copy.wait()

    def latents(layer, cells=(0, 1, 2, 3)):
        return jnp.concatenate([tab[layer, 1 + c // 2, 1 + c % 2] for c in cells], 0)

    averager[...] = jnp.full((D, D), 1.0 / D, BF)
    for layer in range(2):
        w2half[layer] = (0.5 * ew2[layer].astype(F32)).astype(BF)
        w3 = ew3[layer].astype(F32)
        w3mid[layer] = (w3 - jnp.mean(w3, -1, keepdims=True)).astype(BF)
        w3t[layer] = w3mid[layer].T
        w2t[layer] = ew2[layer].T
        w1et[layer] = ew1[layer, 2 * D : 3 * D, :].T
    sums[...] = jnp.zeros_like(sums)
    dw[...] = jnp.zeros_like(dw)
    window[...] = jnp.zeros_like(window)

    count = jnp.sum(mask[...].astype(F32), -1, keepdims=True)
    live_count[...] = jnp.broadcast_to(count, (PARTS, D))
    cell_of = iota((PARTS, 64), 0) // 32
    place = index[...] - (cell_of // 2) * 128 - (cell_of % 2) * 32
    place = (place // 128) * 96 + place % 128
    dead = mask[...] == 0
    high = jnp.where(dead, 127, place // 16)
    low = jnp.where(dead, 0, place % 16)
    digits = jnp.concatenate([high, low], 1).astype(F32).astype(BF)
    spread = jnp.where(iota((D, D), 0) < 64, 16.0, 1.0).astype(BF)
    row = iota((CELL, D), 0)
    lane = iota((CELL, D), 1)
    pick = jnp.where(lane == row // 64, 1.0, 0.0).astype(BF)
    slot_mask, fixed = ge.at[0:CELL], ge.at[CELL : 2 * CELL]
    slot_mask[...] = jnp.where(lane % 64 == row % 64, 1.0, 0.0)
    fixed[...] = jnp.where((lane == 32 + row // 64) | (lane == 64) | (lane == 65), 1.0, 0.0)
    for c in range(4):
        digits_of = jnp.concatenate([digits[32 * c : 32 * c + 32], jnp.zeros((96, D), BF)], 0)
        for g in range(4):
            at = slice(512 * g, 512 * g + 512)
            own = (dot(pick[at], digits_of) * slot_mask[at, :]).astype(BF)
            found = dot(own, spread)
            s = slice(c * CELL + 512 * g, c * CELL + 512 * g + 512)
            column = iota((512, D), 1).astype(F32)
            onehot[s, 0:128] = jnp.where(found == column, 1.0, 0.0).astype(BF)
            onehot[s, 128:256] = jnp.where(found == column + 128.0, 1.0, 0.0).astype(BF)
            onehot[s, 256:384] = jnp.where(found == column + 256.0, 1.0, fixed[at, :]).astype(BF)

    def prepare(layer, cells):
        a0, b0 = min(c // 2 for c in cells), min(c % 2 for c in cells)
        high_a, high_b = max(c // 2 for c in cells) + 3 - a0, max(c % 2 for c in cells) + 3 - b0
        region = tab[layer, a0 : a0 + high_a, b0 : b0 + high_b].reshape(high_a * high_b * 32, D)
        senders = (0.5 * dot(region, ew1[layer, D : 2 * D, :])).astype(BF).reshape(high_a, high_b, 32, D)
        receivers = (0.5 * dot(latents(layer, cells), ew1[layer, 0:D, :])).astype(BF)
        bias = 0.5 * eb1[layer : layer + 1, :]
        bias_high = bias.astype(BF).astype(F32)
        at = iota((64, D), 0)
        bias_rows = jnp.where(at == 0, bias_high, jnp.where(at == 1, bias - bias_high, 0.0)).astype(BF)
        edge_rows = (0.5 * ew1[layer, 2 * D : 3 * D, :].astype(F32)).astype(BF)
        for k, c in enumerate(cells):
            i, j = c // 2 - a0, c % 2 - b0
            for a in range(3):
                wbig[c, 96 * a : 96 * a + 96, :] = senders[i + a, j : j + 3].reshape(96, D)
                window[layer, c, 96 * a : 96 * a + 96, 0:128] = tab[layer, c // 2 + a, c % 2 : c % 2 + 3].reshape(96, D)
            window[layer, c, 288:320, 128:256] = tab[layer, 1 + c // 2, 1 + c % 2]
            wbig[c, 288:320, :] = receivers[32 * k : 32 * k + 32]
            wbig[c, 320:384, :] = bias_rows
            wbig[c, 384:512, :] = edge_rows

    step = CELL // SUB
    per = step // 64

    def live_of(p):
        slot = iota((per, 64, D), 1).astype(F32)
        return slot < live_count[p, :][:, None, :]

    def forward(layer, c, parts=tuple(range(SUB))):
        a1, s1, a2, s2, nn, rr = kept[layer]
        e_in, e_out = edge_in[layer], edge_in[layer + 1]
        b2 = 0.5 * eb2[layer : layer + 1, :]
        b3 = eb3[layer : layer + 1, :]
        b3 = b3 - jnp.mean(b3, -1, keepdims=True)
        gain, shift = egain[layer : layer + 1, :], eshift[layer : layer + 1, :]
        groups = [rows_of(c * CELL + g * step, step) for g in parts]
        ones = [dot(jnp.concatenate([onehot[s, :], e_in[s, :]], 1), wbig[c]) for s in groups]
        first = []
        for s, half in zip(groups, ones):
            act, slope = silu_parts(half)
            a1[s, :] = act.astype(BF)
            s1[s, :] = slope.astype(BF)
            first.append(act.astype(BF))
        twos = [dot(act, w2half[layer]) + b2 for act in first]
        second = []
        for s, half in zip(groups, twos):
            act, slope = silu_parts(half)
            a2[s, :] = act.astype(BF)
            s2[s, :] = slope.astype(BF)
            second.append(act.astype(BF))
        mids = [dot(act, w3mid[layer]) + b3 for act in second]
        spreads = [dot((mid * mid).astype(BF), averager[...]) for mid in mids]
        for g, s, mid, var in zip(parts, groups, mids, spreads):
            inverse = lax.rsqrt(var + EPS)
            normed = mid * inverse
            nn[s, :] = normed.astype(BF)
            rr[s, :] = inverse
            update = (normed * gain + shift).reshape(per, 64, D)
            p = rows_of(c * 32 + g * per, per)
            live = live_of(p)
            new = e_in[s, :].astype(F32).reshape(per, 64, D) + jnp.where(live, update, 0.0)
            e_out[s, :] = new.astype(BF).reshape(step, D)
            msum[p, :] = jnp.sum(jnp.where(live, new, 0.0), 1)

    def node_forward(layer, cells):
        p = slice(32 * cells[0], 32 * cells[-1] + 32)
        h = latents(layer, cells)
        m = msum[p, :].astype(BF)
        z1 = dot(h, nw1[layer, 0:D, :]) + dot(m, nw1[layer, D : 2 * D, :]) + nb1[layer : layer + 1, :]
        c1, slope1 = silu_parts(0.5 * z1)
        c1 = c1.astype(BF)
        z2 = dot(c1, nw2[layer]) + nb2[layer : layer + 1, :]
        c2, slope2 = silu_parts(0.5 * z2)
        c2 = c2.astype(BF)
        z3 = dot(c2, nw3[layer]) + nb3[layer : layer + 1, :]
        mid = z3 - jnp.mean(z3, -1, keepdims=True)
        inverse = lax.rsqrt(jnp.mean(mid * mid, -1, keepdims=True) + EPS)
        normed = mid * inverse
        nm[layer, p], nc1[layer, p], nc2[layer, p] = m, c1, c2
        nsl1[layer, p], nsl2[layer, p], nnorm[layer, p] = slope1, slope2, normed
        ninv[layer, p] = jnp.broadcast_to(inverse, h.shape)
        update = normed * ngain[layer : layer + 1, :] + nshift[layer : layer + 1, :]
        result = (h.astype(F32) + update).astype(BF)
        if layer == 1:
            nodes_out[p, :] = result
        else:
            for k, c in enumerate(cells):
                tab[1, 1 + c // 2, 1 + c % 2] = result[32 * k : 32 * k + 32]

    def node_backward(layer, cells):
        p = slice(32 * cells[0], 32 * cells[-1] + 32)
        gh = gh_buf[p, :]
        normed = nnorm[layer, p]
        q = gh * ngain[layer : layer + 1, :]
        inner = q - jnp.mean(q, -1, keepdims=True) - normed * jnp.mean(q * normed, -1, keepdims=True)
        gz3 = ninv[layer, p] * inner
        gz2 = dot_nt(gz3.astype(BF), nw3[layer]) * nsl2[layer, p]
        gz1 = dot_nt(gz2.astype(BF), nw2[layer]) * nsl1[layer, p]
        gz[0, p], gz[1, p], gz[2, p] = gz1, gz2, gz3
        gm[p, :] = dot_nt(gz1.astype(BF), nw1[layer, D : 2 * D, :])

    def node_grads(layer, dst, row_, vec):
        low1, low2, low3 = (gz[k].astype(BF) for k in range(3))
        dst[row_ : row_ + 128, :] = dot_tn(latents(layer), low1).astype(BF)
        dst[row_ + 128 : row_ + 256, :] = dot_tn(nm[layer], low1).astype(BF)
        dst[row_ + 256 : row_ + 384, :] = dot_tn(nc1[layer], low2).astype(BF)
        dst[row_ + 384 : row_ + 512, :] = dot_tn(nc2[layer], low3).astype(BF)
        gh = gh_buf[...]
        vec.extend([column_sum(gz[k]) for k in range(3)])
        vec.extend([column_sum(gh * nnorm[layer]), column_sum(gh)])

    def backward(layer, c):
        a1, s1, a2, s2, nn, rr = kept[layer]
        e_in = edge_in[layer]
        gain = egain[layer : layer + 1, :]
        groups = [rows_of(c * CELL + g * step, step) for g in range(SUB)]
        firsts = []
        for g, s in enumerate(groups):
            p = rows_of(c * 32 + g * per, per)
            live = live_of(p)
            old = ct[s, :].astype(F32) if layer == 1 else ge[s, :]
            total = old.reshape(per, 64, D) + jnp.where(live, gm[p, :][:, None, :], 0.0)
            gy_ = jnp.where(live, total, 0.0).reshape(step, D)
            normed = nn[s, :].astype(F32)
            q = gy_ * gain
            qn = q * normed
            mean_qn = dot(qn.astype(BF), averager[...])
            firsts.append((total.reshape(step, D), gy_, q, qn, normed, mean_qn))
        g3 = [rr[s, :] * (f[2] - f[4] * f[5]) for s, f in zip(groups, firsts)]
        low3 = [g.astype(BF) for g in g3]
        g2 = [dot(g, w3t[layer]) * s2[s, :].astype(F32) for s, g in zip(groups, low3)]
        low2 = [g.astype(BF) for g in g2]
        low1 = [(dot(g, w2t[layer]) * s1[s, :].astype(F32)).astype(BF) for s, g in zip(groups, low2)]
        for s, g, f in zip(groups, low1, firsts):
            ge[s, :] = f[0]
            s1[s, :] = g
        sums[layer, 0] += sum(partial_rows(f[3]) for f in firsts)
        sums[layer, 1] += sum(partial_rows(f[1]) for f in firsts)
        sums[layer, 2] += sum(partial_rows(g) for g in g3)
        sums[layer, 3] += sum(partial_rows(g) for g in g2)
        s = rows_of(c * CELL, CELL)
        left = jnp.concatenate([onehot[s, :], e_in[s, :]], 1)
        tt[layer, c] = dot_tn(jnp.concatenate(low1, 0), left)
        if layer == 1:
            for s, two, three in zip(groups, low2, low3):
                s2[s, :] = two
                nn[s, :] = three
        else:
            dw[layer, 0:128] += dot_tn(jnp.concatenate(low2, 0), a1[s, :])
            dw[layer, 128:256] += dot_tn(jnp.concatenate(low3, 0), a2[s, :])

    def backward_rest(layer, c):
        a1, s1, a2, s2, nn, rr = kept[layer]
        s = rows_of(c * CELL, CELL)
        ge[s, :] += dot(s1[s, :], w1et[layer])
        if layer == 1:
            dw[layer, 0:128] += dot_tn(s2[s, :], a1[s, :])
            dw[layer, 128:256] += dot_tn(nn[s, :], a2[s, :])

    def rim_copy(layer, k):
        dx, dy = DIRS[k]
        src = sender_low.at[layer, span(dx, 0, 3, pl.ds(1, 2)), span(dy, 0, 3, pl.ds(1, 2))]
        dst = rim_in.at[layer, k, 0] if dx != 0 and dy != 0 else rim_in.at[layer, k]
        return pltpu.make_async_remote_copy(
            src_ref=src,
            dst_ref=dst,
            send_sem=rim_sem.at[layer, 0, k],
            recv_sem=rim_sem.at[layer, 1, k],
            device_id=neighbour(dx, dy),
            device_id_type=MESH,
        )

    def rims_sum(layer):
        sender_sum[...] = jnp.zeros_like(sender_sum)
        for c in range(4):
            i, j = c // 2, c % 2
            by_row = tt[layer, c, :, 0:384].T
            for a in range(3):
                piece = by_row[96 * a : 96 * a + 96].reshape(3, 32, D)
                for b in range(3):
                    sender_sum[i + a, j + b] += piece[b]
            receiver_sum[32 * c : 32 * c + 32, :] = by_row[288:320]
        sender_low[layer] = sender_sum[...].astype(BF)

    def edge_grads(layer, dst, row_, vec):
        by_node = sum(dot(tt[layer, c, :, 0:384].astype(BF), window[layer, c]) for c in range(4))
        by_edge = sum(tt[layer, c, :, 384:512] for c in range(4))
        ones = sum(tt[layer, c, :, 256:384] for c in range(4)).T[64:65]
        dst[row_ : row_ + 128, :] = by_node[:, 128:256].T.astype(BF)
        dst[row_ + 128 : row_ + 256, :] = by_node[:, 0:128].T.astype(BF)
        dst[row_ + 256 : row_ + 384, :] = by_edge.T.astype(BF)
        dst[row_ + 384 : row_ + 512, :] = dw[layer, 0:128].T.astype(BF)
        third = dw[layer, 128:256].T
        dst[row_ + 512 : row_ + 640, :] = (third - jnp.mean(third, -1, keepdims=True)).astype(BF)
        s = [column_sum(sums[layer, k]) for k in range(4)]
        s[2] = s[2] - jnp.mean(s[2], -1, keepdims=True)
        vec.extend([ones, s[3], s[2], s[0] / egain[layer : layer + 1, :], s[1]])

    def node_share(layer):
        part = dot_nt(gz[0].astype(BF), nw1[layer, 0:D, :])
        gh_buf[...] += part + dot_nt(receiver_sum[...].astype(BF), ew1[layer, 0:D, :])

    def sender_share(layer):
        own = [sender_sum[1 + c // 2, 1 + c % 2] for c in range(4)]
        for k, (dx, dy) in enumerate(DIRS):
            cells = [
                (i, j)
                for i in ((0, 1) if dx == 0 else ((0,) if dx > 0 else (1,)))
                for j in ((0, 1) if dy == 0 else ((0,) if dy > 0 else (1,)))
            ]
            for at, (i, j) in enumerate(cells):
                own[2 * i + j] = own[2 * i + j] + rim_in[layer, k, at].astype(F32)
        own = jnp.concatenate(own, 0).astype(BF)
        return gh_buf[...] + dot_nt(own, ew1[layer, D : 2 * D, :])

    def put_vectors(dst, row_, vec):
        at = iota((16, D), 0)
        block = jnp.zeros((16, D), F32)
        for k, v in enumerate(vec):
            block = jnp.where(at == k, v, block)
        dst[row_ : row_ + 16, :] = block.astype(BF)

    exchange_finish(halo_copy)
    prepare(0, (0, 1, 2, 3))
    half = SUB // 2
    for c in range(4):
        load(edges, e0, 0, c).wait()
    forward(0, 0)
    forward(0, 1)
    node_forward(0, (0, 1))
    forward(0, 2, tuple(range(half)))
    cell_start(0)
    cell_start(1)
    forward(0, 2, tuple(range(half, SUB)))
    node_forward(0, (2,))
    forward(0, 3)
    cell_start(2)
    node_forward(0, (3,))
    cell_start(3)

    gh_buf[...] = ct_nodes[...].astype(F32)
    src1[VEC1 + 16 :, :] = jnp.zeros((CH1 * 16 - VEC1 - 16, D), BF)
    src0[VEC0 + 16 :, :] = jnp.zeros((CH0 * 16 - VEC0 - 16, D), BF)
    cells_arrive(1)
    prepare(1, (3,))
    forward(1, 3)
    cells_arrive(2)
    prepare(1, (2,))
    node_forward(1, (3,))
    node_backward(1, (3,))
    forward(1, 2)
    cells_arrive(3)
    prepare(1, (0, 1))
    cells_sent()
    node_forward(1, (2,))
    node_backward(1, (2,))
    forward(1, 1)
    node_forward(1, (1,))
    node_backward(1, (1,))
    forward(1, 0)

    for c in range(4):
        load(ct_edges, ct, 1, c).wait()
    node_forward(1, (0,))
    node_backward(1, (0,))
    for c in (3, 2, 1, 0):
        backward(1, c)
    rims_sum(1)
    exchange_start(functools.partial(rim_copy, 1))
    vec1, vec0 = [], []
    node_grads(1, src1, NODE_W1, vec1)
    for c in range(4):
        backward_rest(1, c)
    edge_grads(1, src1, EDGE_W1, vec1)
    put_vectors(src1, VEC1, vec1)
    node_share(1)
    sum1.scatter_start()
    exchange_finish(functools.partial(rim_copy, 1))
    gh_buf[...] = sender_share(1)

    node_backward(0, (0, 1, 2, 3))
    node_grads(0, srcn, 0, vec0)
    sumn.scatter_start()
    for c in range(4):
        backward(0, c)
    edge_grads(0, src0, EDGE_W1, vec0)
    put_vectors(src0, VEC0, vec0)
    sum0.scatter_start()
    rims_sum(0)
    exchange_start(functools.partial(rim_copy, 0))
    sum1.scatter_finish()
    sum1.column_start()
    sumn.scatter_finish()
    sumn.column_start()
    for c in range(4):
        backward_rest(0, c)
    node_share(0)
    sum0.scatter_finish()
    sum0.column_start()
    sum1.column_finish()
    sum1.gather_start()
    sumn.column_finish()
    sumn.gather_start()
    exchange_finish(functools.partial(rim_copy, 0))
    grad_nodes[...] = sender_share(0)
    sum0.column_finish()
    sum0.gather_start()
    sum1.gather_finish()
    sumn.gather_finish()
    sum0.gather_finish()


def unpack_kernel(nodes_in, edges_in, grad_nodes_in, grad_edges_in, sum1, sumn, sum0, *rest):
    (nodes_out, edges_out, grad_nodes, grad_edges), outs = rest[:4], rest[4:20]
    held, (sems, small) = rest[20:36], rest[36:]
    w1, b1, w2, b2, w3, b3, gain, shift, v1, c1, v2, c2, v3, c3, ngain, nshift = held
    copies = [
        pltpu.make_async_copy(nodes_in, nodes_out, sems.at[2, 0]),
        pltpu.make_async_copy(grad_nodes_in, grad_nodes, sems.at[2, 1]),
    ]
    for t in range(4):
        s = pl.ds(t * CELL, CELL)
        copies.append(pltpu.make_async_copy(grad_edges_in.at[s], grad_edges.at[s], sems.at[0, t]))
        copies.append(pltpu.make_async_copy(edges_in.at[s], edges_out.at[s], sems.at[1, t]))
    for copy in copies:
        copy.start()

    def put(ref, layer, buffer, row):
        height = ref.shape[1]
        ref[layer] = buffer[row : row + height, :].astype(F32)

    for layer, buffer in ((1, sum1), (0, sum0)):
        put(w1, layer, buffer, EDGE_W1)
        put(w2, layer, buffer, EDGE_W2)
        put(w3, layer, buffer, EDGE_W3)
    for layer, buffer, row in ((1, sum1, 0), (0, sumn, -NODE_W1)):
        put(v1, layer, buffer, row + NODE_W1)
        put(v2, layer, buffer, row + NODE_W2)
        put(v3, layer, buffer, row + NODE_W3)
    for layer, block in ((1, sum1[VEC1 : VEC1 + 16, :]), (0, sum0[VEC0 : VEC0 + 16, :])):
        rows = block.astype(F32)
        for k, ref in enumerate((c1, c2, c3, ngain, nshift, b1, b2, b3, gain, shift)):
            ref[layer : layer + 1, :] = rows[k : k + 1]
    for k, (src, dst) in enumerate(zip(held, outs)):
        copies.append(pltpu.make_async_copy(src, dst, small.at[k]))
        copies[-1].start()
    for copy in copies:
        copy.wait()


def per_device(nodes, edges, nbr_index, nbr_mask, *rest):
    weights, ct_nodes, ct_edges = rest[:16], rest[16], rest[17]
    vmem = pl.BlockSpec(memory_space=pltpu.VMEM)
    hbm = pl.BlockSpec(memory_space=pl.ANY)
    shape = jax.ShapeDtypeStruct
    big = pltpu.VMEM((ROWS, D), BF)
    node_bf = pltpu.VMEM((2, PARTS, D), BF)
    node_f32 = pltpu.VMEM((2, PARTS, D), F32)
    square = pltpu.VMEM((2, D, D), BF)
    dma = pltpu.SemaphoreType.DMA

    def sum_scratch(chunk):
        return [
            pltpu.VMEM((16 * chunk, D), BF),
            pltpu.VMEM((16, chunk, D), BF),
            pltpu.VMEM((8, chunk, D), BF),
        ]

    scratch = [
        pltpu.VMEM((PARTS, 64), jnp.int32),
        pltpu.VMEM((PARTS, 64), jnp.int32),
        *(pltpu.VMEM(w.shape, w.dtype) for w in weights),
        pltpu.VMEM((PARTS, D), BF),
        pltpu.VMEM((ROWS, 3 * D), BF),
        big, big, big,
        *(([big] * 5 + [pltpu.VMEM((ROWS, D), F32)]) * 2),
        pltpu.VMEM((PARTS, D), F32),
        pltpu.VMEM((2, 4, 4, 32, D), BF),
        pltpu.VMEM((4, 4 * D, D), BF),
        square, square, square, square, square,
        pltpu.VMEM((D, D), BF),
        pltpu.VMEM((PARTS, D), F32),
        pltpu.VMEM((PARTS, D), F32),
        pltpu.VMEM((2, 4, D, 4 * D), F32),
        pltpu.VMEM((2, 2 * D, D), F32),
        pltpu.VMEM((2, 4, 8, D), F32),
        pltpu.VMEM((2, 4, 3 * D, 2 * D), BF),
        pltpu.VMEM((4, 4, 32, D), F32),
        pltpu.VMEM((2, 4, 4, 32, D), BF),
        pltpu.VMEM((PARTS, D), F32),
        pltpu.VMEM((2, 8, 2, 32, D), BF),
        node_bf, node_bf, node_bf, node_f32, node_f32, node_f32, node_f32,
        pltpu.VMEM((3, PARTS, D), F32),
        pltpu.VMEM((PARTS, D), F32),
        *sum_scratch(CH1),
        *sum_scratch(CHN),
        *sum_scratch(CH0),
        dma((3, 4)), dma((19,)), dma((2, 8)), dma((4, 3)), dma((4, 4)), dma((2, 2, 8)),
        *([dma((3, 2))] * 3),
    ]
    held = pl.pallas_call(
        main_kernel,
        out_shape=(
            pltpu.VMEM((PARTS, D), BF),
            pltpu.VMEM((ROWS, D), BF),
            pltpu.VMEM((PARTS, D), F32),
            pltpu.VMEM((ROWS, D), F32),
            pltpu.VMEM((16 * CH1, D), BF),
            pltpu.VMEM((16 * CHN, D), BF),
            pltpu.VMEM((16 * CH0, D), BF),
        ),
        in_specs=[hbm] * 22,
        out_specs=(vmem,) * 7,
        scratch_shapes=scratch,
        compiler_params=pltpu.CompilerParams(
            collective_id=0, has_side_effects=True, vmem_limit_bytes=53 * 1024 * 1024
        ),
        name="interaction_layers",
    )(
        nodes.reshape(PARTS, D),
        edges.reshape(ROWS, D),
        nbr_index.reshape(PARTS, 64),
        nbr_mask.reshape(PARTS, 64),
        *weights,
        ct_nodes.reshape(PARTS, D),
        ct_edges.reshape(ROWS, D),
    )
    held = [pltpu.with_memory_space_constraint(value, pltpu.VMEM) for value in held]
    nodes_out, edges_out, grad_nodes, grad_edges, *grads = pl.pallas_call(
        unpack_kernel,
        out_shape=(
            shape((PARTS, D), BF),
            shape((ROWS, D), BF),
            shape((PARTS, D), F32),
            shape((ROWS, D), F32),
            *(shape(w.shape, F32) for w in weights),
        ),
        in_specs=[vmem] * 7,
        out_specs=(hbm,) * 20,
        scratch_shapes=[*(pltpu.VMEM(w.shape, F32) for w in weights), dma((3, 4)), dma((16,))],
        compiler_params=pltpu.CompilerParams(vmem_limit_bytes=8 * 1024 * 1024),
        name="unpack_sums",
    )(*held)
    return (
        nodes_out.reshape(nodes.shape),
        edges_out.reshape(edges.shape),
        grad_nodes.reshape(nodes.shape),
        grad_edges.reshape(edges.shape),
        *grads,
    )


def solution(mesh):
    cells = P("gx", "gy", None, None)
    wide = P("gx", "gy", None, None, None)
    in_specs = (cells, wide, cells, cells) + (P(),) * 16 + (cells, wide)
    out_specs = (cells, wide, cells, wide) + (P(),) * 16
    return jax.shard_map(
        per_device, mesh=mesh, in_specs=in_specs, out_specs=out_specs, check_vma=False
    )
```

```python
import functools

import jax
import jax.numpy as jnp
from jax import lax
from jax.experimental import pallas as pl
from jax.experimental.pallas import tpu as pltpu
from jax.sharding import PartitionSpec as P

EPS = 1e-05
BF = jnp.bfloat16
F32 = jnp.float32
MESH = pl.DeviceIdType.MESH

D = 128
ROWS = 8192
CELL = 2048
SUB = 4
PARTS = 128

DIRS = ((1, 0), (1, 1), (1, -1), (0, 1), (0, -1), (-1, 0), (-1, 1), (-1, -1))
EARLY, LATE = range(5), range(5, 8)
PLANE = (
    (2, 2), (1, 2), (2, 1), (3, 2), (2, 3), (2, 0), (0, 2), (1, 1), (3, 3), (1, 3), (3, 1), (1, 0), (0, 1), (3, 0), (0, 3),
)
COLUMN = ((1, 0), (1, 1), (1, 3), (1, 2), (0, 2), (0, 3), (0, 1))

CH1 = 80
CHN = 32
CH0 = 48
EDGE_W1, EDGE_W2, EDGE_W3 = 0, 384, 512
NODE_W1, NODE_W2, NODE_W3 = 640, 896, 1024
VEC1 = 1152
VEC0 = 640


def dot(a, b):
    return jnp.dot(a, b, preferred_element_type=F32)


def dot_nt(a, b):
    return lax.dot_general(a, b, (((1,), (1,)), ((), ())), preferred_element_type=F32)


def dot_tn(a, b):
    return lax.dot_general(a, b, (((0,), (0,)), ((), ())), preferred_element_type=F32)


def iota(shape, dim):
    return lax.broadcasted_iota(jnp.int32, shape, dim)


def silu_parts(half):
    wide = 1.0 + jnp.tanh(half)
    act = half * wide
    slope = wide * (0.5 + half - 0.5 * act)
    return act, slope


def rows_of(start, count):
    if isinstance(start, int):
        return slice(start, start + count)
    return pl.ds(pl.multiple_of(start, count), count)


def partial_rows(x):
    return jnp.sum(x.reshape(-1, 8, D), 0)


def column_sum(x):
    return jnp.sum(x, 0, keepdims=True)


def span(step, low, high, both):
    return low if step < 0 else (high if step > 0 else both)


def drain(view, sem):
    pltpu.make_async_copy(view, view, sem).wait()


class Sum:
    def __init__(self, chunk, refs, place):
        self.chunk = chunk
        self.src, self.part, self.col, self.out = refs[:4]
        self.sems = refs[4]
        self.gx, self.gy = place
        self.x, self.z, self.y = self.gx // 8, (self.gx // 4) % 2, self.gx % 4
        self.me = self.x * 4 + self.y
        self.mine = self.z * 4 + self.gy

    def rows(self, index):
        return pl.ds(pl.multiple_of(index * self.chunk, 16), self.chunk)

    def send(self, src, dst, phase, device):
        pltpu.make_async_remote_copy(
            src_ref=src,
            dst_ref=dst,
            send_sem=self.sems.at[phase, 0],
            recv_sem=self.sems.at[phase, 1],
            device_id=device,
            device_id_type=MESH,
        ).start()

    def wait(self, view, phase):
        drain(view, self.sems.at[phase, 0])
        drain(view, self.sems.at[phase, 1])

    def scatter_start(self):
        for dx, dy in PLANE:
            px, py = (self.x + dx) % 4, (self.y + dy) % 4
            src = self.src.at[self.rows(px * 4 + py)]
            self.send(src, self.part.at[self.me], 0, ((px * 2 + self.z) * 4 + py, self.gy))
        self.part[self.me] = self.src[self.rows(self.me), :]

    def scatter_finish(self):
        self.wait(self.part.at[pl.ds(0, 15)], 0)
        total = self.part[0].astype(F32)
        for k in range(1, 16):
            total = total + self.part[k].astype(F32)
        self.col[self.mine] = total.astype(BF)

    def column_start(self):
        own = self.col.at[self.mine]
        for dz, dg in COLUMN:
            pz, pg = (self.z + dz) % 2, (self.gy + dg) % 4
            self.send(own, own, 1, ((self.x * 2 + pz) * 4 + self.y, pg))

    def column_finish(self):
        self.wait(self.col.at[pl.ds(0, 7)], 1)
        total = self.col[0].astype(F32)
        for k in range(1, 8):
            total = total + self.col[k].astype(F32)
        self.out[self.rows(self.me), :] = total.astype(BF)

    def gather_start(self):
        own = self.out.at[self.rows(self.me)]
        for dx, dy in PLANE:
            px, py = (self.x + dx) % 4, (self.y + dy) % 4
            self.send(own, own, 2, ((px * 2 + self.z) * 4 + py, self.gy))

    def gather_finish(self):
        self.wait(self.out.at[pl.ds(0, 15 * self.chunk)], 2)


def main_kernel(*refs):
    (
        nodes_hbm, edges, index_hbm, mask_hbm, *weights_hbm,
    ) = refs[:20]
    ct_nodes_hbm, ct_edges = refs[20:22]
    (
        nodes_out, e2, grad_nodes, ge, sum1_out, sumn_out, sum0_out,
        index, mask,
        ew1, eb1, ew2, eb2, ew3, eb3, egain, eshift,
        nw1, nb1, nw2, nb2, nw3, nb3, ngain, nshift,
        ct_nodes,
        onehot, e0, e1, ct,
        a1_0, s1_0, a2_0, s2_0, n_0, r_0,
        a1_1, s1_1, a2_1, s2_1, n_1, r_1,
        live_count,
        tab, wbig, w2half, w3mid, w1et, w2t, w3t, averager,
        msum, gm, tt, dw, sums, window,
        sender_sum, sender_low, receiver_sum, rim_in,
        nm, nc1, nc2, nsl1, nsl2, nnorm, ninv, gz, gh_buf,
        src1, part1, col1, srcn, partn, coln, src0, part0, col0,
        in_sem, weight_sem, halo_sem, cell_send, cell_recv, rim_sem,
        *sum_sems,
    ) = refs[22:]
    gx, gy = lax.axis_index("gx"), lax.axis_index("gy")
    sum1 = Sum(CH1, (src1, part1, col1, sum1_out, sum_sems[0]), (gx, gy))
    sumn = Sum(CHN, (srcn, partn, coln, sumn_out, sum_sems[1]), (gx, gy))
    sum0 = Sum(CH0, (src0, part0, col0, sum0_out, sum_sems[2]), (gx, gy))
    kept = ((a1_0, s1_0, a2_0, s2_0, n_0, r_0), (a1_1, s1_1, a2_1, s2_1, n_1, r_1))
    edge_in = (e0, e1, e2)

    def neighbour(dx, dy):
        return (gx + dx, gy + dy)

    def inside(dx, dy):
        there = None
        for step_, at, last in ((dx, gx, 31), (dy, gy, 3)):
            if step_:
                here = at > 0 if step_ < 0 else at < last
                there = here if there is None else there & here
        return there

    def when(there, act):
        pl.when(there)(act)

    own_cells = [tab.at[0, 1 + c // 2, 1 + c % 2] for c in range(4)]
    node_loads = [
        pltpu.make_async_copy(nodes_hbm.at[32 * c : 32 * c + 32], own_cells[c], in_sem.at[2, c])
        for c in range(4)
    ]
    for copy in node_loads:
        copy.start()
    tab[1] = jnp.zeros_like(tab[1])
    for a in range(4):
        for b in range(4):
            if a in (0, 3) or b in (0, 3):
                tab[0, a, b] = jnp.zeros((32, D), BF)
    rim_in[...] = jnp.zeros_like(rim_in)
    barrier = pltpu.get_barrier_semaphore()

    def greet(device):
        pl.semaphore_signal(barrier, inc=1, device_id=device, device_id_type=MESH)

    for dx, dy in DIRS:
        when(inside(dx, dy), functools.partial(greet, neighbour(dx, dy)))
    x, z, y = sum1.x, sum1.z, sum1.y
    for dx, dy in PLANE:
        greet((((x + dx) % 4 * 2 + z) * 4 + (y + dy) % 4, gy))
    for dz, dg in COLUMN:
        greet(((x * 2 + (z + dz) % 2) * 4 + y, (gy + dg) % 4))

    def load(ref, scratch, which, t):
        s = rows_of(t * CELL, CELL)
        return pltpu.make_async_copy(ref.at[s], scratch.at[s], in_sem.at[which, t])

    weights = (
        ew1, eb1, ew2, eb2, ew3, eb3, egain, eshift, nw1, nb1, nw2, nb2, nw3, nb3, ngain, nshift,
    )
    small_loads = [
        pltpu.make_async_copy(src, dst, weight_sem.at[k])
        for k, (src, dst) in enumerate(
            zip((index_hbm, mask_hbm, ct_nodes_hbm, *weights_hbm), (index, mask, ct_nodes, *weights))
        )
    ]
    for copy in small_loads:
        copy.start()
    for t in range(4):
        load(edges, e0, 0, t).start()
    nx = (gx > 0).astype(jnp.int32) + (gx < 31).astype(jnp.int32)
    ny = (gy > 0).astype(jnp.int32) + (gy < 3).astype(jnp.int32)
    pl.semaphore_wait(barrier, nx + ny + nx * ny + len(PLANE) + len(COLUMN))
    for copy in node_loads:
        copy.wait()

    def halo_copy(k):
        dx, dy = DIRS[k]
        src = tab.at[0, span(dx, 1, 2, pl.ds(1, 2)), span(dy, 1, 2, pl.ds(1, 2))]
        dst = tab.at[0, span(dx, 3, 0, pl.ds(1, 2)), span(dy, 3, 0, pl.ds(1, 2))]
        return pltpu.make_async_remote_copy(
            src_ref=src,
            dst_ref=dst,
            send_sem=halo_sem.at[0, k],
            recv_sem=halo_sem.at[1, k],
            device_id=neighbour(dx, dy),
            device_id_type=MESH,
        )

    def exchange_start(copy_of, directions=range(8)):
        for k in directions:
            when(inside(*DIRS[k]), lambda k=k: copy_of(k).start())

    def exchange_finish(copy_of, directions=range(8)):
        for k in directions:
            dx, dy = DIRS[k]
            when(inside(-dx, -dy), lambda k=k: copy_of(k).wait_recv())

    def all_sent():
        for copy_of in (halo_copy, functools.partial(rim_copy, 1), functools.partial(rim_copy, 0)):
            for k, (dx, dy) in enumerate(DIRS):
                when(inside(dx, dy), lambda copy_of=copy_of, k=k: copy_of(k).wait_send())
        for c in range(4):
            for dx, dy, copy in cell_copies(c):
                when(inside(dx, dy), copy.wait_send)

    def cell_copies(c):
        i, j = c // 2, c % 2
        for k, (dx, dy) in enumerate(((2 * i - 1, 0), (0, 2 * j - 1), (2 * i - 1, 2 * j - 1))):
            a = 3 - 3 * i if dx else 1 + i
            b = 3 - 3 * j if dy else 1 + j
            copy = pltpu.make_async_remote_copy(
                src_ref=tab.at[1, 1 + i, 1 + j],
                dst_ref=tab.at[1, a, b],
                send_sem=cell_send.at[c, k],
                recv_sem=cell_recv.at[a, b],
                device_id=neighbour(dx, dy),
                device_id_type=MESH,
            )
            yield dx, dy, copy

    def cell_start(c):
        for dx, dy, copy in cell_copies(c):
            when(inside(dx, dy), copy.start)

    def cells_arrive(group):
        views = {
            1: ((1, 0, ((3, 1), (3, 2))), (0, 1, ((1, 3), (2, 3))), (1, 1, ((3, 3),))),
            2: ((0, -1, ((1, 0), (2, 0))), (1, -1, ((3, 0),))),
            3: ((-1, 0, ((0, 1), (0, 2))), (-1, -1, ((0, 0),)), (-1, 1, ((0, 3),))),
        }[group]

        def wait(places):
            for a, b in places:
                drain(tab.at[1, a, b], cell_recv.at[a, b])

        for dx, dy, places in views:
            when(inside(dx, dy), functools.partial(wait, places))

    exchange_start(halo_copy, EARLY)
    for t in range(4):
        load(ct_edges, ct, 1, t).start()
    for copy in small_loads:
        copy.wait()

    def latents(layer, cells=(0, 1, 2, 3)):
        return jnp.concatenate([tab[layer, 1 + c // 2, 1 + c % 2] for c in cells], 0)

    averager[...] = jnp.full((D, D), 1.0 / D, BF)
    for layer in range(2):
        w2half[layer] = (0.5 * ew2[layer].astype(F32)).astype(BF)
        w3 = ew3[layer].astype(F32)
        w3mid[layer] = (w3 - jnp.mean(w3, -1, keepdims=True)).astype(BF)
        w3t[layer] = w3mid[layer].T
        w2t[layer] = ew2[layer].T
        w1et[layer] = ew1[layer, 2 * D : 3 * D, :].T
    exchange_start(halo_copy, LATE)
    sums[...] = jnp.zeros_like(sums)
    dw[...] = jnp.zeros_like(dw)
    window[...] = jnp.zeros_like(window)

    count = jnp.sum(mask[...].astype(F32), -1, keepdims=True)
    live_count[...] = jnp.broadcast_to(count, (PARTS, D))
    cell_of = iota((PARTS, 64), 0) // 32
    place = index[...] - (cell_of // 2) * 128 - (cell_of % 2) * 32
    place = (place // 128) * 96 + place % 128
    dead = mask[...] == 0
    high = jnp.where(dead, 127, place // 16)
    low = jnp.where(dead, 0, place % 16)
    digits = jnp.concatenate([high, low], 1).astype(F32).astype(BF)
    spread = jnp.where(iota((D, D), 0) < 64, 16.0, 1.0).astype(BF)
    row = iota((CELL, D), 0)
    lane = iota((CELL, D), 1)
    pick = jnp.where(lane == row // 64, 1.0, 0.0).astype(BF)
    slot_mask, fixed = ge.at[0:CELL], ge.at[CELL : 2 * CELL]
    slot_mask[...] = jnp.where(lane % 64 == row % 64, 1.0, 0.0)
    fixed[...] = jnp.where((lane == 32 + row // 64) | (lane == 64) | (lane == 65), 1.0, 0.0)
    for c in range(4):
        digits_of = jnp.concatenate([digits[32 * c : 32 * c + 32], jnp.zeros((96, D), BF)], 0)
        for g in range(4):
            at = slice(512 * g, 512 * g + 512)
            own = (dot(pick[at], digits_of) * slot_mask[at, :]).astype(BF)
            found = dot(own, spread)
            s = slice(c * CELL + 512 * g, c * CELL + 512 * g + 512)
            column = iota((512, D), 1).astype(F32)
            onehot[s, 0:128] = jnp.where(found == column, 1.0, 0.0).astype(BF)
            onehot[s, 128:256] = jnp.where(found == column + 128.0, 1.0, 0.0).astype(BF)
            onehot[s, 256:384] = jnp.where(found == column + 256.0, 1.0, fixed[at, :]).astype(BF)

    def prepare(layer, cells):
        a0, b0 = min(c // 2 for c in cells), min(c % 2 for c in cells)
        high_a, high_b = max(c // 2 for c in cells) + 3 - a0, max(c % 2 for c in cells) + 3 - b0
        region = tab[layer, a0 : a0 + high_a, b0 : b0 + high_b].reshape(high_a * high_b * 32, D)
        senders = (0.5 * dot(region, ew1[layer, D : 2 * D, :])).astype(BF).reshape(high_a, high_b, 32, D)
        receivers = (0.5 * dot(latents(layer, cells), ew1[layer, 0:D, :])).astype(BF)
        bias = 0.5 * eb1[layer : layer + 1, :]
        bias_high = bias.astype(BF).astype(F32)
        at = iota((64, D), 0)
        bias_rows = jnp.where(at == 0, bias_high, jnp.where(at == 1, bias - bias_high, 0.0)).astype(BF)
        edge_rows = (0.5 * ew1[layer, 2 * D : 3 * D, :].astype(F32)).astype(BF)
        for k, c in enumerate(cells):
            i, j = c // 2 - a0, c % 2 - b0
            for a in range(3):
                wbig[c, 96 * a : 96 * a + 96, :] = senders[i + a, j : j + 3].reshape(96, D)
                window[layer, c, 96 * a : 96 * a + 96, 0:128] = tab[layer, c // 2 + a, c % 2 : c % 2 + 3].reshape(96, D)
            window[layer, c, 288:320, 128:256] = tab[layer, 1 + c // 2, 1 + c % 2]
            wbig[c, 288:320, :] = receivers[32 * k : 32 * k + 32]
            wbig[c, 320:384, :] = bias_rows
            wbig[c, 384:512, :] = edge_rows

    step = CELL // SUB
    per = step // 64

    def live_of(p):
        slot = iota((per, 64, D), 1).astype(F32)
        return slot < live_count[p, :][:, None, :]

    def forward(layer, c, parts=tuple(range(SUB))):
        a1, s1, a2, s2, nn, rr = kept[layer]
        e_in, e_out = edge_in[layer], edge_in[layer + 1]
        b2 = 0.5 * eb2[layer : layer + 1, :]
        b3 = eb3[layer : layer + 1, :]
        b3 = b3 - jnp.mean(b3, -1, keepdims=True)
        gain, shift = egain[layer : layer + 1, :], eshift[layer : layer + 1, :]
        groups = [rows_of(c * CELL + g * step, step) for g in parts]
        ones = [dot(jnp.concatenate([onehot[s, :], e_in[s, :]], 1), wbig[c]) for s in groups]
        first = []
        for s, half in zip(groups, ones):
            act, slope = silu_parts(half)
            a1[s, :] = act.astype(BF)
            s1[s, :] = slope.astype(BF)
            first.append(act.astype(BF))
        twos = [dot(act, w2half[layer]) + b2 for act in first]
        second = []
        for s, half in zip(groups, twos):
            act, slope = silu_parts(half)
            a2[s, :] = act.astype(BF)
            s2[s, :] = slope.astype(BF)
            second.append(act.astype(BF))
        mids = [dot(act, w3mid[layer]) + b3 for act in second]
        spreads = [dot((mid * mid).astype(BF), averager[...]) for mid in mids]
        for g, s, mid, var in zip(parts, groups, mids, spreads):
            inverse = lax.rsqrt(var + EPS)
            normed = mid * inverse
            nn[s, :] = normed.astype(BF)
            rr[s, :] = inverse
            update = (normed * gain + shift).reshape(per, 64, D)
            p = rows_of(c * 32 + g * per, per)
            live = live_of(p)
            new = e_in[s, :].astype(F32).reshape(per, 64, D) + jnp.where(live, update, 0.0)
            e_out[s, :] = new.astype(BF).reshape(step, D)
            msum[p, :] = jnp.sum(jnp.where(live, new, 0.0), 1)

    def node_forward(layer, cells):
        p = slice(32 * cells[0], 32 * cells[-1] + 32)
        h = latents(layer, cells)
        m = msum[p, :].astype(BF)
        z1 = dot(h, nw1[layer, 0:D, :]) + dot(m, nw1[layer, D : 2 * D, :]) + nb1[layer : layer + 1, :]
        c1, slope1 = silu_parts(0.5 * z1)
        c1 = c1.astype(BF)
        z2 = dot(c1, nw2[layer]) + nb2[layer : layer + 1, :]
        c2, slope2 = silu_parts(0.5 * z2)
        c2 = c2.astype(BF)
        z3 = dot(c2, nw3[layer]) + nb3[layer : layer + 1, :]
        mid = z3 - jnp.mean(z3, -1, keepdims=True)
        inverse = lax.rsqrt(jnp.mean(mid * mid, -1, keepdims=True) + EPS)
        normed = mid * inverse
        nm[layer, p], nc1[layer, p], nc2[layer, p] = m, c1, c2
        nsl1[layer, p], nsl2[layer, p], nnorm[layer, p] = slope1, slope2, normed
        ninv[layer, p] = jnp.broadcast_to(inverse, h.shape)
        update = normed * ngain[layer : layer + 1, :] + nshift[layer : layer + 1, :]
        result = (h.astype(F32) + update).astype(BF)
        if layer == 1:
            nodes_out[p, :] = result
        else:
            for k, c in enumerate(cells):
                tab[1, 1 + c // 2, 1 + c % 2] = result[32 * k : 32 * k + 32]

    def node_backward(layer, cells):
        p = slice(32 * cells[0], 32 * cells[-1] + 32)
        gh = gh_buf[p, :]
        normed = nnorm[layer, p]
        q = gh * ngain[layer : layer + 1, :]
        inner = q - jnp.mean(q, -1, keepdims=True) - normed * jnp.mean(q * normed, -1, keepdims=True)
        gz3 = ninv[layer, p] * inner
        gz2 = dot_nt(gz3.astype(BF), nw3[layer]) * nsl2[layer, p]
        gz1 = dot_nt(gz2.astype(BF), nw2[layer]) * nsl1[layer, p]
        gz[0, p], gz[1, p], gz[2, p] = gz1, gz2, gz3
        gm[p, :] = dot_nt(gz1.astype(BF), nw1[layer, D : 2 * D, :])

    def node_grads(layer, dst, row_, vec):
        low1, low2, low3 = (gz[k].astype(BF) for k in range(3))
        dst[row_ : row_ + 128, :] = dot_tn(latents(layer), low1).astype(BF)
        dst[row_ + 128 : row_ + 256, :] = dot_tn(nm[layer], low1).astype(BF)
        dst[row_ + 256 : row_ + 384, :] = dot_tn(nc1[layer], low2).astype(BF)
        dst[row_ + 384 : row_ + 512, :] = dot_tn(nc2[layer], low3).astype(BF)
        gh = gh_buf[...]
        vec.extend([column_sum(gz[k]) for k in range(3)])
        vec.extend([column_sum(gh * nnorm[layer]), column_sum(gh)])

    def backward(layer, c):
        a1, s1, a2, s2, nn, rr = kept[layer]
        e_in = edge_in[layer]
        gain = egain[layer : layer + 1, :]
        groups = [rows_of(c * CELL + g * step, step) for g in range(SUB)]
        firsts = []
        for g, s in enumerate(groups):
            p = rows_of(c * 32 + g * per, per)
            live = live_of(p)
            old = ct[s, :].astype(F32) if layer == 1 else ge[s, :]
            total = old.reshape(per, 64, D) + jnp.where(live, gm[p, :][:, None, :], 0.0)
            gy_ = jnp.where(live, total, 0.0).reshape(step, D)
            normed = nn[s, :].astype(F32)
            q = gy_ * gain
            qn = q * normed
            mean_qn = dot(qn.astype(BF), averager[...])
            firsts.append((total.reshape(step, D), gy_, q, qn, normed, mean_qn))
        g3 = [rr[s, :] * (f[2] - f[4] * f[5]) for s, f in zip(groups, firsts)]
        low3 = [g.astype(BF) for g in g3]
        g2 = [dot(g, w3t[layer]) * s2[s, :].astype(F32) for s, g in zip(groups, low3)]
        low2 = [g.astype(BF) for g in g2]
        low1 = [(dot(g, w2t[layer]) * s1[s, :].astype(F32)).astype(BF) for s, g in zip(groups, low2)]
        for s, g, f in zip(groups, low1, firsts):
            ge[s, :] = f[0]
            s1[s, :] = g
        sums[layer, 0] += sum(partial_rows(f[3]) for f in firsts)
        sums[layer, 1] += sum(partial_rows(f[1]) for f in firsts)
        sums[layer, 2] += sum(partial_rows(g) for g in g3)
        sums[layer, 3] += sum(partial_rows(g) for g in g2)
        s = rows_of(c * CELL, CELL)
        left = jnp.concatenate([onehot[s, :], e_in[s, :]], 1)
        tt[layer, c] = dot_tn(jnp.concatenate(low1, 0), left)
        if layer == 1:
            for s, two, three in zip(groups, low2, low3):
                s2[s, :] = two
                nn[s, :] = three
        else:
            dw[layer, 0:128] += dot_tn(jnp.concatenate(low2, 0), a1[s, :])
            dw[layer, 128:256] += dot_tn(jnp.concatenate(low3, 0), a2[s, :])

    def backward_rest(layer, c):
        a1, s1, a2, s2, nn, rr = kept[layer]
        s = rows_of(c * CELL, CELL)
        ge[s, :] += dot(s1[s, :], w1et[layer])
        if layer == 1:
            dw[layer, 0:128] += dot_tn(s2[s, :], a1[s, :])
            dw[layer, 128:256] += dot_tn(nn[s, :], a2[s, :])

    def rim_copy(layer, k):
        dx, dy = DIRS[k]
        src = sender_low.at[layer, span(dx, 0, 3, pl.ds(1, 2)), span(dy, 0, 3, pl.ds(1, 2))]
        dst = rim_in.at[layer, k, 0] if dx != 0 and dy != 0 else rim_in.at[layer, k]
        return pltpu.make_async_remote_copy(
            src_ref=src,
            dst_ref=dst,
            send_sem=rim_sem.at[layer, 0, k],
            recv_sem=rim_sem.at[layer, 1, k],
            device_id=neighbour(dx, dy),
            device_id_type=MESH,
        )

    def rims_sum(layer):
        sender_sum[...] = jnp.zeros_like(sender_sum)
        for c in range(4):
            i, j = c // 2, c % 2
            by_row = tt[layer, c, :, 0:384].T
            for a in range(3):
                piece = by_row[96 * a : 96 * a + 96].reshape(3, 32, D)
                for b in range(3):
                    sender_sum[i + a, j + b] += piece[b]
            receiver_sum[32 * c : 32 * c + 32, :] = by_row[288:320]
        sender_low[layer] = sender_sum[...].astype(BF)

    def edge_grads(layer, dst, row_, vec):
        by_node = sum(dot(tt[layer, c, :, 0:384].astype(BF), window[layer, c]) for c in range(4))
        by_edge = sum(tt[layer, c, :, 384:512] for c in range(4))
        ones = sum(tt[layer, c, :, 256:384] for c in range(4)).T[64:65]
        dst[row_ : row_ + 128, :] = by_node[:, 128:256].T.astype(BF)
        dst[row_ + 128 : row_ + 256, :] = by_node[:, 0:128].T.astype(BF)
        dst[row_ + 256 : row_ + 384, :] = by_edge.T.astype(BF)
        dst[row_ + 384 : row_ + 512, :] = dw[layer, 0:128].T.astype(BF)
        third = dw[layer, 128:256].T
        dst[row_ + 512 : row_ + 640, :] = (third - jnp.mean(third, -1, keepdims=True)).astype(BF)
        s = [column_sum(sums[layer, k]) for k in range(4)]
        s[2] = s[2] - jnp.mean(s[2], -1, keepdims=True)
        vec.extend([ones, s[3], s[2], s[0] / egain[layer : layer + 1, :], s[1]])

    def node_share(layer):
        part = dot_nt(gz[0].astype(BF), nw1[layer, 0:D, :])
        gh_buf[...] += part + dot_nt(receiver_sum[...].astype(BF), ew1[layer, 0:D, :])

    def sender_share(layer):
        own = [sender_sum[1 + c // 2, 1 + c % 2] for c in range(4)]
        for k, (dx, dy) in enumerate(DIRS):
            cells = [
                (i, j)
                for i in ((0, 1) if dx == 0 else ((0,) if dx > 0 else (1,)))
                for j in ((0, 1) if dy == 0 else ((0,) if dy > 0 else (1,)))
            ]
            for at, (i, j) in enumerate(cells):
                own[2 * i + j] = own[2 * i + j] + rim_in[layer, k, at].astype(F32)
        own = jnp.concatenate(own, 0).astype(BF)
        return gh_buf[...] + dot_nt(own, ew1[layer, D : 2 * D, :])

    def put_vectors(dst, row_, vec):
        at = iota((16, D), 0)
        block = jnp.zeros((16, D), F32)
        for k, v in enumerate(vec):
            block = jnp.where(at == k, v, block)
        dst[row_ : row_ + 16, :] = block.astype(BF)

    exchange_finish(halo_copy, EARLY)
    prepare(0, (0, 1))
    half = SUB // 2
    for c in range(4):
        load(edges, e0, 0, c).wait()
    forward(0, 0)
    forward(0, 1)
    exchange_finish(halo_copy, LATE)
    prepare(0, (2, 3))
    node_forward(0, (0, 1))
    forward(0, 2, tuple(range(half)))
    cell_start(0)
    cell_start(1)
    forward(0, 2, tuple(range(half, SUB)))
    node_forward(0, (2,))
    forward(0, 3)
    cell_start(2)
    node_forward(0, (3,))
    cell_start(3)

    gh_buf[...] = ct_nodes[...].astype(F32)
    src1[VEC1 + 16 :, :] = jnp.zeros((CH1 * 16 - VEC1 - 16, D), BF)
    src0[VEC0 + 16 :, :] = jnp.zeros((CH0 * 16 - VEC0 - 16, D), BF)
    cells_arrive(1)
    prepare(1, (3,))
    forward(1, 3)
    cells_arrive(2)
    prepare(1, (2,))
    node_forward(1, (3,))
    node_backward(1, (3,))
    forward(1, 2)
    cells_arrive(3)
    prepare(1, (0, 1))
    node_forward(1, (2,))
    node_backward(1, (2,))
    forward(1, 1)
    node_forward(1, (1,))
    node_backward(1, (1,))
    forward(1, 0)

    for c in range(4):
        load(ct_edges, ct, 1, c).wait()
    node_forward(1, (0,))
    node_backward(1, (0,))
    for c in (3, 2, 1, 0):
        backward(1, c)
    rims_sum(1)
    exchange_start(functools.partial(rim_copy, 1))
    vec1, vec0 = [], []
    node_grads(1, src1, NODE_W1, vec1)
    for c in range(4):
        backward_rest(1, c)
    edge_grads(1, src1, EDGE_W1, vec1)
    put_vectors(src1, VEC1, vec1)
    node_share(1)
    sum1.scatter_start()
    exchange_finish(functools.partial(rim_copy, 1))
    gh_buf[...] = sender_share(1)

    node_backward(0, (0, 1, 2, 3))
    node_grads(0, srcn, 0, vec0)
    sumn.scatter_start()
    for c in range(4):
        backward(0, c)
    edge_grads(0, src0, EDGE_W1, vec0)
    put_vectors(src0, VEC0, vec0)
    sum0.scatter_start()
    rims_sum(0)
    exchange_start(functools.partial(rim_copy, 0))
    sum1.scatter_finish()
    sum1.column_start()
    sumn.scatter_finish()
    sumn.column_start()
    for c in range(4):
        backward_rest(0, c)
    node_share(0)
    sum0.scatter_finish()
    sum0.column_start()
    sum1.column_finish()
    sum1.gather_start()
    sumn.column_finish()
    sumn.gather_start()
    sum0.column_finish()
    sum0.gather_start()
    exchange_finish(functools.partial(rim_copy, 0))
    grad_nodes[...] = sender_share(0)
    all_sent()
    sum1.gather_finish()
    sumn.gather_finish()
    sum0.gather_finish()


def unpack_kernel(nodes_in, edges_in, grad_nodes_in, grad_edges_in, sum1, sumn, sum0, *rest):
    (nodes_out, edges_out, grad_nodes, grad_edges), outs = rest[:4], rest[4:20]
    held, (sems, small) = rest[20:36], rest[36:]
    w1, b1, w2, b2, w3, b3, gain, shift, v1, c1, v2, c2, v3, c3, ngain, nshift = held
    copies = [
        pltpu.make_async_copy(nodes_in, nodes_out, sems.at[2, 0]),
        pltpu.make_async_copy(grad_nodes_in, grad_nodes, sems.at[2, 1]),
    ]
    for t in range(4):
        s = pl.ds(t * CELL, CELL)
        copies.append(pltpu.make_async_copy(grad_edges_in.at[s], grad_edges.at[s], sems.at[0, t]))
        copies.append(pltpu.make_async_copy(edges_in.at[s], edges_out.at[s], sems.at[1, t]))
    for copy in copies:
        copy.start()

    def put(ref, layer, buffer, row):
        height = ref.shape[1]
        ref[layer] = buffer[row : row + height, :].astype(F32)

    for layer, buffer in ((1, sum1), (0, sum0)):
        put(w1, layer, buffer, EDGE_W1)
        put(w2, layer, buffer, EDGE_W2)
        put(w3, layer, buffer, EDGE_W3)
    for layer, buffer, row in ((1, sum1, 0), (0, sumn, -NODE_W1)):
        put(v1, layer, buffer, row + NODE_W1)
        put(v2, layer, buffer, row + NODE_W2)
        put(v3, layer, buffer, row + NODE_W3)
    for layer, block in ((1, sum1[VEC1 : VEC1 + 16, :]), (0, sum0[VEC0 : VEC0 + 16, :])):
        rows = block.astype(F32)
        for k, ref in enumerate((c1, c2, c3, ngain, nshift, b1, b2, b3, gain, shift)):
            ref[layer : layer + 1, :] = rows[k : k + 1]
    for k, (src, dst) in enumerate(zip(held, outs)):
        copies.append(pltpu.make_async_copy(src, dst, small.at[k]))
        copies[-1].start()
    for copy in copies:
        copy.wait()


def per_device(nodes, edges, nbr_index, nbr_mask, *rest):
    weights, ct_nodes, ct_edges = rest[:16], rest[16], rest[17]
    vmem = pl.BlockSpec(memory_space=pltpu.VMEM)
    hbm = pl.BlockSpec(memory_space=pl.ANY)
    shape = jax.ShapeDtypeStruct
    big = pltpu.VMEM((ROWS, D), BF)
    node_bf = pltpu.VMEM((2, PARTS, D), BF)
    node_f32 = pltpu.VMEM((2, PARTS, D), F32)
    square = pltpu.VMEM((2, D, D), BF)
    dma = pltpu.SemaphoreType.DMA

    def sum_scratch(chunk):
        return [
            pltpu.VMEM((16 * chunk, D), BF),
            pltpu.VMEM((16, chunk, D), BF),
            pltpu.VMEM((8, chunk, D), BF),
        ]

    scratch = [
        pltpu.VMEM((PARTS, 64), jnp.int32),
        pltpu.VMEM((PARTS, 64), jnp.int32),
        *(pltpu.VMEM(w.shape, w.dtype) for w in weights),
        pltpu.VMEM((PARTS, D), BF),
        pltpu.VMEM((ROWS, 3 * D), BF),
        big, big, big,
        *(([big] * 5 + [pltpu.VMEM((ROWS, D), F32)]) * 2),
        pltpu.VMEM((PARTS, D), F32),
        pltpu.VMEM((2, 4, 4, 32, D), BF),
        pltpu.VMEM((4, 4 * D, D), BF),
        square, square, square, square, square,
        pltpu.VMEM((D, D), BF),
        pltpu.VMEM((PARTS, D), F32),
        pltpu.VMEM((PARTS, D), F32),
        pltpu.VMEM((2, 4, D, 4 * D), F32),
        pltpu.VMEM((2, 2 * D, D), F32),
        pltpu.VMEM((2, 4, 8, D), F32),
        pltpu.VMEM((2, 4, 3 * D, 2 * D), BF),
        pltpu.VMEM((4, 4, 32, D), F32),
        pltpu.VMEM((2, 4, 4, 32, D), BF),
        pltpu.VMEM((PARTS, D), F32),
        pltpu.VMEM((2, 8, 2, 32, D), BF),
        node_bf, node_bf, node_bf, node_f32, node_f32, node_f32, node_f32,
        pltpu.VMEM((3, PARTS, D), F32),
        pltpu.VMEM((PARTS, D), F32),
        *sum_scratch(CH1),
        *sum_scratch(CHN),
        *sum_scratch(CH0),
        dma((3, 4)), dma((19,)), dma((2, 8)), dma((4, 3)), dma((4, 4)), dma((2, 2, 8)),
        *([dma((3, 2))] * 3),
    ]
    held = pl.pallas_call(
        main_kernel,
        out_shape=(
            pltpu.VMEM((PARTS, D), BF),
            pltpu.VMEM((ROWS, D), BF),
            pltpu.VMEM((PARTS, D), F32),
            pltpu.VMEM((ROWS, D), F32),
            pltpu.VMEM((16 * CH1, D), BF),
            pltpu.VMEM((16 * CHN, D), BF),
            pltpu.VMEM((16 * CH0, D), BF),
        ),
        in_specs=[hbm] * 22,
        out_specs=(vmem,) * 7,
        scratch_shapes=scratch,
        compiler_params=pltpu.CompilerParams(
            collective_id=0, has_side_effects=True, vmem_limit_bytes=53 * 1024 * 1024
        ),
        name="interaction_layers",
    )(
        nodes.reshape(PARTS, D),
        edges.reshape(ROWS, D),
        nbr_index.reshape(PARTS, 64),
        nbr_mask.reshape(PARTS, 64),
        *weights,
        ct_nodes.reshape(PARTS, D),
        ct_edges.reshape(ROWS, D),
    )
    held = [pltpu.with_memory_space_constraint(value, pltpu.VMEM) for value in held]
    nodes_out, edges_out, grad_nodes, grad_edges, *grads = pl.pallas_call(
        unpack_kernel,
        out_shape=(
            shape((PARTS, D), BF),
            shape((ROWS, D), BF),
            shape((PARTS, D), F32),
            shape((ROWS, D), F32),
            *(shape(w.shape, F32) for w in weights),
        ),
        in_specs=[vmem] * 7,
        out_specs=(hbm,) * 20,
        scratch_shapes=[*(pltpu.VMEM(w.shape, F32) for w in weights), dma((3, 4)), dma((16,))],
        compiler_params=pltpu.CompilerParams(vmem_limit_bytes=8 * 1024 * 1024),
        name="unpack_sums",
    )(*held)
    return (
        nodes_out.reshape(nodes.shape),
        edges_out.reshape(edges.shape),
        grad_nodes.reshape(nodes.shape),
        grad_edges.reshape(edges.shape),
        *grads,
    )


def solution(mesh):
    cells = P("gx", "gy", None, None)
    wide = P("gx", "gy", None, None, None)
    in_specs = (cells, wide, cells, cells) + (P(),) * 16 + (cells, wide)
    out_specs = (cells, wide, cells, wide) + (P(),) * 16
    return jax.shard_map(
        per_device, mesh=mesh, in_specs=in_specs, out_specs=out_specs, check_vma=False
    )
```

```python
import functools

import jax
import jax.numpy as jnp
from jax import lax
from jax.experimental import pallas as pl
from jax.experimental.pallas import tpu as pltpu
from jax.sharding import PartitionSpec as P

EPS = 1e-05
BF = jnp.bfloat16
F32 = jnp.float32
MESH = pl.DeviceIdType.MESH

D = 128
ROWS = 8192
CELL = 2048
SUB = 4
PARTS = 128

DIRS = ((1, 0), (1, 1), (1, -1), (0, 1), (0, -1), (-1, 0), (-1, 1), (-1, -1))
EARLY, LATE = range(5), range(5, 8)
PLANE = (
    (2, 2), (1, 2), (2, 1), (3, 2), (2, 3), (2, 0), (0, 2), (1, 1), (3, 3), (1, 3), (3, 1), (1, 0), (0, 1), (3, 0), (0, 3),
)
COLUMN = ((1, 0), (1, 1), (1, 3), (1, 2), (0, 2), (0, 3), (0, 1))

CH1 = 80
CHN = 32
CH0 = 48
EDGE_W1, EDGE_W2, EDGE_W3 = 0, 384, 512
NODE_W1, NODE_W2, NODE_W3 = 640, 896, 1024
VEC1 = 1152
VEC0 = 640


def dot(a, b):
    return jnp.dot(a, b, preferred_element_type=F32)


def dot_nt(a, b):
    return lax.dot_general(a, b, (((1,), (1,)), ((), ())), preferred_element_type=F32)


def dot_tn(a, b):
    return lax.dot_general(a, b, (((0,), (0,)), ((), ())), preferred_element_type=F32)


def iota(shape, dim):
    return lax.broadcasted_iota(jnp.int32, shape, dim)


def silu_parts(half):
    t = jnp.tanh(half)
    wide = 1.0 + t
    act = half * wide
    return act, wide + act * (1.0 - t)


def rows_of(start, count):
    if isinstance(start, int):
        return slice(start, start + count)
    return pl.ds(pl.multiple_of(start, count), count)


def partial_rows(x):
    return jnp.sum(x.reshape(-1, 8, D), 0)


def column_sum(x):
    return jnp.sum(x, 0, keepdims=True)


def span(step, low, high, both):
    return low if step < 0 else (high if step > 0 else both)


def drain(view, sem):
    pltpu.make_async_copy(view, view, sem).wait()


class Sum:
    def __init__(self, chunk, refs, place):
        self.chunk = chunk
        self.src, self.part, self.col, self.out = refs[:4]
        self.sems = refs[4]
        self.gx, self.gy = place
        self.x, self.z, self.y = self.gx // 8, (self.gx // 4) % 2, self.gx % 4
        self.me = self.x * 4 + self.y
        self.mine = self.z * 4 + self.gy

    def rows(self, index):
        return pl.ds(pl.multiple_of(index * self.chunk, 16), self.chunk)

    def send(self, src, dst, phase, device):
        pltpu.make_async_remote_copy(
            src_ref=src,
            dst_ref=dst,
            send_sem=self.sems.at[phase, 0],
            recv_sem=self.sems.at[phase, 1],
            device_id=device,
            device_id_type=MESH,
        ).start()

    def wait(self, view, phase):
        drain(view, self.sems.at[phase, 0])
        drain(view, self.sems.at[phase, 1])

    def scatter_start(self):
        for dx, dy in PLANE:
            px, py = (self.x + dx) % 4, (self.y + dy) % 4
            src = self.src.at[self.rows(px * 4 + py)]
            self.send(src, self.part.at[self.me], 0, ((px * 2 + self.z) * 4 + py, self.gy))
        self.part[self.me] = self.src[self.rows(self.me), :]

    def scatter_finish(self):
        self.wait(self.part.at[pl.ds(0, 15)], 0)
        total = self.part[0].astype(F32)
        for k in range(1, 16):
            total = total + self.part[k].astype(F32)
        self.col[self.mine] = total.astype(BF)

    def column_start(self):
        own = self.col.at[self.mine]
        for dz, dg in COLUMN:
            pz, pg = (self.z + dz) % 2, (self.gy + dg) % 4
            self.send(own, own, 1, ((self.x * 2 + pz) * 4 + self.y, pg))

    def column_finish(self):
        self.wait(self.col.at[pl.ds(0, 7)], 1)
        total = self.col[0].astype(F32)
        for k in range(1, 8):
            total = total + self.col[k].astype(F32)
        self.out[self.rows(self.me), :] = total.astype(BF)

    def gather_start(self):
        own = self.out.at[self.rows(self.me)]
        for dx, dy in PLANE:
            px, py = (self.x + dx) % 4, (self.y + dy) % 4
            self.send(own, own, 2, ((px * 2 + self.z) * 4 + py, self.gy))

    def gather_finish(self):
        self.wait(self.out.at[pl.ds(0, 15 * self.chunk)], 2)


def main_kernel(*refs):
    (
        nodes_hbm, edges, index_hbm, mask_hbm, *weights_hbm,
    ) = refs[:20]
    ct_nodes_hbm, ct_edges = refs[20:22]
    (
        nodes_out, e2, grad_nodes, ge, sum1_out, sumn_out, sum0_out,
        index, mask,
        ew1, eb1, ew2, eb2, ew3, eb3, egain, eshift,
        nw1, nb1, nw2, nb2, nw3, nb3, ngain, nshift,
        ct_nodes,
        onehot, e0, e1, ct,
        a1_0, s1_0, a2_0, s2_0, n_0, r_0,
        a1_1, s1_1, a2_1, s2_1, n_1, r_1,
        live_count,
        tab, wbig, w2half, w3mid, w1et, w2t, w3t, averager,
        msum, gm, tt, dw, sums, window,
        sender_sum, sender_low, receiver_sum, rim_in,
        nm, nc1, nc2, nsl1, nsl2, nnorm, ninv, gz, gh_buf,
        src1, part1, col1, srcn, partn, coln, src0, part0, col0,
        in_sem, weight_sem, halo_sem, cell_send, cell_recv, rim_sem,
        *sum_sems,
    ) = refs[22:]
    gx, gy = lax.axis_index("gx"), lax.axis_index("gy")
    sum1 = Sum(CH1, (src1, part1, col1, sum1_out, sum_sems[0]), (gx, gy))
    sumn = Sum(CHN, (srcn, partn, coln, sumn_out, sum_sems[1]), (gx, gy))
    sum0 = Sum(CH0, (src0, part0, col0, sum0_out, sum_sems[2]), (gx, gy))
    kept = ((a1_0, s1_0, a2_0, s2_0, n_0, r_0), (a1_1, s1_1, a2_1, s2_1, n_1, r_1))
    edge_in = (e0, e1, e2)

    def neighbour(dx, dy):
        return (gx + dx, gy + dy)

    def inside(dx, dy):
        there = None
        for step_, at, last in ((dx, gx, 31), (dy, gy, 3)):
            if step_:
                here = at > 0 if step_ < 0 else at < last
                there = here if there is None else there & here
        return there

    def when(there, act):
        pl.when(there)(act)

    own_cells = [tab.at[0, 1 + c // 2, 1 + c % 2] for c in range(4)]
    node_loads = [
        pltpu.make_async_copy(nodes_hbm.at[32 * c : 32 * c + 32], own_cells[c], in_sem.at[2, c])
        for c in range(4)
    ]
    for copy in node_loads:
        copy.start()
    tab[1] = jnp.zeros_like(tab[1])
    for a in range(4):
        for b in range(4):
            if a in (0, 3) or b in (0, 3):
                tab[0, a, b] = jnp.zeros((32, D), BF)
    rim_in[...] = jnp.zeros_like(rim_in)
    barrier = pltpu.get_barrier_semaphore()

    def greet(device):
        pl.semaphore_signal(barrier, inc=1, device_id=device, device_id_type=MESH)

    for dx, dy in DIRS:
        when(inside(dx, dy), functools.partial(greet, neighbour(dx, dy)))
    x, z, y = sum1.x, sum1.z, sum1.y
    for dx, dy in PLANE:
        greet((((x + dx) % 4 * 2 + z) * 4 + (y + dy) % 4, gy))
    for dz, dg in COLUMN:
        greet(((x * 2 + (z + dz) % 2) * 4 + y, (gy + dg) % 4))

    def load(ref, scratch, which, t):
        s = rows_of(t * CELL, CELL)
        return pltpu.make_async_copy(ref.at[s], scratch.at[s], in_sem.at[which, t])

    weights = (
        ew1, eb1, ew2, eb2, ew3, eb3, egain, eshift, nw1, nb1, nw2, nb2, nw3, nb3, ngain, nshift,
    )
    small_loads = [
        pltpu.make_async_copy(src, dst, weight_sem.at[k])
        for k, (src, dst) in enumerate(
            zip((index_hbm, mask_hbm, ct_nodes_hbm, *weights_hbm), (index, mask, ct_nodes, *weights))
        )
    ]
    for copy in small_loads:
        copy.start()
    for t in range(4):
        load(edges, e0, 0, t).start()
    nx = (gx > 0).astype(jnp.int32) + (gx < 31).astype(jnp.int32)
    ny = (gy > 0).astype(jnp.int32) + (gy < 3).astype(jnp.int32)
    pl.semaphore_wait(barrier, nx + ny + nx * ny + len(PLANE) + len(COLUMN))
    for copy in node_loads:
        copy.wait()

    def halo_copy(k):
        dx, dy = DIRS[k]
        src = tab.at[0, span(dx, 1, 2, pl.ds(1, 2)), span(dy, 1, 2, pl.ds(1, 2))]
        dst = tab.at[0, span(dx, 3, 0, pl.ds(1, 2)), span(dy, 3, 0, pl.ds(1, 2))]
        return pltpu.make_async_remote_copy(
            src_ref=src,
            dst_ref=dst,
            send_sem=halo_sem.at[0, k],
            recv_sem=halo_sem.at[1, k],
            device_id=neighbour(dx, dy),
            device_id_type=MESH,
        )

    def exchange_start(copy_of, directions=range(8)):
        for k in directions:
            when(inside(*DIRS[k]), lambda k=k: copy_of(k).start())

    def exchange_finish(copy_of, directions=range(8)):
        for k in directions:
            dx, dy = DIRS[k]
            when(inside(-dx, -dy), lambda k=k: copy_of(k).wait_recv())

    def all_sent():
        for copy_of in (halo_copy, functools.partial(rim_copy, 1), functools.partial(rim_copy, 0)):
            for k, (dx, dy) in enumerate(DIRS):
                when(inside(dx, dy), lambda copy_of=copy_of, k=k: copy_of(k).wait_send())
        for c in range(4):
            for dx, dy, copy in cell_copies(c):
                when(inside(dx, dy), copy.wait_send)

    def cell_copies(c):
        i, j = c // 2, c % 2
        for k, (dx, dy) in enumerate(((2 * i - 1, 0), (0, 2 * j - 1), (2 * i - 1, 2 * j - 1))):
            a = 3 - 3 * i if dx else 1 + i
            b = 3 - 3 * j if dy else 1 + j
            copy = pltpu.make_async_remote_copy(
                src_ref=tab.at[1, 1 + i, 1 + j],
                dst_ref=tab.at[1, a, b],
                send_sem=cell_send.at[c, k],
                recv_sem=cell_recv.at[a, b],
                device_id=neighbour(dx, dy),
                device_id_type=MESH,
            )
            yield dx, dy, copy

    def cell_start(c):
        for dx, dy, copy in cell_copies(c):
            when(inside(dx, dy), copy.start)

    def cells_arrive(group):
        views = {
            1: ((1, 0, ((3, 1), (3, 2))), (0, 1, ((1, 3), (2, 3))), (1, 1, ((3, 3),))),
            2: ((0, -1, ((1, 0), (2, 0))), (1, -1, ((3, 0),))),
            3: ((-1, 0, ((0, 1), (0, 2))), (-1, -1, ((0, 0),)), (-1, 1, ((0, 3),))),
        }[group]

        def wait(places):
            for a, b in places:
                drain(tab.at[1, a, b], cell_recv.at[a, b])

        for dx, dy, places in views:
            when(inside(dx, dy), functools.partial(wait, places))

    exchange_start(halo_copy, EARLY)
    for t in range(4):
        load(ct_edges, ct, 1, t).start()
    for copy in small_loads:
        copy.wait()

    def latents(layer, cells=(0, 1, 2, 3)):
        return jnp.concatenate([tab[layer, 1 + c // 2, 1 + c % 2] for c in cells], 0)

    averager[...] = jnp.full((D, D), 1.0 / D, BF)
    for layer in range(2):
        w2half[layer] = (0.5 * ew2[layer].astype(F32)).astype(BF)
        w3 = ew3[layer].astype(F32)
        w3mid[layer] = (w3 - jnp.mean(w3, -1, keepdims=True)).astype(BF)
        w3t[layer] = (0.5 * w3mid[layer].astype(F32)).astype(BF).T
        w2t[layer] = w2half[layer].T
        w1et[layer] = ew1[layer, 2 * D : 3 * D, :].T
    exchange_start(halo_copy, LATE)
    sums[...] = jnp.zeros_like(sums)
    dw[...] = jnp.zeros_like(dw)
    window[...] = jnp.zeros_like(window)

    count = jnp.sum(mask[...].astype(F32), -1, keepdims=True)
    live_count[...] = jnp.broadcast_to(count, (PARTS, D))
    cell_of = iota((PARTS, 64), 0) // 32
    place = index[...] - (cell_of // 2) * 128 - (cell_of % 2) * 32
    place = (place // 128) * 96 + place % 128
    dead = mask[...] == 0
    high = jnp.where(dead, 127, place // 16)
    low = jnp.where(dead, 0, place % 16)
    digits = jnp.concatenate([high, low], 1).astype(F32).astype(BF)
    spread = jnp.where(iota((D, D), 0) < 64, 16.0, 1.0).astype(BF)
    row = iota((CELL, D), 0)
    lane = iota((CELL, D), 1)
    pick = jnp.where(lane == row // 64, 1.0, 0.0).astype(BF)
    slot_mask, fixed = ge.at[0:CELL], ge.at[CELL : 2 * CELL]
    slot_mask[...] = jnp.where(lane % 64 == row % 64, 1.0, 0.0)
    fixed[...] = jnp.where((lane == 32 + row // 64) | (lane == 64) | (lane == 65), 1.0, 0.0)
    for c in range(4):
        digits_of = jnp.concatenate([digits[32 * c : 32 * c + 32], jnp.zeros((96, D), BF)], 0)
        for g in range(4):
            at = slice(512 * g, 512 * g + 512)
            own = (dot(pick[at], digits_of) * slot_mask[at, :]).astype(BF)
            found = dot(own, spread)
            s = slice(c * CELL + 512 * g, c * CELL + 512 * g + 512)
            column = iota((512, D), 1).astype(F32)
            onehot[s, 0:128] = jnp.where(found == column, 1.0, 0.0).astype(BF)
            onehot[s, 128:256] = jnp.where(found == column + 128.0, 1.0, 0.0).astype(BF)
            onehot[s, 256:384] = jnp.where(found == column + 256.0, 1.0, fixed[at, :]).astype(BF)

    def prepare(layer, cells):
        a0, b0 = min(c // 2 for c in cells), min(c % 2 for c in cells)
        high_a, high_b = max(c // 2 for c in cells) + 3 - a0, max(c % 2 for c in cells) + 3 - b0
        region = tab[layer, a0 : a0 + high_a, b0 : b0 + high_b].reshape(high_a * high_b * 32, D)
        senders = (0.5 * dot(region, ew1[layer, D : 2 * D, :])).astype(BF).reshape(high_a, high_b, 32, D)
        receivers = (0.5 * dot(latents(layer, cells), ew1[layer, 0:D, :])).astype(BF)
        bias = 0.5 * eb1[layer : layer + 1, :]
        bias_high = bias.astype(BF).astype(F32)
        at = iota((64, D), 0)
        bias_rows = jnp.where(at == 0, bias_high, jnp.where(at == 1, bias - bias_high, 0.0)).astype(BF)
        edge_rows = (0.5 * ew1[layer, 2 * D : 3 * D, :].astype(F32)).astype(BF)
        for k, c in enumerate(cells):
            i, j = c // 2 - a0, c % 2 - b0
            for a in range(3):
                wbig[c, 96 * a : 96 * a + 96, :] = senders[i + a, j : j + 3].reshape(96, D)
                window[layer, c, 96 * a : 96 * a + 96, 0:128] = tab[layer, c // 2 + a, c % 2 : c % 2 + 3].reshape(96, D)
            window[layer, c, 288:320, 128:256] = tab[layer, 1 + c // 2, 1 + c % 2]
            wbig[c, 288:320, :] = receivers[32 * k : 32 * k + 32]
            wbig[c, 320:384, :] = bias_rows
            wbig[c, 384:512, :] = edge_rows

    step = CELL // SUB
    per = step // 64

    def live_of(p):
        slot = iota((per, 64, D), 1).astype(F32)
        return slot < live_count[p, :][:, None, :]

    def forward(layer, c, parts=tuple(range(SUB))):
        a1, s1, a2, s2, nn, rr = kept[layer]
        e_in, e_out = edge_in[layer], edge_in[layer + 1]
        b2 = 0.5 * eb2[layer : layer + 1, :]
        b3 = eb3[layer : layer + 1, :]
        b3 = b3 - jnp.mean(b3, -1, keepdims=True)
        gain, shift = egain[layer : layer + 1, :], eshift[layer : layer + 1, :]
        groups = [rows_of(c * CELL + g * step, step) for g in parts]
        ones = [dot(jnp.concatenate([onehot[s, :], e_in[s, :]], 1), wbig[c]) for s in groups]
        first = []
        for s, half in zip(groups, ones):
            act, slope = silu_parts(half)
            a1[s, :] = act.astype(BF)
            s1[s, :] = slope.astype(BF)
            first.append(act.astype(BF))
        twos = [dot(act, w2half[layer]) + b2 for act in first]
        second = []
        for s, half in zip(groups, twos):
            act, slope = silu_parts(half)
            a2[s, :] = act.astype(BF)
            s2[s, :] = slope.astype(BF)
            second.append(act.astype(BF))
        mids = [dot(act, w3mid[layer]) + b3 for act in second]
        spreads = [dot((mid * mid).astype(BF), averager[...]) for mid in mids]
        for g, s, mid, var in zip(parts, groups, mids, spreads):
            inverse = lax.rsqrt(var + EPS)
            normed = mid * inverse
            nn[s, :] = normed.astype(BF)
            rr[s, :] = inverse
            update = (normed * gain + shift).reshape(per, 64, D)
            p = rows_of(c * 32 + g * per, per)
            live = live_of(p)
            new = e_in[s, :].astype(F32).reshape(per, 64, D) + jnp.where(live, update, 0.0)
            e_out[s, :] = new.astype(BF).reshape(step, D)
            msum[p, :] = jnp.sum(jnp.where(live, new, 0.0), 1)

    def node_forward(layer, cells):
        p = slice(32 * cells[0], 32 * cells[-1] + 32)
        h = latents(layer, cells)
        m = msum[p, :].astype(BF)
        z1 = dot(h, nw1[layer, 0:D, :]) + dot(m, nw1[layer, D : 2 * D, :]) + nb1[layer : layer + 1, :]
        c1, slope1 = silu_parts(0.5 * z1)
        c1 = c1.astype(BF)
        z2 = dot(c1, nw2[layer]) + nb2[layer : layer + 1, :]
        c2, slope2 = silu_parts(0.5 * z2)
        c2 = c2.astype(BF)
        z3 = dot(c2, nw3[layer]) + nb3[layer : layer + 1, :]
        mid = z3 - jnp.mean(z3, -1, keepdims=True)
        inverse = lax.rsqrt(jnp.mean(mid * mid, -1, keepdims=True) + EPS)
        normed = mid * inverse
        nm[layer, p], nc1[layer, p], nc2[layer, p] = m, c1, c2
        nsl1[layer, p], nsl2[layer, p], nnorm[layer, p] = 0.5 * slope1, 0.5 * slope2, normed
        ninv[layer, p] = jnp.broadcast_to(inverse, h.shape)
        update = normed * ngain[layer : layer + 1, :] + nshift[layer : layer + 1, :]
        result = (h.astype(F32) + update).astype(BF)
        if layer == 1:
            nodes_out[p, :] = result
        else:
            for k, c in enumerate(cells):
                tab[1, 1 + c // 2, 1 + c % 2] = result[32 * k : 32 * k + 32]

    def node_backward(layer, cells):
        p = slice(32 * cells[0], 32 * cells[-1] + 32)
        gh = gh_buf[p, :]
        normed = nnorm[layer, p]
        q = gh * ngain[layer : layer + 1, :]
        inner = q - jnp.mean(q, -1, keepdims=True) - normed * jnp.mean(q * normed, -1, keepdims=True)
        gz3 = ninv[layer, p] * inner
        gz2 = dot_nt(gz3.astype(BF), nw3[layer]) * nsl2[layer, p]
        gz1 = dot_nt(gz2.astype(BF), nw2[layer]) * nsl1[layer, p]
        gz[0, p], gz[1, p], gz[2, p] = gz1, gz2, gz3
        gm[p, :] = dot_nt(gz1.astype(BF), nw1[layer, D : 2 * D, :])

    def node_grads(layer, dst, row_, vec):
        low1, low2, low3 = (gz[k].astype(BF) for k in range(3))
        dst[row_ : row_ + 128, :] = dot_tn(latents(layer), low1).astype(BF)
        dst[row_ + 128 : row_ + 256, :] = dot_tn(nm[layer], low1).astype(BF)
        dst[row_ + 256 : row_ + 384, :] = dot_tn(nc1[layer], low2).astype(BF)
        dst[row_ + 384 : row_ + 512, :] = dot_tn(nc2[layer], low3).astype(BF)
        gh = gh_buf[...]
        vec.extend([column_sum(gz[k]) for k in range(3)])
        vec.extend([column_sum(gh * nnorm[layer]), column_sum(gh)])

    def backward(layer, c):
        a1, s1, a2, s2, nn, rr = kept[layer]
        e_in = edge_in[layer]
        gain = egain[layer : layer + 1, :]
        groups = [rows_of(c * CELL + g * step, step) for g in range(SUB)]
        firsts = []
        for g, s in enumerate(groups):
            p = rows_of(c * 32 + g * per, per)
            live = live_of(p)
            old = ct[s, :].astype(F32) if layer == 1 else ge[s, :]
            total = old.reshape(per, 64, D) + jnp.where(live, gm[p, :][:, None, :], 0.0)
            gy_ = jnp.where(live, total, 0.0).reshape(step, D)
            normed = nn[s, :].astype(F32)
            q = gy_ * gain
            qn = q * normed
            mean_qn = dot(qn.astype(BF), averager[...])
            firsts.append((total.reshape(step, D), gy_, q, qn, normed, mean_qn))
        g3 = [rr[s, :] * (f[2] - f[4] * f[5]) for s, f in zip(groups, firsts)]
        low3 = [g.astype(BF) for g in g3]
        g2 = [dot(g, w3t[layer]) * s2[s, :].astype(F32) for s, g in zip(groups, low3)]
        low2 = [g.astype(BF) for g in g2]
        low1 = [(dot(g, w2t[layer]) * s1[s, :].astype(F32)).astype(BF) for s, g in zip(groups, low2)]
        for s, g, f in zip(groups, low1, firsts):
            ge[s, :] = f[0]
            s1[s, :] = g
        sums[layer, 0] += sum(partial_rows(f[3]) for f in firsts)
        sums[layer, 1] += sum(partial_rows(f[1]) for f in firsts)
        sums[layer, 2] += sum(partial_rows(g) for g in g3)
        sums[layer, 3] += sum(partial_rows(g) for g in g2)
        s = rows_of(c * CELL, CELL)
        left = jnp.concatenate([onehot[s, :], e_in[s, :]], 1)
        tt[layer, c] = dot_tn(jnp.concatenate(low1, 0), left)
        if layer == 1:
            for s, two, three in zip(groups, low2, low3):
                s2[s, :] = two
                nn[s, :] = three
        else:
            dw[layer, 0:128] += dot_tn(jnp.concatenate(low2, 0), a1[s, :])
            dw[layer, 128:256] += dot_tn(jnp.concatenate(low3, 0), a2[s, :])

    def backward_rest(layer, c):
        a1, s1, a2, s2, nn, rr = kept[layer]
        s = rows_of(c * CELL, CELL)
        ge[s, :] += dot(s1[s, :], w1et[layer])
        if layer == 1:
            dw[layer, 0:128] += dot_tn(s2[s, :], a1[s, :])
            dw[layer, 128:256] += dot_tn(nn[s, :], a2[s, :])

    def rim_copy(layer, k):
        dx, dy = DIRS[k]
        src = sender_low.at[layer, span(dx, 0, 3, pl.ds(1, 2)), span(dy, 0, 3, pl.ds(1, 2))]
        dst = rim_in.at[layer, k, 0] if dx != 0 and dy != 0 else rim_in.at[layer, k]
        return pltpu.make_async_remote_copy(
            src_ref=src,
            dst_ref=dst,
            send_sem=rim_sem.at[layer, 0, k],
            recv_sem=rim_sem.at[layer, 1, k],
            device_id=neighbour(dx, dy),
            device_id_type=MESH,
        )

    def rims_sum(layer):
        sender_sum[...] = jnp.zeros_like(sender_sum)
        for c in range(4):
            i, j = c // 2, c % 2
            by_row = tt[layer, c, :, 0:384].T
            for a in range(3):
                piece = by_row[96 * a : 96 * a + 96].reshape(3, 32, D)
                for b in range(3):
                    sender_sum[i + a, j + b] += piece[b]
            receiver_sum[32 * c : 32 * c + 32, :] = by_row[288:320]
        sender_low[layer] = sender_sum[...].astype(BF)

    def edge_grads(layer, dst, row_, vec):
        by_node = sum(dot(tt[layer, c, :, 0:384].astype(BF), window[layer, c]) for c in range(4))
        by_edge = sum(tt[layer, c, :, 384:512] for c in range(4))
        ones = sum(tt[layer, c, :, 256:384] for c in range(4)).T[64:65]
        dst[row_ : row_ + 128, :] = by_node[:, 128:256].T.astype(BF)
        dst[row_ + 128 : row_ + 256, :] = by_node[:, 0:128].T.astype(BF)
        dst[row_ + 256 : row_ + 384, :] = by_edge.T.astype(BF)
        dst[row_ + 384 : row_ + 512, :] = dw[layer, 0:128].T.astype(BF)
        third = dw[layer, 128:256].T
        dst[row_ + 512 : row_ + 640, :] = (third - jnp.mean(third, -1, keepdims=True)).astype(BF)
        s = [column_sum(sums[layer, k]) for k in range(4)]
        s[2] = s[2] - jnp.mean(s[2], -1, keepdims=True)
        vec.extend([ones, s[3], s[2], s[0] / egain[layer : layer + 1, :], s[1]])

    def node_share(layer):
        part = dot_nt(gz[0].astype(BF), nw1[layer, 0:D, :])
        gh_buf[...] += part + dot_nt(receiver_sum[...].astype(BF), ew1[layer, 0:D, :])

    def sender_share(layer):
        own = [sender_sum[1 + c // 2, 1 + c % 2] for c in range(4)]
        for k, (dx, dy) in enumerate(DIRS):
            cells = [
                (i, j)
                for i in ((0, 1) if dx == 0 else ((0,) if dx > 0 else (1,)))
                for j in ((0, 1) if dy == 0 else ((0,) if dy > 0 else (1,)))
            ]
            for at, (i, j) in enumerate(cells):
                own[2 * i + j] = own[2 * i + j] + rim_in[layer, k, at].astype(F32)
        own = jnp.concatenate(own, 0).astype(BF)
        return gh_buf[...] + dot_nt(own, ew1[layer, D : 2 * D, :])

    def put_vectors(dst, row_, vec):
        at = iota((16, D), 0)
        block = jnp.zeros((16, D), F32)
        for k, v in enumerate(vec):
            block = jnp.where(at == k, v, block)
        dst[row_ : row_ + 16, :] = block.astype(BF)

    exchange_finish(halo_copy, EARLY)
    prepare(0, (0, 1))
    half = SUB // 2
    for c in range(4):
        load(edges, e0, 0, c).wait()
    forward(0, 0)
    forward(0, 1)
    exchange_finish(halo_copy, LATE)
    prepare(0, (2, 3))
    node_forward(0, (0, 1))
    forward(0, 2, tuple(range(half)))
    cell_start(0)
    cell_start(1)
    forward(0, 2, tuple(range(half, SUB)))
    node_forward(0, (2,))
    forward(0, 3)
    cell_start(2)
    node_forward(0, (3,))
    cell_start(3)

    gh_buf[...] = ct_nodes[...].astype(F32)
    src1[VEC1 + 16 :, :] = jnp.zeros((CH1 * 16 - VEC1 - 16, D), BF)
    src0[VEC0 + 16 :, :] = jnp.zeros((CH0 * 16 - VEC0 - 16, D), BF)
    cells_arrive(1)
    prepare(1, (3,))
    forward(1, 3)
    cells_arrive(2)
    prepare(1, (2,))
    node_forward(1, (3,))
    node_backward(1, (3,))
    forward(1, 2)
    cells_arrive(3)
    prepare(1, (0, 1))
    node_forward(1, (2,))
    node_backward(1, (2,))
    forward(1, 1)
    node_forward(1, (1,))
    node_backward(1, (1,))
    forward(1, 0)

    for c in range(4):
        load(ct_edges, ct, 1, c).wait()
    node_forward(1, (0,))
    node_backward(1, (0,))
    for c in (3, 2, 1, 0):
        backward(1, c)
    rims_sum(1)
    exchange_start(functools.partial(rim_copy, 1))
    vec1, vec0 = [], []
    node_grads(1, src1, NODE_W1, vec1)
    for c in range(4):
        backward_rest(1, c)
    edge_grads(1, src1, EDGE_W1, vec1)
    put_vectors(src1, VEC1, vec1)
    node_share(1)
    sum1.scatter_start()
    exchange_finish(functools.partial(rim_copy, 1))
    gh_buf[...] = sender_share(1)

    node_backward(0, (0, 1, 2, 3))
    node_grads(0, srcn, 0, vec0)
    sumn.scatter_start()
    for c in range(4):
        backward(0, c)
    edge_grads(0, src0, EDGE_W1, vec0)
    put_vectors(src0, VEC0, vec0)
    sum0.scatter_start()
    rims_sum(0)
    exchange_start(functools.partial(rim_copy, 0))
    sum1.scatter_finish()
    sum1.column_start()
    sumn.scatter_finish()
    sumn.column_start()
    for c in range(4):
        backward_rest(0, c)
    node_share(0)
    sum0.scatter_finish()
    sum0.column_start()
    sum1.column_finish()
    sum1.gather_start()
    sumn.column_finish()
    sumn.gather_start()
    sum0.column_finish()
    sum0.gather_start()
    exchange_finish(functools.partial(rim_copy, 0))
    grad_nodes[...] = sender_share(0)
    all_sent()
    sum1.gather_finish()
    sumn.gather_finish()
    sum0.gather_finish()


def unpack_kernel(nodes_in, edges_in, grad_nodes_in, grad_edges_in, sum1, sumn, sum0, *rest):
    (nodes_out, edges_out, grad_nodes, grad_edges), outs = rest[:4], rest[4:20]
    held, (sems, small) = rest[20:36], rest[36:]
    w1, b1, w2, b2, w3, b3, gain, shift, v1, c1, v2, c2, v3, c3, ngain, nshift = held
    copies = [
        pltpu.make_async_copy(nodes_in, nodes_out, sems.at[2, 0]),
        pltpu.make_async_copy(grad_nodes_in, grad_nodes, sems.at[2, 1]),
    ]
    for t in range(4):
        s = pl.ds(t * CELL, CELL)
        copies.append(pltpu.make_async_copy(grad_edges_in.at[s], grad_edges.at[s], sems.at[0, t]))
        copies.append(pltpu.make_async_copy(edges_in.at[s], edges_out.at[s], sems.at[1, t]))
    for copy in copies:
        copy.start()

    def put(ref, layer, buffer, row):
        height = ref.shape[1]
        ref[layer] = buffer[row : row + height, :].astype(F32)

    for layer, buffer in ((1, sum1), (0, sum0)):
        put(w1, layer, buffer, EDGE_W1)
        put(w2, layer, buffer, EDGE_W2)
        put(w3, layer, buffer, EDGE_W3)
    for layer, buffer, row in ((1, sum1, 0), (0, sumn, -NODE_W1)):
        put(v1, layer, buffer, row + NODE_W1)
        put(v2, layer, buffer, row + NODE_W2)
        put(v3, layer, buffer, row + NODE_W3)
    for layer, block in ((1, sum1[VEC1 : VEC1 + 16, :]), (0, sum0[VEC0 : VEC0 + 16, :])):
        rows = block.astype(F32)
        for k, ref in enumerate((c1, c2, c3, ngain, nshift, b1, b2, b3, gain, shift)):
            ref[layer : layer + 1, :] = rows[k : k + 1]
    for k, (src, dst) in enumerate(zip(held, outs)):
        copies.append(pltpu.make_async_copy(src, dst, small.at[k]))
        copies[-1].start()
    for copy in copies:
        copy.wait()


def per_device(nodes, edges, nbr_index, nbr_mask, *rest):
    weights, ct_nodes, ct_edges = rest[:16], rest[16], rest[17]
    vmem = pl.BlockSpec(memory_space=pltpu.VMEM)
    hbm = pl.BlockSpec(memory_space=pl.ANY)
    shape = jax.ShapeDtypeStruct
    big = pltpu.VMEM((ROWS, D), BF)
    node_bf = pltpu.VMEM((2, PARTS, D), BF)
    node_f32 = pltpu.VMEM((2, PARTS, D), F32)
    square = pltpu.VMEM((2, D, D), BF)
    dma = pltpu.SemaphoreType.DMA

    def sum_scratch(chunk):
        return [
            pltpu.VMEM((16 * chunk, D), BF),
            pltpu.VMEM((16, chunk, D), BF),
            pltpu.VMEM((8, chunk, D), BF),
        ]

    scratch = [
        pltpu.VMEM((PARTS, 64), jnp.int32),
        pltpu.VMEM((PARTS, 64), jnp.int32),
        *(pltpu.VMEM(w.shape, w.dtype) for w in weights),
        pltpu.VMEM((PARTS, D), BF),
        pltpu.VMEM((ROWS, 3 * D), BF),
        big, big, big,
        *(([big] * 5 + [pltpu.VMEM((ROWS, D), F32)]) * 2),
        pltpu.VMEM((PARTS, D), F32),
        pltpu.VMEM((2, 4, 4, 32, D), BF),
        pltpu.VMEM((4, 4 * D, D), BF),
        square, square, square, square, square,
        pltpu.VMEM((D, D), BF),
        pltpu.VMEM((PARTS, D), F32),
        pltpu.VMEM((PARTS, D), F32),
        pltpu.VMEM((2, 4, D, 4 * D), F32),
        pltpu.VMEM((2, 2 * D, D), F32),
        pltpu.VMEM((2, 4, 8, D), F32),
        pltpu.VMEM((2, 4, 3 * D, 2 * D), BF),
        pltpu.VMEM((4, 4, 32, D), F32),
        pltpu.VMEM((2, 4, 4, 32, D), BF),
        pltpu.VMEM((PARTS, D), F32),
        pltpu.VMEM((2, 8, 2, 32, D), BF),
        node_bf, node_bf, node_bf, node_f32, node_f32, node_f32, node_f32,
        pltpu.VMEM((3, PARTS, D), F32),
        pltpu.VMEM((PARTS, D), F32),
        *sum_scratch(CH1),
        *sum_scratch(CHN),
        *sum_scratch(CH0),
        dma((3, 4)), dma((19,)), dma((2, 8)), dma((4, 3)), dma((4, 4)), dma((2, 2, 8)),
        *([dma((3, 2))] * 3),
    ]
    held = pl.pallas_call(
        main_kernel,
        out_shape=(
            pltpu.VMEM((PARTS, D), BF),
            pltpu.VMEM((ROWS, D), BF),
            pltpu.VMEM((PARTS, D), F32),
            pltpu.VMEM((ROWS, D), F32),
            pltpu.VMEM((16 * CH1, D), BF),
            pltpu.VMEM((16 * CHN, D), BF),
            pltpu.VMEM((16 * CH0, D), BF),
        ),
        in_specs=[hbm] * 22,
        out_specs=(vmem,) * 7,
        scratch_shapes=scratch,
        compiler_params=pltpu.CompilerParams(
            collective_id=0, has_side_effects=True, vmem_limit_bytes=53 * 1024 * 1024
        ),
        name="interaction_layers",
    )(
        nodes.reshape(PARTS, D),
        edges.reshape(ROWS, D),
        nbr_index.reshape(PARTS, 64),
        nbr_mask.reshape(PARTS, 64),
        *weights,
        ct_nodes.reshape(PARTS, D),
        ct_edges.reshape(ROWS, D),
    )
    held = [pltpu.with_memory_space_constraint(value, pltpu.VMEM) for value in held]
    nodes_out, edges_out, grad_nodes, grad_edges, *grads = pl.pallas_call(
        unpack_kernel,
        out_shape=(
            shape((PARTS, D), BF),
            shape((ROWS, D), BF),
            shape((PARTS, D), F32),
            shape((ROWS, D), F32),
            *(shape(w.shape, F32) for w in weights),
        ),
        in_specs=[vmem] * 7,
        out_specs=(hbm,) * 20,
        scratch_shapes=[*(pltpu.VMEM(w.shape, F32) for w in weights), dma((3, 4)), dma((16,))],
        compiler_params=pltpu.CompilerParams(vmem_limit_bytes=8 * 1024 * 1024),
        name="unpack_sums",
    )(*held)
    return (
        nodes_out.reshape(nodes.shape),
        edges_out.reshape(edges.shape),
        grad_nodes.reshape(nodes.shape),
        grad_edges.reshape(edges.shape),
        *grads,
    )


def solution(mesh):
    cells = P("gx", "gy", None, None)
    wide = P("gx", "gy", None, None, None)
    in_specs = (cells, wide, cells, cells) + (P(),) * 16 + (cells, wide)
    out_specs = (cells, wide, cells, wide) + (P(),) * 16
    return jax.shard_map(
        per_device, mesh=mesh, in_specs=in_specs, out_specs=out_specs, check_vma=False
    )
```
